32 devices in a mesh: wide: 8 (over y, x, core), narrow: 4 (over z).
Axes of the slice: x: 2, y: 2, z: 4, core: 2. Of those that a mesh axis runs over, the one named last changes fastest.
Arguments:
- saturation: float32 [128, 64, 512], P('wide', None, 'narrow'), may hold values from 0.05 to 0.95
- pressure: float32 [128, 64, 512], P('wide', None, 'narrow'), may hold values from -6 to 6
- rock_class: int32 [128, 64, 512], P('wide', None, 'narrow'), may hold values from 0 to 15
- rock_table: float32 [3, 16], replicated, may hold values from 0.2 to 5
- well_columns: int32 [64], replicated, may hold values from 0 to 32767
- well_rates: float32 [64], replicated, may hold values from 2 to 8
- residual: float32 [128, 64, 512], P(None, 'wide', 'narrow'), may hold values from -7 to 7
Outputs:
- sat_new: float32 [128, 64, 512], P('wide', None, 'narrow')
- precond: float32 [128, 64, 512], P(None, 'wide', 'narrow')
The draws below stay inside these ranges and needn't reach their ends.
Inputs may be any that keep to these rules, and one draw needn't show every extreme that they name: `well_columns`: a well with column c injects into every depth layer at row c // 512, column c % 512; columns may repeat.
All inputs are finite; a program needn't handle non-finite values.
Results may differ from the reference program's by a relative error of at most 0.0003.
Values sent between devices are 32-bit elements; how exact they have to be, the bound alone decides.
A program may use at most 64 MiB of HBM per device.

```python
import math
import jax
import jax.numpy as jnp
from jax import lax

YB = 8
XD = 128
ROCKS = 16
WELLS = 64
SWEEPS = 6
NZ = 128
NY = 64
NX = 512
N_WIDE = 8
N_NARROW = 4


def draw_residual(key, part):
    rough_key, wave_key, phase_key = jax.random.split(jax.random.fold_in(key, 17), 3)
    rough = jnp.clip(jax.random.normal(rough_key, (NZ, NY, NX), jnp.float32), -6.0, 6.0)
    waves = jax.random.randint(wave_key, (3, 3), 0, 3).astype(jnp.float32)
    phases = jax.random.uniform(phase_key, (3,), jnp.float32, 0.0, 2.0 * math.pi)
    depth = (jnp.arange(NZ, dtype=jnp.float32) / NZ)[:, None, None]
    across = (jnp.arange(NY, dtype=jnp.float32) / NY)[None, :, None]
    along = (jnp.arange(NX, dtype=jnp.float32) / NX)[None, None, :]
    smooth = jnp.zeros((NZ, NY, NX), jnp.float32)
    for number in range(3):
        angle_sum = 2.0 * math.pi * (waves[number, 0] * depth + waves[number, 1] * across + waves[number, 2] * along)
        smooth = smooth + 0.1 * jnp.cos(angle_sum + phases[number])
    return rough + smooth


def touch_ends(array, rng, low, top_value):
    place = [jax.random.randint(jax.random.fold_in(rng, axis), (), 0, length) for axis, length in enumerate(array.shape)]
    longest = array.shape.index(max(array.shape))
    beside = place[:longest] + [(place[longest] + 1) % array.shape[longest]] + place[longest + 1:]
    return array.at[tuple(place)].set(low).at[tuple(beside)].set(top_value)


def block_scale(rng, dims, cuts, least, largest):
    level = 1.0
    for dim, blocks in cuts:
        heights = jax.random.uniform(jax.random.fold_in(jax.random.fold_in(rng, 6), dim), (blocks,), jnp.float32, least / len(cuts), largest / len(cuts))
        level = level * jnp.repeat(jnp.exp(heights), dims[dim] // blocks).reshape((-1,) + (1,) * (len(dims) - 1 - dim))
    return level


def centred(key, extent, scale, bound, cuts=(), kind=jnp.bfloat16):
    factor_of = block_scale(key, extent, cuts, -0.22, 0.18) if cuts else 1.0
    array = jax.random.normal(key, extent, jnp.float32) * scale * factor_of
    return jnp.minimum(jnp.maximum(array, -bound), bound).astype(kind)


def setup_inputs(seed: int = 0) -> dict:
    streams_of = jax.random.split(jax.random.key(seed), 8)
    return {
        "saturation": jnp.clip(0.05 + 0.9 * jax.random.uniform(streams_of[0], (NZ, NY, NX), jnp.float32) ** block_scale(streams_of[0], (NZ, NY, NX), ((0, 8), (2, 4)), -0.2, 0.2), 0.05, 0.95),
        "pressure": centred(streams_of[1], (NZ, NY, NX), 1.0, 6.0, ((0, 8), (2, 4)), jnp.float32),
        "rock_class": touch_ends(jax.random.randint(streams_of[2], (NZ, NY, NX), 0, ROCKS), jax.random.fold_in(streams_of[2], 1), 0, ROCKS - 1).astype(jnp.int32),
        "rock_table": jnp.clip(jnp.exp(jax.random.uniform(streams_of[3], (3, ROCKS), jnp.float32, math.log(0.2), math.log(5.0))), 0.2, 5.0),
        "well_columns": touch_ends(jax.random.randint(streams_of[4], (WELLS,), 0, NY * NX), jax.random.fold_in(streams_of[4], 1), 0, (NY * NX) - 1).astype(jnp.int32),
        "well_rates": jnp.clip(jax.random.uniform(streams_of[5], (WELLS,), jnp.float32, 2.0, 8.0), 2.0, 8.0),
        "residual": draw_residual(jax.random.fold_in(streams_of[7], 71), 0),
    }


compress = 0.05
relax = 0.8
gravity = 0.5
courant = 0.5
tiny = 1e-06

def harmonic(lower_side, upper_side):
    return 2.0 * lower_side * upper_side / (lower_side + upper_side)

def pad_along(array_in, direction):
    widths = [(0, 0)] * array_in.ndim
    widths[direction] = (1, 1)
    return jnp.pad(array_in, widths)

def shifted(array_in, direction):
    padded = pad_along(array_in, direction)
    length = padded.shape[direction]
    return (lax.slice_in_dim(padded, 0, length - 1, axis=direction), lax.slice_in_dim(padded, 1, length, axis=direction))

def flows_between(lower_side, upper_side, lift):
    transmit = harmonic(lower_side[1], upper_side[1])
    total_flow = transmit * (lower_side[0] - upper_side[0] + lift)
    water_flow = total_flow * jnp.where(total_flow > 0, lower_side[2], upper_side[2])
    return (total_flow, water_flow)

def local_apply(values, diag_local, depth_inner, row_inner, col_inner):
    depth_pad = pad_along(values, 0)
    row_pad = pad_along(values, 1)
    col_pad = pad_along(values, 2)
    return diag_local * values - (depth_inner[:-1] * depth_pad[:-2] + depth_inner[1:] * depth_pad[2:] + row_inner[:, :-1] * row_pad[:, :-2] + row_inner[:, 1:] * row_pad[:, 2:] + col_inner[:, :, :-1] * col_pad[:, :, :-2] + col_inner[:, :, 1:] * col_pad[:, :, 2:])

def coarse_solve(rows, column_count):
    rhs_total = rows[:, 0]
    diagonal = rows[:, 1]
    low_rows = rows[:, 2]
    high_rows = rows[:, 3]
    low_cols = rows[:, 4]
    high_cols = rows[:, 5]
    matrix = jnp.diag(diagonal) - jnp.diag(low_rows[column_count:], -column_count) - jnp.diag(high_rows[:-column_count], column_count) - jnp.diag(low_cols[1:], -1) - jnp.diag(high_cols[:-1], 1)
    factor = jnp.linalg.cholesky(matrix)
    return jax.scipy.linalg.cho_solve((factor, True), rhs_total)

def transport(saturation, pressure, rock_class, rock_table, well_columns, well_rates):
    perm_cell = rock_table[0][rock_class]
    water_gain = rock_table[1][rock_class]
    oil_gain = rock_table[2][rock_class]
    water_mob = water_gain * saturation * saturation
    oil_mob = oil_gain * (1.0 - saturation) * (1.0 - saturation)
    water_frac = water_mob / (water_mob + oil_mob)
    net_parts = []
    out_parts = []
    for direction in range(3):
        lift = gravity if direction == 0 else 0.0
        press_low, press_high = shifted(pressure, direction)
        perm_low, perm_high = shifted(perm_cell, direction)
        frac_low, frac_high = shifted(water_frac, direction)
        total_flow, water_flow = flows_between((press_low, perm_low, frac_low), (press_high, perm_high, frac_high), lift)
        length = total_flow.shape[direction]
        upper_water = lax.slice_in_dim(water_flow, 1, length, axis=direction)
        lower_water = lax.slice_in_dim(water_flow, 0, length - 1, axis=direction)
        upper_total = lax.slice_in_dim(total_flow, 1, length, axis=direction)
        lower_total = lax.slice_in_dim(total_flow, 0, length - 1, axis=direction)
        net_parts.append(upper_water - lower_water)
        out_parts.append(jnp.maximum(upper_total, 0.0) + jnp.maximum(-lower_total, 0.0))
    net_water = net_parts[0] + net_parts[1] + net_parts[2]
    outflow = out_parts[0] + out_parts[1] + out_parts[2]
    step_size = courant / (jnp.max(outflow) + tiny)
    source = jnp.zeros((NY * NX,), jnp.float32).at[well_columns].add(well_rates).reshape(NY, NX)
    sat_new = saturation - step_size * net_water + step_size * source[None]
    coefficient = perm_cell * (water_gain * sat_new * sat_new + oil_gain * (1.0 - sat_new) * (1.0 - sat_new))
    return (sat_new, coefficient)

def brick_total(array_in):
    return jnp.sum(array_in.reshape(NZ, N_WIDE, YB, N_NARROW, XD), axis=(0, 2, 4)).reshape(-1)

def precondition(coefficient, residual):
    depth_faces = harmonic(coefficient[:-1], coefficient[1:])
    row_faces = harmonic(coefficient[:, :-1], coefficient[:, 1:])
    col_faces = harmonic(coefficient[:, :, :-1], coefficient[:, :, 1:])
    row_face_index = lax.broadcasted_iota(jnp.int32, row_faces.shape, 1)
    col_face_index = lax.broadcasted_iota(jnp.int32, col_faces.shape, 2)
    depth_inner = pad_along(depth_faces, 0)
    row_inner = pad_along(jnp.where((row_face_index + 1) % YB == 0, 0.0, row_faces), 1)
    col_inner = pad_along(jnp.where((col_face_index + 1) % XD == 0, 0.0, col_faces), 2)
    diag_local = compress * coefficient + depth_inner[:-1] + depth_inner[1:] + row_inner[:, :-1] + row_inner[:, 1:] + col_inner[:, :, :-1] + col_inner[:, :, 1:]
    values = relax * residual / diag_local
    for number in range(SWEEPS - 1):
        values = values + relax * (residual - local_apply(values, diag_local, depth_inner, row_inner, col_inner)) / diag_local
    rows_index = lax.broadcasted_iota(jnp.int32, values.shape, 1)
    cols_index = lax.broadcasted_iota(jnp.int32, values.shape, 2)
    value_rows = pad_along(values, 1)
    coeff_rows = pad_along(coefficient, 1)
    value_cols = pad_along(values, 2)
    coeff_cols = pad_along(coefficient, 2)
    first_row = rows_index % YB == 0
    last_row = (rows_index + 1) % YB == 0
    first_col = cols_index % XD == 0
    last_col = (cols_index + 1) % XD == 0
    weighted = coefficient * values
    weights = coefficient
    weighted = weighted + jnp.where(first_row, coeff_rows[:, :-2] * value_rows[:, :-2], 0.0)
    weights = weights + jnp.where(first_row, coeff_rows[:, :-2], 0.0)
    weighted = weighted + jnp.where(last_row, coeff_rows[:, 2:] * value_rows[:, 2:], 0.0)
    weights = weights + jnp.where(last_row, coeff_rows[:, 2:], 0.0)
    weighted = weighted + jnp.where(first_col, coeff_cols[:, :, :-2] * value_cols[:, :, :-2], 0.0)
    weights = weights + jnp.where(first_col, coeff_cols[:, :, :-2], 0.0)
    weighted = weighted + jnp.where(last_col, coeff_cols[:, :, 2:] * value_cols[:, :, 2:], 0.0)
    weights = weights + jnp.where(last_col, coeff_cols[:, :, 2:], 0.0)
    averaged = weighted / weights
    cross_rows = jnp.sum(row_faces[:, YB - 1::YB].reshape(NZ, N_WIDE - 1, N_NARROW, XD), axis=(0, 3))
    zero_row = jnp.zeros((1, N_NARROW), jnp.float32)
    high_rows = jnp.concatenate([cross_rows, zero_row], axis=0).reshape(-1)
    low_rows = jnp.concatenate([zero_row, cross_rows], axis=0).reshape(-1)
    cross_cols = jnp.sum(col_faces[:, :, XD - 1::XD].reshape(NZ, N_WIDE, YB, N_NARROW - 1), axis=(0, 2))
    zero_col = jnp.zeros((N_WIDE, 1), jnp.float32)
    high_cols = jnp.concatenate([cross_cols, zero_col], axis=1).reshape(-1)
    low_cols = jnp.concatenate([zero_col, cross_cols], axis=1).reshape(-1)
    diagonal = compress * brick_total(coefficient) + low_rows + high_rows + low_cols + high_cols
    rows = jnp.stack([brick_total(residual), diagonal, low_rows, high_rows, low_cols, high_cols], axis=1)
    solved = coarse_solve(rows, N_NARROW)
    result = averaged.reshape(NZ, N_WIDE, YB, N_NARROW, XD) + solved.reshape(1, N_WIDE, 1, N_NARROW, 1)
    return result.reshape(NZ, NY, NX)

def reference(saturation, pressure, rock_class, rock_table, well_columns, well_rates, residual):
    sat_new, coefficient = transport(saturation, pressure, rock_class, rock_table, well_columns, well_rates)
    precond = precondition(coefficient, residual)
    return (sat_new, precond)
```

```python
import functools

import jax
import jax.numpy as jnp
from jax import lax
from jax.experimental import pallas as pl
from jax.experimental.pallas import tpu as pltpu
from jax.sharding import PartitionSpec as P

SWEEPS = 6

compress = 0.05
relax = 0.8
gravity = 0.5
courant = 0.5
tiny = 1e-06

F32 = jnp.float32


def harmonic(a, b):
    return 2.0 * a * b / (a + b)


def flows(low, high, lift):
    total = harmonic(low[1], high[1]) * (low[0] - high[0] + lift)
    return total, total * jnp.where(total > 0, low[2], high[2])


def lookup(bits, table_ref, row, count):
    level = [table_ref[row, i] for i in range(count)]
    for bit in bits:
        level = [jnp.where(bit, level[i + 1], level[i]) for i in range(0, len(level), 2)]
    return level[0]


def kernel(
    n_wide, n_narrow,
    sat_ref, pres_ref, rock_ref, table_ref, wcol_ref, wrate_ref, res_ref,
    satnew_ref, prec_ref,
    fields, gains, net, colpack, colhalo, colflow, source, maxw, maxn,
    slab, coef, dface, rface, cface, scale, first, va, vb,
    rowsend, rowhalo, rowterm, packs, packhalo, packterm, cw, cn, mat, rhs,
    sends, recvs,
):
    depth, rows, cols = sat_ref.shape
    layers, brick_rows, _ = res_ref.shape
    w = lax.axis_index("wide")
    k = lax.axis_index("narrow")
    tiles = layers // cols
    band = depth * brick_rows
    has = {"wide": (w > 0, w < n_wide - 1), "narrow": (k > 0, k < n_narrow - 1)}
    place = {"wide": w, "narrow": k}
    size = {"wide": n_wide, "narrow": n_narrow}
    count = [0]

    def slot():
        count[0] += 1
        return count[0] - 1

    barrier = pltpu.get_barrier_semaphore()
    for axis in ("wide", "narrow"):
        for off in range(1, size[axis]):
            peer = lax.rem(place[axis] + off, size[axis])
            pl.semaphore_signal(
                barrier, inc=1, device_id={axis: peer}, device_id_type=pl.DeviceIdType.MESH
            )

    def remote(src, dst, number, axis, peer):
        return pltpu.make_async_remote_copy(
            src_ref=src, dst_ref=dst, send_sem=sends.at[number], recv_sem=recvs.at[number],
            device_id={axis: peer}, device_id_type=pl.DeviceIdType.MESH,
        )

    def neighbours(axis, low_src, high_src, from_low, from_high):
        down, up = slot(), slot()
        me = place[axis]
        has_low, has_high = has[axis]

        @pl.when(has_low)
        def _():
            remote(low_src, from_high, down, axis, me - 1).start()

        @pl.when(has_high)
        def _():
            remote(high_src, from_low, up, axis, me + 1).start()

        def wait():
            @pl.when(has_low)
            def _():
                remote(low_src, from_high, down, axis, me - 1).wait_send()
                remote(high_src, from_low, up, axis, me - 1).wait_recv()

            @pl.when(has_high)
            def _():
                remote(high_src, from_low, up, axis, me + 1).wait_send()
                remote(low_src, from_high, down, axis, me + 1).wait_recv()

        return wait

    def everyone(axis, src_of, dst_from):
        copies = []
        me = place[axis]
        n = size[axis]
        for off in range(1, n):
            number = slot()
            peer = lax.rem(me + off, n)
            copy = remote(src_of(peer), dst_from(me), number, axis, peer)
            copy.start()
            sender = lax.rem(me + n - off, n)
            copies.append((copy, remote(src_of(peer), dst_from(sender), number, axis, peer)))

        def wait():
            for sent, received in copies:
                sent.wait_send()
                received.wait_recv()

        return wait

    lane = lax.broadcasted_iota(jnp.int32, (rows, cols), 1)
    row = lax.broadcasted_iota(jnp.int32, (rows, cols), 0)
    tlane = lax.broadcasted_iota(jnp.int32, (brick_rows, cols), 1)
    trow = lax.broadcasted_iota(jnp.int32, (brick_rows, cols), 0)
    zero = jnp.zeros((brick_rows, cols), F32)
    one = jnp.ones((brick_rows, cols), F32)

    @pl.when(w == 0)
    def _():
        fields[0] = jnp.ones((3, rows, cols), F32)
        rowhalo[0] = jnp.ones((2, layers, cols), F32)

    @pl.when(w == n_wide - 1)
    def _():
        fields[depth + 1] = jnp.ones((3, rows, cols), F32)
        rowhalo[1] = jnp.ones((2, layers, cols), F32)

    @pl.when(k == 0)
    def _():
        colhalo[0] = jnp.ones((rows, cols), F32)
        packhalo[0] = jnp.ones((2, tiles * brick_rows, cols), F32)

    @pl.when(k == n_narrow - 1)
    def _():
        colhalo[1] = jnp.ones((rows, cols), F32)
        packhalo[1] = jnp.ones((2, tiles * brick_rows, cols), F32)

    coef[pl.ds(layers * brick_rows, brick_rows), :] = one
    va[pl.ds(layers * brick_rows, brick_rows), :] = zero
    vb[pl.ds(layers * brick_rows, brick_rows), :] = zero

    rocks = table_ref.shape[1]

    def derive(d, carry):
        packed_low, packed_high = carry
        rock = rock_ref[d]
        bits = []
        step = 1
        while step < rocks:
            bits.append((rock & step) != 0)
            step *= 2
        perm = lookup(bits, table_ref, 0, rocks)
        water = lookup(bits, table_ref, 1, rocks)
        oil = lookup(bits, table_ref, 2, rocks)
        s = sat_ref[d]
        water_mob = water * s * s
        oil_mob = oil * (1.0 - s) * (1.0 - s)
        frac = water_mob / (water_mob + oil_mob)
        gains[d, 0] = water
        gains[d, 1] = oil
        for f, value in enumerate((pres_ref[d], perm, frac)):
            fields[d + 1, f] = value
            turned = pltpu.roll(value, d + f * depth, 1)
            packed_low = jnp.where(lane == d + f * depth, turned, packed_low)
            packed_high = jnp.where(lane == lax.rem(d + f * depth + cols - 1, cols), turned, packed_high)
        return packed_low, packed_high

    blank = jnp.ones((rows, cols), F32)
    packed_low, packed_high = lax.fori_loop(0, depth, derive, (blank, blank))
    colpack[0] = packed_low
    colpack[1] = pltpu.roll(packed_high, 1, 1)

    pl.semaphore_wait(barrier, n_wide + n_narrow - 2)
    wait_planes = neighbours(
        "wide", fields.at[1], fields.at[depth], fields.at[0], fields.at[depth + 1]
    )
    wait_cols = neighbours(
        "narrow", colpack.at[0], colpack.at[1], colhalo.at[0], colhalo.at[1]
    )

    all_cols = cols * n_narrow

    def well(i, total):
        column = wcol_ref[i]
        inside = column % all_cols - k * cols
        return total + jnp.where(
            (row == column // all_cols) & (lane == inside), wrate_ref[i], 0.0
        )

    source[...] = lax.fori_loop(0, wcol_ref.shape[0], well, jnp.zeros((rows, cols), F32))

    def add_res(z, total):
        return total + res_ref[z]

    res_total = lax.fori_loop(0, layers, add_res, zero)

    wait_cols()

    def unpack(block):
        return [block] + [pltpu.roll(block, cols - f * depth, 1) for f in (1, 2)]

    low_total, low_water = flows(unpack(colhalo[0]), unpack(colpack[0]), 0.0)
    high_total, high_water = flows(unpack(colpack[1]), unpack(colhalo[1]), 0.0)
    has_left, has_right = has["narrow"]
    nothing = jnp.zeros((rows, cols), F32)
    colflow[0] = jnp.where(has_left, low_total, nothing)
    colflow[1] = jnp.where(has_left, low_water, nothing)
    colflow[2] = jnp.where(has_right, high_total, nothing)
    colflow[3] = jnp.where(has_right, high_water, nothing)

    wait_planes()
    has_below, has_above = has["wide"]

    def plane(d):
        return [fields[d, f] for f in range(3)]

    under_total, under_water = flows(plane(0), plane(1), gravity)
    under_total = jnp.where(has_below, under_total, nothing)
    under_water = jnp.where(has_below, under_water, nothing)

    def transport(d, carry):
        below_total, below_water, most = carry
        here = plane(d + 1)
        above_total, above_water = flows(here, plane(d + 2), gravity)
        open_face = (d < depth - 1) | has_above
        above_total = jnp.where(open_face, above_total, nothing)
        above_water = jnp.where(open_face, above_water, nothing)
        flow = above_water - below_water
        out = jnp.maximum(above_total, 0.0) + jnp.maximum(-below_total, 0.0)

        total, water = flows(here, [pltpu.roll(x, rows - 1, 0) for x in here], 0.0)
        total = jnp.where(row == rows - 1, 0.0, total)
        water = jnp.where(row == rows - 1, 0.0, water)
        flow = flow + (water - pltpu.roll(water, 1, 0))
        out = out + (jnp.maximum(total, 0.0) + jnp.maximum(-pltpu.roll(total, 1, 0), 0.0))

        total, water = flows(here, [pltpu.roll(x, cols - 1, 1) for x in here], 0.0)
        to_low = lax.rem(cols - d, cols)
        low = [jnp.where(lane == 0, pltpu.roll(colflow[i], to_low, 1), pltpu.roll(x, 1, 1))
               for i, x in ((0, total), (1, water))]
        high = [jnp.where(lane == cols - 1, pltpu.roll(colflow[i], cols - 1 - d, 1), x)
                for i, x in ((2, total), (3, water))]
        flow = flow + (high[1] - low[1])
        out = out + (jnp.maximum(high[0], 0.0) + jnp.maximum(-low[0], 0.0))
        net[d] = flow
        return above_total, above_water, jnp.maximum(most, out)

    _, _, most = lax.fori_loop(0, depth, transport, (under_total, under_water, nothing))

    maxw[w] = jnp.max(most.reshape(rows // brick_rows, brick_rows, cols), axis=0)
    everyone("wide", lambda peer: maxw.at[w], lambda sender: maxw.at[sender])()
    maxn[k] = jnp.max(maxw[...], axis=0)
    everyone("narrow", lambda peer: maxn.at[k], lambda sender: maxn.at[sender])()
    top_rate = jnp.max(jnp.max(maxn[...], axis=0), axis=(0, 1), keepdims=True)
    step_size = courant / (top_rate + tiny)

    def update(d, carry):
        s = sat_ref[d] - step_size * net[d] + step_size * source[...]
        satnew_ref[d] = s
        value = fields[d + 1, 1] * (gains[d, 0] * s * s + gains[d, 1] * (1.0 - s) * (1.0 - s))
        at = pl.multiple_of(d * brick_rows, brick_rows)
        for p in range(n_wide):
            slab[p, pl.ds(at, brick_rows), :] = value[p * brick_rows:(p + 1) * brick_rows]
        return carry

    lax.fori_loop(0, depth, update, 0)

    def part(sender):
        return coef.at[pl.ds(pl.multiple_of(sender * band, band), band), :]

    wait_bricks = everyone("wide", lambda peer: slab.at[peer], part)
    coef[pl.ds(pl.multiple_of(w * band, band), band), :] = slab[w]
    wait_bricks()

    last_row = brick_rows - 1

    def send_sides(ref, which):
        rowsend[0, which] = ref[pl.ds(0, layers, stride=brick_rows), :]
        rowsend[1, which] = ref[pl.ds(last_row, layers, stride=brick_rows), :]
        wait_rows = neighbours(
            "wide", rowsend.at[0, which], rowsend.at[1, which],
            rowhalo.at[0, which], rowhalo.at[1, which],
        )
        for t in range(tiles):
            def collect(i, carry):
                low, high = carry
                for u in range(4):
                    z = i * 4 + u
                    at = pl.multiple_of((t * cols + z) * brick_rows, brick_rows)
                    turned = pltpu.roll(ref[pl.ds(at, brick_rows), :], z, 1)
                    low = jnp.where(tlane == z, turned, low)
                    high = jnp.where(tlane == lax.rem(z + cols - 1, cols), turned, high)
                return low, high

            low, high = lax.fori_loop(0, cols // 4, collect, (zero, zero))
            packs[0, which, pl.ds(t * brick_rows, brick_rows), :] = low
            packs[1, which, pl.ds(t * brick_rows, brick_rows), :] = pltpu.roll(high, 1, 1)
        wait_packs = neighbours(
            "narrow", packs.at[0, which], packs.at[1, which],
            packhalo.at[0, which], packhalo.at[1, which],
        )
        return wait_rows, wait_packs

    wait_rows, wait_packs = send_sides(coef, 0)

    unroll = 4

    def at_layer(z):
        return pl.ds(pl.multiple_of(z * brick_rows, brick_rows), brick_rows)

    def assemble(i, carry):
        below, here, total = carry
        for u in range(unroll):
            z = i * unroll + u
            above = coef[at_layer(z + 1), :]
            df = jnp.where(z < layers - 1, harmonic(here, above), zero)
            rf = jnp.where(trow == last_row, 0.0, harmonic(here, pltpu.roll(here, last_row, 0)))
            cf = jnp.where(tlane == cols - 1, 0.0, harmonic(here, pltpu.roll(here, cols - 1, 1)))
            diag = (
                compress * here + below + df + pltpu.roll(rf, 1, 0) + rf + pltpu.roll(cf, 1, 1) + cf
            )
            sc = relax / diag
            dface[at_layer(z), :] = df
            rface[at_layer(z), :] = rf
            cface[at_layer(z), :] = cf
            scale[at_layer(z), :] = sc
            v = sc * res_ref[z]
            first[at_layer(z), :] = v
            va[at_layer(z), :] = v
            total = total + here
            below, here = df, above
        return below, here, total

    _, _, coef_total = lax.fori_loop(
        0, layers // unroll, assemble, (zero, coef[pl.ds(0, brick_rows), :], zero)
    )

    def sweep(src, dst):
        def body(i, carry):
            v_below, d_below, v = carry
            for u in range(unroll):
                z = i * unroll + u
                v_above = src[at_layer(z + 1), :]
                df = dface[at_layer(z), :]
                rf = rface[at_layer(z), :]
                cf = cface[at_layer(z), :]
                off = (
                    d_below * v_below + df * v_above
                    + pltpu.roll(rf * v, 1, 0) + rf * pltpu.roll(v, last_row, 0)
                    + pltpu.roll(cf * v, 1, 1) + cf * pltpu.roll(v, cols - 1, 1)
                )
                dst[at_layer(z), :] = (
                    (1.0 - relax) * v + first[at_layer(z), :] + scale[at_layer(z), :] * off
                )
                v_below, d_below, v = v, df, v_above
            return v_below, d_below, v

        lax.fori_loop(0, layers // unroll, body, (zero, zero, src[pl.ds(0, brick_rows), :]))

    def coarse_row():
        wait_rows()
        wait_packs()

        def side(own, halo, present):
            return jnp.where(present, jnp.sum(harmonic(own, halo), axis=(0, 1), keepdims=True), 0.0)

        low_rows = side(rowsend[0, 0], rowhalo[0, 0], has_below)
        high_rows = side(rowsend[1, 0], rowhalo[1, 0], has_above)
        low_cols = side(packs[0, 0], packhalo[0, 0], has_left)
        high_cols = side(packs[1, 0], packhalo[1, 0], has_right)
        diagonal = (
            compress * jnp.sum(coef_total, axis=(0, 1), keepdims=True)
            + low_rows + high_rows + low_cols + high_cols
        )
        total = jnp.sum(res_total, axis=(0, 1), keepdims=True)
        message = zero
        for i, value in enumerate((total, diagonal, low_rows, high_rows, low_cols, high_cols)):
            message = jnp.where(tlane == i, value, message)
        cw[pl.ds(pl.multiple_of(w * brick_rows, brick_rows), brick_rows), :] = message

        def at_wide(sender):
            return cw.at[pl.ds(pl.multiple_of(sender * brick_rows, brick_rows), brick_rows), :]

        return everyone("wide", lambda peer: at_wide(w), at_wide)

    def coarse_gather():
        cn[pl.ds(pl.multiple_of(k * n_wide, n_wide), n_wide), :] = cw[
            pl.ds(0, n_wide, stride=brick_rows), :
        ]

        def at_narrow(sender):
            return cn.at[pl.ds(pl.multiple_of(sender * n_wide, n_wide), n_wide), :]

        return everyone("narrow", lambda peer: at_narrow(k), at_narrow)

    bricks = n_wide * n_narrow
    blane = lax.broadcasted_iota(jnp.int32, (bricks, cols), 1)
    brow = lax.broadcasted_iota(jnp.int32, (bricks, cols), 0)

    def coarse_build():
        gathered = cn[...]
        matrix = jnp.where(blane == brow, gathered[:, 1:2], 0.0)
        for i, away in ((2, -1), (3, 1), (4, -n_wide), (5, n_wide)):
            matrix = jnp.where(blane == brow + away, matrix - gathered[:, i:i + 1], matrix)
        mat[...] = matrix
        rhs[...] = jnp.broadcast_to(gathered[:, 0:1], (bricks, cols))

    mine = k * n_wide + w

    def eliminate(j, carry):
        matrix = mat[...]
        right = rhs[...]
        pivot_row = mat[pl.ds(j, 1), :]
        pivot_rhs = rhs[pl.ds(j, 1), :]
        column = jnp.sum(jnp.where(blane == j, matrix, 0.0), axis=1, keepdims=True)
        pivot = jnp.sum(jnp.where(blane[:1] == j, pivot_row, 0.0), axis=1, keepdims=True)
        factor = jnp.where((brow == j) | (j == mine), 0.0, column / pivot)
        mat[...] = matrix - factor * pivot_row
        rhs[...] = right - factor * pivot_rhs
        return carry

    wait_gather = coarse_row_wait = None
    src, dst = va, vb
    for number in range(SWEEPS - 1):
        if number == 1:
            coarse_row_wait = coarse_row()
        if number == 3:
            coarse_row_wait()
            wait_gather = coarse_gather()
        sweep(src, dst)
        src, dst = dst, src
    wait_value_rows, wait_value_packs = send_sides(src, 1)

    wait_gather()
    coarse_build()
    lax.fori_loop(0, bricks, eliminate, 0)
    own_row = mat[pl.ds(mine, 1), :]
    own_pivot = jnp.sum(jnp.where(blane[:1] == mine, own_row, 0.0), axis=1, keepdims=True)
    coarse_value = rhs[pl.ds(mine, 1), :] / own_pivot

    wait_value_rows()
    wait_value_packs()
    for side, present in ((0, has_below), (1, has_above)):
        c = jnp.where(present, rowhalo[side, 0], 0.0)
        rowterm[side, 0] = c
        rowterm[side, 1] = jnp.where(present, c * rowhalo[side, 1], 0.0)
    for side, present in ((0, has_left), (1, has_right)):
        c = jnp.where(present, packhalo[side, 0], 0.0)
        packterm[side, 0] = c
        packterm[side, 1] = jnp.where(present, c * packhalo[side, 1], 0.0)

    for t in range(tiles):
        tile = pl.ds(t * brick_rows, brick_rows)

        def average(i, carry):
            for u in range(unroll):
                z = i * unroll + u
                layer = t * cols + z
                c = coef[at_layer(layer), :]
                sums = [c, c * src[at_layer(layer), :]]
                for j in range(2):
                    low = rowterm[0, j, pl.ds(layer, 1), :]
                    high = rowterm[1, j, pl.ds(layer, 1), :]
                    left = pltpu.roll(packterm[0, j, tile, :], lax.rem(cols - z, cols), 1)
                    right = pltpu.roll(packterm[1, j, tile, :], cols - 1 - z, 1)
                    sums[j] = (
                        sums[j]
                        + jnp.where(trow == 0, low, 0.0) + jnp.where(trow == last_row, high, 0.0)
                        + jnp.where(tlane == 0, left, 0.0)
                        + jnp.where(tlane == cols - 1, right, 0.0)
                    )
                prec_ref[layer] = sums[1] / sums[0] + coarse_value
            return carry

        lax.fori_loop(0, cols // unroll, average, 0)


def shards(n_wide, n_narrow, *args):
    sat, residual = args[0], args[6]
    depth, rows, cols = sat.shape
    layers, brick_rows, _ = residual.shape
    tiles = layers // cols
    bricks = n_wide * n_narrow
    cells = layers * brick_rows
    copies = 3 * 4 + 3 * (n_wide - 1) + 2 * (n_narrow - 1)
    vmem = pl.BlockSpec(memory_space=pltpu.VMEM)
    smem = pl.BlockSpec(memory_space=pltpu.SMEM)

    def buffer(*shape):
        return pltpu.VMEM(shape, F32)

    return pl.pallas_call(
        functools.partial(kernel, n_wide, n_narrow),
        out_shape=(
            jax.ShapeDtypeStruct(sat.shape, F32),
            jax.ShapeDtypeStruct(residual.shape, F32),
        ),
        in_specs=[vmem, vmem, vmem, smem, smem, smem, vmem],
        out_specs=(vmem, vmem),
        scratch_shapes=[
            buffer(depth + 2, 3, rows, cols),
            buffer(depth, 2, rows, cols),
            buffer(depth, rows, cols),
            buffer(2, rows, cols),
            buffer(2, rows, cols),
            buffer(4, rows, cols),
            buffer(rows, cols),
            buffer(n_wide, brick_rows, cols),
            buffer(n_narrow, brick_rows, cols),
            buffer(n_wide, depth * brick_rows, cols),
            buffer(cells + brick_rows, cols),
            buffer(cells, cols),
            buffer(cells, cols),
            buffer(cells, cols),
            buffer(cells, cols),
            buffer(cells, cols),
            buffer(cells + brick_rows, cols),
            buffer(cells + brick_rows, cols),
            buffer(2, 2, layers, cols),
            buffer(2, 2, layers, cols),
            buffer(2, 2, layers, cols),
            buffer(2, 2, tiles * brick_rows, cols),
            buffer(2, 2, tiles * brick_rows, cols),
            buffer(2, 2, tiles * brick_rows, cols),
            buffer(n_wide * brick_rows, cols),
            buffer(bricks, cols),
            buffer(bricks, cols),
            buffer(bricks, cols),
            pltpu.SemaphoreType.DMA((copies,)),
            pltpu.SemaphoreType.DMA((copies,)),
        ],
        compiler_params=pltpu.CompilerParams(
            collective_id=0, has_side_effects=True, vmem_limit_bytes=40 * 1024 * 1024
        ),
    )(*args)


def solution(mesh):
    placed = (
        P("wide", None, "narrow"),
        P("wide", None, "narrow"),
        P("wide", None, "narrow"),
        P(),
        P(),
        P(),
        P(None, "wide", "narrow"),
    )
    return jax.shard_map(
        functools.partial(shards, mesh.shape["wide"], mesh.shape["narrow"]),
        mesh=mesh,
        in_specs=placed,
        out_specs=(P("wide", None, "narrow"), P(None, "wide", "narrow")),
        check_vma=False,
    )
```

```python
import functools

import jax
import jax.numpy as jnp
from jax import lax
from jax.experimental import pallas as pl
from jax.experimental.pallas import tpu as pltpu
from jax.sharding import PartitionSpec as P

SWEEPS = 6

compress = 0.05
relax = 0.8
gravity = 0.5
courant = 0.5
tiny = 1e-06

F32 = jnp.float32


def harmonic(a, b):
    return 2.0 * a * b / (a + b)


def flows(low, high, lift):
    total = harmonic(low[1], high[1]) * (low[0] - high[0] + lift)
    return total, total * jnp.where(total > 0, low[2], high[2])


def lookup(bits, table_ref, row, count):
    level = [table_ref[row, i] for i in range(count)]
    for bit in bits:
        level = [jnp.where(bit, level[i + 1], level[i]) for i in range(0, len(level), 2)]
    return level[0]


def kernel(
    n_wide, n_narrow,
    sat_in, pres_in, rock_in, table_in, wcol_in, wrate_in, res_in,
    satnew_ref, prec_ref,
    sat_ref, pres_ref, rock_ref, table_ref, wcol_ref, wrate_ref, res_ref,
    fields, gains, net, colpack, colhalo, colflow, source, maxw, maxn,
    slab, coef, dface, rface, cface, scale, first, va, vb,
    rowsend, rowhalo, rowterm, packs, packhalo, packterm, cw, cn, sidepack, sidehalo,
    loads, sends, recvs,
):
    depth, rows, cols = sat_ref.shape
    layers, brick_rows, _ = res_ref.shape
    w = lax.axis_index("wide")
    k = lax.axis_index("narrow")
    tiles = layers // cols
    band = depth * brick_rows
    has = {"wide": (w > 0, w < n_wide - 1), "narrow": (k > 0, k < n_narrow - 1)}
    place = {"wide": w, "narrow": k}
    size = {"wide": n_wide, "narrow": n_narrow}
    count = [0]

    loading = [
        pltpu.make_async_copy(src, dst, loads.at[i])
        for i, (src, dst) in enumerate((
            (table_in, table_ref), (rock_in, rock_ref), (sat_in, sat_ref), (pres_in, pres_ref),
            (wcol_in, wcol_ref), (wrate_in, wrate_ref), (res_in, res_ref),
        ))
    ]
    for copy in loading:
        copy.start()

    def slot():
        count[0] += 1
        return count[0] - 1

    barrier = pltpu.get_barrier_semaphore()
    for axis in ("wide", "narrow"):
        for off in range(1, size[axis]):
            peer = lax.rem(place[axis] + off, size[axis])
            pl.semaphore_signal(
                barrier, inc=1, device_id={axis: peer}, device_id_type=pl.DeviceIdType.MESH
            )

    def remote(src, dst, number, axis, peer):
        return pltpu.make_async_remote_copy(
            src_ref=src, dst_ref=dst, send_sem=sends.at[number], recv_sem=recvs.at[number],
            device_id={axis: peer}, device_id_type=pl.DeviceIdType.MESH,
        )

    def neighbours(axis, low_src, high_src, from_low, from_high):
        down, up = slot(), slot()
        me = place[axis]
        has_low, has_high = has[axis]

        @pl.when(has_low)
        def _():
            remote(low_src, from_high, down, axis, me - 1).start()

        @pl.when(has_high)
        def _():
            remote(high_src, from_low, up, axis, me + 1).start()

        def wait():
            @pl.when(has_low)
            def _():
                remote(low_src, from_high, down, axis, me - 1).wait_send()
                remote(high_src, from_low, up, axis, me - 1).wait_recv()

            @pl.when(has_high)
            def _():
                remote(high_src, from_low, up, axis, me + 1).wait_send()
                remote(low_src, from_high, down, axis, me + 1).wait_recv()

        return wait

    def everyone(axis, src_of, dst_from):
        copies = []
        me = place[axis]
        n = size[axis]
        for off in range(1, n):
            number = slot()
            peer = lax.rem(me + off, n)
            copy = remote(src_of(peer), dst_from(me), number, axis, peer)
            copy.start()
            sender = lax.rem(me + n - off, n)
            copies.append((copy, remote(src_of(peer), dst_from(sender), number, axis, peer)))

        def wait():
            for sent, received in copies:
                sent.wait_send()
                received.wait_recv()

        return wait

    lane = lax.broadcasted_iota(jnp.int32, (rows, cols), 1)
    row = lax.broadcasted_iota(jnp.int32, (rows, cols), 0)
    tlane = lax.broadcasted_iota(jnp.int32, (brick_rows, cols), 1)
    trow = lax.broadcasted_iota(jnp.int32, (brick_rows, cols), 0)
    zero = jnp.zeros((brick_rows, cols), F32)
    one = jnp.ones((brick_rows, cols), F32)

    @pl.when(w == 0)
    def _():
        fields[0] = jnp.ones((3, rows, cols), F32)
        rowhalo[0] = jnp.ones((2, layers, cols), F32)

    @pl.when(w == n_wide - 1)
    def _():
        fields[depth + 1] = jnp.ones((3, rows, cols), F32)
        rowhalo[1] = jnp.ones((2, layers, cols), F32)

    @pl.when(k == 0)
    def _():
        sidehalo[0] = jnp.ones((rows, cols), F32)
        colhalo[0] = jnp.ones((rows, cols), F32)
        packhalo[0] = jnp.ones((2, tiles * brick_rows, cols), F32)

    @pl.when(k == n_narrow - 1)
    def _():
        sidehalo[1] = jnp.ones((rows, cols), F32)
        colhalo[1] = jnp.ones((rows, cols), F32)
        packhalo[1] = jnp.ones((2, tiles * brick_rows, cols), F32)

    coef[pl.ds(layers * brick_rows, brick_rows), :] = one
    va[pl.ds(layers * brick_rows, brick_rows), :] = zero
    vb[pl.ds(layers * brick_rows, brick_rows), :] = zero

    rocks = table_ref.shape[1]
    for copy in loading[:4]:
        copy.wait()

    def derive(d, carry):
        packed_low, packed_high = carry
        rock = rock_ref[d]
        bits = []
        step = 1
        while step < rocks:
            bits.append((rock & step) != 0)
            step *= 2
        perm = lookup(bits, table_ref, 0, rocks)
        water = lookup(bits, table_ref, 1, rocks)
        oil = lookup(bits, table_ref, 2, rocks)
        s = sat_ref[d]
        water_mob = water * s * s
        oil_mob = oil * (1.0 - s) * (1.0 - s)
        frac = water_mob / (water_mob + oil_mob)
        gains[d, 0] = water
        gains[d, 1] = oil
        for f, value in enumerate((pres_ref[d], perm, frac)):
            fields[d + 1, f] = value
            turned = pltpu.roll(value, d + f * depth, 1)
            packed_low = jnp.where(lane == d + f * depth, turned, packed_low)
            packed_high = jnp.where(lane == lax.rem(d + f * depth + cols - 1, cols), turned, packed_high)
        return packed_low, packed_high

    blank = jnp.ones((rows, cols), F32)
    packed_low, packed_high = lax.fori_loop(0, depth, derive, (blank, blank))
    colpack[0] = packed_low
    colpack[1] = pltpu.roll(packed_high, 1, 1)

    pl.semaphore_wait(barrier, n_wide + n_narrow - 2)
    wait_planes = neighbours(
        "wide", fields.at[1], fields.at[depth], fields.at[0], fields.at[depth + 1]
    )
    wait_cols = neighbours(
        "narrow", colpack.at[0], colpack.at[1], colhalo.at[0], colhalo.at[1]
    )

    all_cols = cols * n_narrow

    for copy in loading[4:]:
        copy.wait()
    cell = row * cols + lane

    def well(i, total):
        for u in range(8):
            column = wcol_ref[i * 8 + u]
            inside = lax.rem(column, all_cols) - k * cols
            target = lax.div(column, all_cols) * cols + inside
            target = jnp.where((inside >= 0) & (inside < cols), target, -1)
            total = total + jnp.where(cell == target, wrate_ref[i * 8 + u], 0.0)
        return total

    source[...] = lax.fori_loop(0, wcol_ref.shape[0] // 8, well, jnp.zeros((rows, cols), F32))

    def add_res(i, total):
        return total + jnp.sum(res_ref[pl.ds(i * 16, 16)], axis=0)

    res_total = jnp.sum(lax.fori_loop(0, layers // 16, add_res, zero), axis=(0, 1), keepdims=True)

    wait_cols()

    def unpack(block):
        return [block] + [pltpu.roll(block, cols - f * depth, 1) for f in (1, 2)]

    low_total, low_water = flows(unpack(colhalo[0]), unpack(colpack[0]), 0.0)
    high_total, high_water = flows(unpack(colpack[1]), unpack(colhalo[1]), 0.0)
    has_left, has_right = has["narrow"]
    nothing = jnp.zeros((rows, cols), F32)
    colflow[0] = jnp.where(has_left, low_total, nothing)
    colflow[1] = jnp.where(has_left, low_water, nothing)
    colflow[2] = jnp.where(has_right, high_total, nothing)
    colflow[3] = jnp.where(has_right, high_water, nothing)

    wait_planes()
    has_below, has_above = has["wide"]

    def plane(d):
        return [fields[d, f] for f in range(3)]

    under_total, under_water = flows(plane(0), plane(1), gravity)
    under_total = jnp.where(has_below, under_total, nothing)
    under_water = jnp.where(has_below, under_water, nothing)

    def transport(d, carry):
        below_total, below_water, most = carry
        here = plane(d + 1)
        above_total, above_water = flows(here, plane(d + 2), gravity)
        open_face = (d < depth - 1) | has_above
        above_total = jnp.where(open_face, above_total, nothing)
        above_water = jnp.where(open_face, above_water, nothing)
        flow = above_water - below_water
        out = jnp.maximum(above_total, 0.0) + jnp.maximum(-below_total, 0.0)

        total, water = flows(here, [pltpu.roll(x, rows - 1, 0) for x in here], 0.0)
        total = jnp.where(row == rows - 1, 0.0, total)
        water = jnp.where(row == rows - 1, 0.0, water)
        flow = flow + (water - pltpu.roll(water, 1, 0))
        out = out + (jnp.maximum(total, 0.0) + jnp.maximum(-pltpu.roll(total, 1, 0), 0.0))

        total, water = flows(here, [pltpu.roll(x, cols - 1, 1) for x in here], 0.0)
        to_low = lax.rem(cols - d, cols)
        low = [jnp.where(lane == 0, pltpu.roll(colflow[i], to_low, 1), pltpu.roll(x, 1, 1))
               for i, x in ((0, total), (1, water))]
        high = [jnp.where(lane == cols - 1, pltpu.roll(colflow[i], cols - 1 - d, 1), x)
                for i, x in ((2, total), (3, water))]
        flow = flow + (high[1] - low[1])
        out = out + (jnp.maximum(high[0], 0.0) + jnp.maximum(-low[0], 0.0))
        net[d] = flow
        return above_total, above_water, jnp.maximum(most, out)

    _, _, most = lax.fori_loop(0, depth, transport, (under_total, under_water, nothing))

    maxw[w] = jnp.max(most.reshape(rows // brick_rows, brick_rows, cols), axis=0)
    everyone("wide", lambda peer: maxw.at[w], lambda sender: maxw.at[sender])()
    maxn[k] = jnp.max(maxw[...], axis=0)
    everyone("narrow", lambda peer: maxn.at[k], lambda sender: maxn.at[sender])()
    top_rate = jnp.max(jnp.max(maxn[...], axis=0), axis=(0, 1), keepdims=True)
    step_size = courant / (top_rate + tiny)

    def update(d, carry):
        total, cross, packed_low, packed_high = carry
        s = sat_ref[d] - step_size * net[d] + step_size * source[...]
        satnew_ref[d] = s
        value = fields[d + 1, 1] * (gains[d, 0] * s * s + gains[d, 1] * (1.0 - s) * (1.0 - s))
        at = pl.multiple_of(d * brick_rows, brick_rows)
        for p in range(n_wide):
            slab[p, pl.ds(at, brick_rows), :] = value[p * brick_rows:(p + 1) * brick_rows]
        turned = pltpu.roll(value, d, 1)
        packed_low = jnp.where(lane == d, turned, packed_low)
        packed_high = jnp.where(lane == lax.rem(d + cols - 1, cols), turned, packed_high)
        cross = cross + harmonic(value, pltpu.roll(value, rows - 1, 0))
        return total + value, cross, packed_low, packed_high

    total, cross, packed_low, packed_high = lax.fori_loop(
        0, depth, update, (nothing, nothing, blank, blank)
    )
    sidepack[0] = packed_low
    sidepack[1] = pltpu.roll(packed_high, 1, 1)
    wait_sides = neighbours(
        "narrow", sidepack.at[0], sidepack.at[1], sidehalo.at[0], sidehalo.at[1]
    )

    def part(sender):
        return coef.at[pl.ds(pl.multiple_of(sender * band, band), band), :]

    wait_bricks = everyone("wide", lambda peer: slab.at[peer], part)
    coef[pl.ds(pl.multiple_of(w * band, band), band), :] = slab[w]

    brick_count = n_wide

    def by_brick(block):
        summed = jnp.sum(block.reshape(brick_count, brick_rows, cols), axis=1)
        return jnp.sum(summed, axis=1, keepdims=True)

    clane = lax.broadcasted_iota(jnp.int32, (brick_count, cols), 1)
    crow = lax.broadcasted_iota(jnp.int32, (brick_count, cols), 0)
    high_rows = by_brick(jnp.where((lax.rem(row, brick_rows) == brick_rows - 1) & (row < rows - 1), cross, 0.0))
    low_rows = by_brick(
        pltpu.roll(jnp.where((lax.rem(row, brick_rows) == brick_rows - 1) & (row < rows - 1), cross, 0.0), 1, 0)
    )
    coef_sum = by_brick(total)
    wait_sides()
    low_cols = by_brick(jnp.where((lane < depth) & has_left, harmonic(sidepack[0], sidehalo[0]), 0.0))
    high_cols = by_brick(jnp.where((lane < depth) & has_right, harmonic(sidepack[1], sidehalo[1]), 0.0))
    diagonal = compress * coef_sum + low_rows + high_rows + low_cols + high_cols
    message = jnp.where((clane == 0) & (crow == w), res_total, 0.0)
    for i, value in enumerate((diagonal, low_rows, high_rows, low_cols, high_cols)):
        message = jnp.where(clane == i + 1, value, message)
    cw[w] = message
    everyone("wide", lambda peer: cw.at[w], lambda sender: cw.at[sender])()

    def at_narrow(sender):
        return cn.at[pl.ds(pl.multiple_of(sender * n_wide, n_wide), n_wide), :]

    cn[pl.ds(pl.multiple_of(k * n_wide, n_wide), n_wide), :] = jnp.sum(cw[...], axis=0)
    wait_coarse = everyone("narrow", lambda peer: at_narrow(k), at_narrow)
    wait_bricks()

    last_row = brick_rows - 1

    def send_sides(ref, which):
        rowsend[0, which] = ref[pl.ds(0, layers, stride=brick_rows), :]
        rowsend[1, which] = ref[pl.ds(last_row, layers, stride=brick_rows), :]
        wait_rows = neighbours(
            "wide", rowsend.at[0, which], rowsend.at[1, which],
            rowhalo.at[0, which], rowhalo.at[1, which],
        )
        for t in range(tiles):
            def collect(i, carry):
                low, high = carry
                for u in range(32):
                    z = i * 32 + u
                    at = pl.multiple_of((t * cols + z) * brick_rows, brick_rows)
                    turned = pltpu.roll(ref[pl.ds(at, brick_rows), :], z, 1)
                    low = jnp.where(tlane == z, turned, low)
                    high = jnp.where(tlane == lax.rem(z + cols - 1, cols), turned, high)
                return low, high

            low, high = lax.fori_loop(0, cols // 32, collect, (zero, zero))
            packs[0, which, pl.ds(t * brick_rows, brick_rows), :] = low
            packs[1, which, pl.ds(t * brick_rows, brick_rows), :] = pltpu.roll(high, 1, 1)
        wait_packs = neighbours(
            "narrow", packs.at[0, which], packs.at[1, which],
            packhalo.at[0, which], packhalo.at[1, which],
        )
        return wait_rows, wait_packs

    wait_rows, wait_packs = send_sides(coef, 0)

    unroll = 16

    def at_layer(z):
        return pl.ds(pl.multiple_of(z * brick_rows, brick_rows), brick_rows)

    def assemble(i, carry):
        below, here = carry
        for u in range(unroll):
            z = i * unroll + u
            above = coef[at_layer(z + 1), :]
            df = jnp.where(z < layers - 1, harmonic(here, above), zero)
            rf = jnp.where(trow == last_row, 0.0, harmonic(here, pltpu.roll(here, last_row, 0)))
            cf = jnp.where(tlane == cols - 1, 0.0, harmonic(here, pltpu.roll(here, cols - 1, 1)))
            diag = (
                compress * here + below + df + pltpu.roll(rf, 1, 0) + rf + pltpu.roll(cf, 1, 1) + cf
            )
            sc = relax / diag
            dface[at_layer(z), :] = df
            rface[at_layer(z), :] = rf
            cface[at_layer(z), :] = cf
            scale[at_layer(z), :] = sc
            v = sc * res_ref[z]
            first[at_layer(z), :] = v
            va[at_layer(z), :] = v
            below, here = df, above
        return below, here

    lax.fori_loop(0, layers // unroll, assemble, (zero, coef[pl.ds(0, brick_rows), :]))

    def sweep(src, dst):
        def body(i, carry):
            v_below, d_below, v = carry
            for u in range(32):
                z = i * 32 + u
                v_above = src[at_layer(z + 1), :]
                df = dface[at_layer(z), :]
                rf = rface[at_layer(z), :]
                cf = cface[at_layer(z), :]
                off = (
                    d_below * v_below + df * v_above
                    + pltpu.roll(rf * v, 1, 0) + rf * pltpu.roll(v, last_row, 0)
                    + pltpu.roll(cf * v, 1, 1) + cf * pltpu.roll(v, cols - 1, 1)
                )
                dst[at_layer(z), :] = (
                    (1.0 - relax) * v + first[at_layer(z), :] + scale[at_layer(z), :] * off
                )
                v_below, d_below, v = v, df, v_above
            return v_below, d_below, v

        lax.fori_loop(0, layers // 32, body, (zero, zero, src[pl.ds(0, brick_rows), :]))

    bricks = n_wide * n_narrow
    blane = lax.broadcasted_iota(jnp.int32, (bricks, cols), 1)
    brow = lax.broadcasted_iota(jnp.int32, (bricks, cols), 0)

    mine = k * n_wide + w

    def coarse_solve():
        gathered = cn[...]
        matrix = jnp.where(blane == brow, gathered[:, 1:2], 0.0)
        for i, away in ((2, -1), (3, 1), (4, -n_wide), (5, n_wide)):
            matrix = jnp.where(blane == brow + away, matrix - gathered[:, i:i + 1], matrix)
        right = jnp.broadcast_to(gathered[:, 0:1], (bricks, cols))
        for j in range(bricks):
            column = jnp.broadcast_to(matrix[:, j:j + 1], (bricks, cols))
            factor = jnp.where(brow == j, 0.0, column / column[j:j + 1])
            matrix, right = (
                matrix - factor * matrix[j:j + 1], right - factor * right[j:j + 1]
            )
        own = brow == mine
        pivot = jnp.sum(jnp.where(own & (blane == mine), matrix, 0.0), axis=(0, 1), keepdims=True)
        answer = jnp.sum(jnp.where(own & (blane == 0), right, 0.0), axis=(0, 1), keepdims=True)
        return answer / pivot

    src, dst = va, vb
    for number in range(SWEEPS - 1):
        sweep(src, dst)
        src, dst = dst, src
    wait_value_rows, wait_value_packs = send_sides(src, 1)
    wait_coarse()
    coarse_value = coarse_solve()

    wait_rows()
    wait_packs()
    wait_value_rows()
    wait_value_packs()
    for side, present in ((0, has_below), (1, has_above)):
        c = jnp.where(present, rowhalo[side, 0], 0.0)
        rowterm[side, 0] = c
        rowterm[side, 1] = jnp.where(present, c * rowhalo[side, 1], 0.0)
    for side, present in ((0, has_left), (1, has_right)):
        c = jnp.where(present, packhalo[side, 0], 0.0)
        packterm[side, 0] = c
        packterm[side, 1] = jnp.where(present, c * packhalo[side, 1], 0.0)

    for t in range(tiles):
        tile = pl.ds(t * brick_rows, brick_rows)

        def average(i, carry):
            for u in range(unroll):
                z = i * unroll + u
                layer = t * cols + z
                c = coef[at_layer(layer), :]
                sums = [c, c * src[at_layer(layer), :]]
                for j in range(2):
                    low = rowterm[0, j, pl.ds(layer, 1), :]
                    high = rowterm[1, j, pl.ds(layer, 1), :]
                    left = pltpu.roll(packterm[0, j, tile, :], lax.rem(cols - z, cols), 1)
                    right = pltpu.roll(packterm[1, j, tile, :], cols - 1 - z, 1)
                    sums[j] = (
                        sums[j]
                        + jnp.where(trow == 0, low, 0.0) + jnp.where(trow == last_row, high, 0.0)
                        + jnp.where(tlane == 0, left, 0.0)
                        + jnp.where(tlane == cols - 1, right, 0.0)
                    )
                prec_ref[layer] = sums[1] / sums[0] + coarse_value
            return carry

        lax.fori_loop(0, cols // unroll, average, 0)


def shards(n_wide, n_narrow, *args):
    sat, residual = args[0], args[6]
    depth, rows, cols = sat.shape
    layers, brick_rows, _ = residual.shape
    tiles = layers // cols
    bricks = n_wide * n_narrow
    cells = layers * brick_rows
    copies = 2 * 7 + 3 * (n_wide - 1) + 2 * (n_narrow - 1)
    vmem = pl.BlockSpec(memory_space=pltpu.VMEM)
    anywhere = pl.BlockSpec(memory_space=pl.ANY)
    table, wells = args[3].shape, args[4].shape

    def buffer(*shape):
        return pltpu.VMEM(shape, F32)

    return pl.pallas_call(
        functools.partial(kernel, n_wide, n_narrow),
        out_shape=(
            jax.ShapeDtypeStruct(sat.shape, F32),
            jax.ShapeDtypeStruct(residual.shape, F32),
        ),
        in_specs=[anywhere] * 7,
        out_specs=(vmem, vmem),
        scratch_shapes=[
            buffer(*sat.shape),
            buffer(*sat.shape),
            pltpu.VMEM(sat.shape, jnp.int32),
            pltpu.SMEM(table, F32),
            pltpu.SMEM(wells, jnp.int32),
            pltpu.SMEM(wells, F32),
            buffer(*residual.shape),
            buffer(depth + 2, 3, rows, cols),
            buffer(depth, 2, rows, cols),
            buffer(depth, rows, cols),
            buffer(2, rows, cols),
            buffer(2, rows, cols),
            buffer(4, rows, cols),
            buffer(rows, cols),
            buffer(n_wide, brick_rows, cols),
            buffer(n_narrow, brick_rows, cols),
            buffer(n_wide, depth * brick_rows, cols),
            buffer(cells + brick_rows, cols),
            buffer(cells, cols),
            buffer(cells, cols),
            buffer(cells, cols),
            buffer(cells, cols),
            buffer(cells, cols),
            buffer(cells + brick_rows, cols),
            buffer(cells + brick_rows, cols),
            buffer(2, 2, layers, cols),
            buffer(2, 2, layers, cols),
            buffer(2, 2, layers, cols),
            buffer(2, 2, tiles * brick_rows, cols),
            buffer(2, 2, tiles * brick_rows, cols),
            buffer(2, 2, tiles * brick_rows, cols),
            buffer(n_wide, n_wide, cols),
            buffer(bricks, cols),
            buffer(2, rows, cols),
            buffer(2, rows, cols),
            pltpu.SemaphoreType.DMA((7,)),
            pltpu.SemaphoreType.DMA((copies,)),
            pltpu.SemaphoreType.DMA((copies,)),
        ],
        compiler_params=pltpu.CompilerParams(
            collective_id=0, has_side_effects=True, vmem_limit_bytes=56 * 1024 * 1024
        ),
    )(*args)


def solution(mesh):
    placed = (
        P("wide", None, "narrow"),
        P("wide", None, "narrow"),
        P("wide", None, "narrow"),
        P(),
        P(),
        P(),
        P(None, "wide", "narrow"),
    )
    return jax.shard_map(
        functools.partial(shards, mesh.shape["wide"], mesh.shape["narrow"]),
        mesh=mesh,
        in_specs=placed,
        out_specs=(P("wide", None, "narrow"), P(None, "wide", "narrow")),
        check_vma=False,
    )
```

```python
import functools

import jax
import jax.numpy as jnp
from jax import lax
from jax.experimental import pallas as pl
from jax.experimental.pallas import tpu as pltpu
from jax.sharding import PartitionSpec as P

SWEEPS = 6

compress = 0.05
relax = 0.8
gravity = 0.5
courant = 0.5
tiny = 1e-06

F32 = jnp.float32


def harmonic(a, b):
    return 2.0 * a * b / (a + b)


def flows(low, high, lift):
    total = harmonic(low[1], high[1]) * (low[0] - high[0] + lift)
    return total, total * jnp.where(total > 0, low[2], high[2])


def lookup(bits, table_ref, row, count):
    level = [table_ref[row, i] for i in range(count)]
    for bit in bits:
        level = [jnp.where(bit, level[i + 1], level[i]) for i in range(0, len(level), 2)]
    return level[0]


def kernel(
    n_wide, n_narrow,
    sat_in, pres_in, rock_in, table_in, wcol_in, wrate_in, res_in,
    satnew_out, prec_out,
    satnew_ref, prec_ref, outs,
    sat_ref, pres_ref, rock_ref, table_ref, wcol_ref, wrate_ref, res_ref,
    fields, gains, net, colpack, colhalo, colflow, source, maxw, maxn,
    slab, coef, dface, rface, cface, scale, first, va, vb,
    rowsend, rowhalo, rowterm, packs, packhalo, packterm, cw, cn, sidepack, sidehalo,
    loads, stores, sends, recvs,
):
    depth, rows, cols = sat_ref.shape
    layers, brick_rows, _ = res_ref.shape
    w = lax.axis_index("wide")
    k = lax.axis_index("narrow")
    tiles = layers // cols
    band = depth * brick_rows
    has = {"wide": (w > 0, w < n_wide - 1), "narrow": (k > 0, k < n_narrow - 1)}
    place = {"wide": w, "narrow": k}
    size = {"wide": n_wide, "narrow": n_narrow}
    count = [0]

    loading = [
        pltpu.make_async_copy(src, dst, loads.at[i])
        for i, (src, dst) in enumerate((
            (table_in, table_ref), (rock_in, rock_ref), (sat_in, sat_ref), (pres_in, pres_ref),
            (wcol_in, wcol_ref), (wrate_in, wrate_ref), (res_in, res_ref),
        ))
    ]
    for copy in loading:
        copy.start()

    def slot():
        count[0] += 1
        return count[0] - 1

    barrier = pltpu.get_barrier_semaphore()
    for axis in ("wide", "narrow"):
        for off in range(1, size[axis]):
            peer = lax.rem(place[axis] + off, size[axis])
            pl.semaphore_signal(
                barrier, inc=1, device_id={axis: peer}, device_id_type=pl.DeviceIdType.MESH
            )

    def remote(src, dst, number, axis, peer):
        return pltpu.make_async_remote_copy(
            src_ref=src, dst_ref=dst, send_sem=sends.at[number], recv_sem=recvs.at[number],
            device_id={axis: peer}, device_id_type=pl.DeviceIdType.MESH,
        )

    def neighbours(axis, low_src, high_src, from_low, from_high):
        down, up = slot(), slot()
        me = place[axis]
        has_low, has_high = has[axis]

        @pl.when(has_low)
        def _():
            remote(low_src, from_high, down, axis, me - 1).start()

        @pl.when(has_high)
        def _():
            remote(high_src, from_low, up, axis, me + 1).start()

        def wait():
            @pl.when(has_low)
            def _():
                remote(low_src, from_high, down, axis, me - 1).wait_send()
                remote(high_src, from_low, up, axis, me - 1).wait_recv()

            @pl.when(has_high)
            def _():
                remote(high_src, from_low, up, axis, me + 1).wait_send()
                remote(low_src, from_high, down, axis, me + 1).wait_recv()

        return wait

    def everyone(axis, src_of, dst_from):
        copies = []
        me = place[axis]
        n = size[axis]
        for off in range(1, n):
            number = slot()
            peer = lax.rem(me + off, n)
            copy = remote(src_of(peer), dst_from(me), number, axis, peer)
            copy.start()
            sender = lax.rem(me + n - off, n)
            copies.append((copy, remote(src_of(peer), dst_from(sender), number, axis, peer)))

        def wait():
            for sent, received in copies:
                sent.wait_send()
                received.wait_recv()

        return wait

    lane = lax.broadcasted_iota(jnp.int32, (rows, cols), 1)
    row = lax.broadcasted_iota(jnp.int32, (rows, cols), 0)
    tlane = lax.broadcasted_iota(jnp.int32, (brick_rows, cols), 1)
    trow = lax.broadcasted_iota(jnp.int32, (brick_rows, cols), 0)
    zero = jnp.zeros((brick_rows, cols), F32)
    one = jnp.ones((brick_rows, cols), F32)

    @pl.when(w == 0)
    def _():
        fields[0] = jnp.ones((3, rows, cols), F32)
        rowhalo[0] = jnp.ones((2, layers, cols), F32)

    @pl.when(w == n_wide - 1)
    def _():
        fields[depth + 1] = jnp.ones((3, rows, cols), F32)
        rowhalo[1] = jnp.ones((2, layers, cols), F32)

    @pl.when(k == 0)
    def _():
        sidehalo[0] = jnp.ones((rows, cols), F32)
        colhalo[0] = jnp.ones((rows, cols), F32)
        packhalo[0] = jnp.ones((2, tiles * brick_rows, cols), F32)

    @pl.when(k == n_narrow - 1)
    def _():
        sidehalo[1] = jnp.ones((rows, cols), F32)
        colhalo[1] = jnp.ones((rows, cols), F32)
        packhalo[1] = jnp.ones((2, tiles * brick_rows, cols), F32)

    coef[pl.ds(layers * brick_rows, brick_rows), :] = one
    va[pl.ds(layers * brick_rows, brick_rows), :] = zero
    vb[pl.ds(layers * brick_rows, brick_rows), :] = zero

    rocks = table_ref.shape[1]
    for copy in loading[:4]:
        copy.wait()

    def derive(d, carry):
        packed_low, packed_high = carry
        rock = rock_ref[d]
        bits = []
        step = 1
        while step < rocks:
            bits.append((rock & step) != 0)
            step *= 2
        perm = lookup(bits, table_ref, 0, rocks)
        water = lookup(bits, table_ref, 1, rocks)
        oil = lookup(bits, table_ref, 2, rocks)
        s = sat_ref[d]
        water_mob = water * s * s
        oil_mob = oil * (1.0 - s) * (1.0 - s)
        frac = water_mob / (water_mob + oil_mob)
        gains[d, 0] = water
        gains[d, 1] = oil
        for f, value in enumerate((pres_ref[d], perm, frac)):
            fields[d + 1, f] = value
            spot = 2 * (d + f * depth)
            turned = pltpu.roll(value, spot, 1)
            packed_low = jnp.where(lane == spot, turned, packed_low)
            packed_high = jnp.where(lane == lax.rem(spot + cols - 1, cols), turned, packed_high)
        return packed_low, packed_high

    blank = jnp.ones((rows, cols), F32)
    packed_low, packed_high = lax.fori_loop(0, depth, derive, (blank, blank))
    colpack[0] = packed_low
    colpack[1] = pltpu.roll(packed_high, 1, 1)

    pl.semaphore_wait(barrier, n_wide + n_narrow - 2)
    wait_planes = neighbours(
        "wide", fields.at[1], fields.at[depth], fields.at[0], fields.at[depth + 1]
    )
    wait_cols = neighbours(
        "narrow", colpack.at[0], colpack.at[1], colhalo.at[0], colhalo.at[1]
    )

    nothing = jnp.zeros((rows, cols), F32)
    has_below, has_above = has["wide"]
    has_left, has_right = has["narrow"]

    def plane(d):
        return [fields[d, f] for f in range(3)]

    def transport(d, carry):
        below_total, below_water = carry
        here = plane(d + 1)
        above_total, above_water = flows(here, plane(lax.min(d + 2, depth)), gravity)
        above_total = jnp.where(d < depth - 1, above_total, nothing)
        above_water = jnp.where(d < depth - 1, above_water, nothing)
        flow = above_water - below_water
        out = jnp.maximum(above_total, 0.0) + jnp.maximum(-below_total, 0.0)

        total, water = flows(here, [pltpu.roll(x, rows - 1, 0) for x in here], 0.0)
        total = jnp.where(row == rows - 1, 0.0, total)
        water = jnp.where(row == rows - 1, 0.0, water)
        flow = flow + (water - pltpu.roll(water, 1, 0))
        out = out + (jnp.maximum(total, 0.0) + jnp.maximum(-pltpu.roll(total, 1, 0), 0.0))

        total, water = flows(here, [pltpu.roll(x, cols - 1, 1) for x in here], 0.0)
        total = jnp.where(lane == cols - 1, 0.0, total)
        water = jnp.where(lane == cols - 1, 0.0, water)
        net[d] = flow + (water - pltpu.roll(water, 1, 1))
        outs[d] = out + (jnp.maximum(total, 0.0) + jnp.maximum(-pltpu.roll(total, 1, 1), 0.0))
        return above_total, above_water

    lax.fori_loop(0, depth, transport, (nothing, nothing))

    wait_cols()

    def unpack(block):
        return [block] + [pltpu.roll(block, cols - 2 * f * depth, 1) for f in (1, 2)]

    low_total, low_water = flows(unpack(colhalo[0]), unpack(colpack[0]), 0.0)
    high_total, high_water = flows(unpack(colpack[1]), unpack(colhalo[1]), 0.0)
    even = lax.rem(lane, 2) == 0
    colflow[0] = jnp.where(
        even,
        jnp.where(has_right, high_water, nothing),
        pltpu.roll(jnp.where(has_left, -low_water, nothing), 1, 1),
    )
    colflow[1] = jnp.maximum(jnp.where(
        even,
        jnp.where(has_right, high_total, nothing),
        pltpu.roll(jnp.where(has_left, -low_total, nothing), 1, 1),
    ), 0.0)

    wait_planes()
    side_total, side_water = flows(plane(0), plane(1), gravity)
    net[0] = net[0] - jnp.where(has_below, side_water, nothing)
    outs[0] = outs[0] + jnp.maximum(jnp.where(has_below, -side_total, nothing), 0.0)
    side_total, side_water = flows(plane(depth), plane(depth + 1), gravity)
    net[depth - 1] = net[depth - 1] + jnp.where(has_above, side_water, nothing)
    outs[depth - 1] = outs[depth - 1] + jnp.maximum(jnp.where(has_above, side_total, nothing), 0.0)
    edge = (lane == 0) | (lane == cols - 1)

    def add_sides(i, most):
        for u in range(2):
            d = i * 2 + u
            turn = cols - 1 - 2 * d
            net[d] = net[d] + jnp.where(edge, pltpu.roll(colflow[0], turn, 1), 0.0)
            most = jnp.maximum(
                most, outs[d] + jnp.where(edge, pltpu.roll(colflow[1], turn, 1), 0.0)
            )
        return most

    most = lax.fori_loop(0, depth // 2, add_sides, nothing)

    maxw[w] = jnp.max(most.reshape(rows // brick_rows, brick_rows, cols), axis=0)
    wait_wide = everyone("wide", lambda peer: maxw.at[w], lambda sender: maxw.at[sender])

    all_cols = cols * n_narrow
    for copy in loading[4:]:
        copy.wait()
    cell = row * cols + lane

    def well(i, total):
        for u in range(8):
            column = wcol_ref[i * 8 + u]
            inside = lax.rem(column, all_cols) - k * cols
            target = lax.div(column, all_cols) * cols + inside
            target = jnp.where((inside >= 0) & (inside < cols), target, -1)
            total = total + jnp.where(cell == target, wrate_ref[i * 8 + u], 0.0)
        return total

    source[...] = lax.fori_loop(0, wcol_ref.shape[0] // 8, well, nothing)

    def add_res(i, total):
        return total + jnp.sum(res_ref[pl.ds(i * 16, 16)], axis=0)

    res_total = jnp.sum(lax.fori_loop(0, layers // 16, add_res, zero), axis=(0, 1), keepdims=True)
    wait_wide()
    maxn[k] = jnp.max(maxw[...], axis=0)
    everyone("narrow", lambda peer: maxn.at[k], lambda sender: maxn.at[sender])()
    top_rate = jnp.max(jnp.max(maxn[...], axis=0), axis=(0, 1), keepdims=True)
    step_size = courant / (top_rate + tiny)

    def update(d, carry):
        total, cross, packed_low, packed_high = carry
        s = sat_ref[d] - step_size * net[d] + step_size * source[...]
        satnew_ref[d] = s
        value = fields[d + 1, 1] * (gains[d, 0] * s * s + gains[d, 1] * (1.0 - s) * (1.0 - s))
        at = pl.multiple_of(d * brick_rows, brick_rows)
        for p in range(n_wide):
            slab[p, pl.ds(at, brick_rows), :] = value[p * brick_rows:(p + 1) * brick_rows]
        turned = pltpu.roll(value, d, 1)
        packed_low = jnp.where(lane == d, turned, packed_low)
        packed_high = jnp.where(lane == lax.rem(d + cols - 1, cols), turned, packed_high)
        cross = cross + harmonic(value, pltpu.roll(value, rows - 1, 0))
        return total + value, cross, packed_low, packed_high

    total, cross, packed_low, packed_high = lax.fori_loop(
        0, depth, update, (nothing, nothing, blank, blank)
    )
    storing = pltpu.make_async_copy(satnew_ref, satnew_out, loads.at[0])
    storing.start()
    sidepack[0] = packed_low
    sidepack[1] = pltpu.roll(packed_high, 1, 1)
    wait_sides = neighbours(
        "narrow", sidepack.at[0], sidepack.at[1], sidehalo.at[0], sidehalo.at[1]
    )

    def part(sender):
        return coef.at[pl.ds(pl.multiple_of(sender * band, band), band), :]

    wait_bricks = everyone("wide", lambda peer: slab.at[peer], part)
    coef[pl.ds(pl.multiple_of(w * band, band), band), :] = slab[w]

    brick_count = n_wide

    def by_brick(block):
        summed = jnp.sum(block.reshape(brick_count, brick_rows, cols), axis=1)
        return jnp.sum(summed, axis=1, keepdims=True)

    clane = lax.broadcasted_iota(jnp.int32, (brick_count, cols), 1)
    crow = lax.broadcasted_iota(jnp.int32, (brick_count, cols), 0)
    high_rows = by_brick(jnp.where((lax.rem(row, brick_rows) == brick_rows - 1) & (row < rows - 1), cross, 0.0))
    low_rows = by_brick(
        pltpu.roll(jnp.where((lax.rem(row, brick_rows) == brick_rows - 1) & (row < rows - 1), cross, 0.0), 1, 0)
    )
    coef_sum = by_brick(total)
    wait_sides()
    low_cols = by_brick(jnp.where((lane < depth) & has_left, harmonic(sidepack[0], sidehalo[0]), 0.0))
    high_cols = by_brick(jnp.where((lane < depth) & has_right, harmonic(sidepack[1], sidehalo[1]), 0.0))
    diagonal = compress * coef_sum + low_rows + high_rows + low_cols + high_cols
    message = jnp.where((clane == 0) & (crow == w), res_total, 0.0)
    for i, value in enumerate((diagonal, low_rows, high_rows, low_cols, high_cols)):
        message = jnp.where(clane == i + 1, value, message)
    cw[w] = message
    everyone("wide", lambda peer: cw.at[w], lambda sender: cw.at[sender])()

    def at_narrow(sender):
        return cn.at[pl.ds(pl.multiple_of(sender * n_wide, n_wide), n_wide), :]

    cn[pl.ds(pl.multiple_of(k * n_wide, n_wide), n_wide), :] = jnp.sum(cw[...], axis=0)
    wait_coarse = everyone("narrow", lambda peer: at_narrow(k), at_narrow)
    wait_bricks()

    last_row = brick_rows - 1

    def send_sides(ref, which):
        rowsend[0, which] = ref[pl.ds(0, layers, stride=brick_rows), :]
        rowsend[1, which] = ref[pl.ds(last_row, layers, stride=brick_rows), :]
        wait_rows = neighbours(
            "wide", rowsend.at[0, which], rowsend.at[1, which],
            rowhalo.at[0, which], rowhalo.at[1, which],
        )
        for t in range(tiles):
            def collect(i, carry):
                low, high = carry
                for u in range(32):
                    z = i * 32 + u
                    at = pl.multiple_of((t * cols + z) * brick_rows, brick_rows)
                    turned = pltpu.roll(ref[pl.ds(at, brick_rows), :], z, 1)
                    low = jnp.where(tlane == z, turned, low)
                    high = jnp.where(tlane == lax.rem(z + cols - 1, cols), turned, high)
                return low, high

            low, high = lax.fori_loop(0, cols // 32, collect, (zero, zero))
            packs[0, which, pl.ds(t * brick_rows, brick_rows), :] = low
            packs[1, which, pl.ds(t * brick_rows, brick_rows), :] = pltpu.roll(high, 1, 1)
        wait_packs = neighbours(
            "narrow", packs.at[0, which], packs.at[1, which],
            packhalo.at[0, which], packhalo.at[1, which],
        )
        return wait_rows, wait_packs

    wait_rows, wait_packs = send_sides(coef, 0)

    unroll = 16

    def at_layer(z):
        return pl.ds(pl.multiple_of(z * brick_rows, brick_rows), brick_rows)

    def assemble(i, carry):
        below, here = carry
        for u in range(unroll):
            z = i * unroll + u
            above = coef[at_layer(z + 1), :]
            df = jnp.where(z < layers - 1, harmonic(here, above), zero)
            rf = jnp.where(trow == last_row, 0.0, harmonic(here, pltpu.roll(here, last_row, 0)))
            cf = jnp.where(tlane == cols - 1, 0.0, harmonic(here, pltpu.roll(here, cols - 1, 1)))
            diag = (
                compress * here + below + df + pltpu.roll(rf, 1, 0) + rf + pltpu.roll(cf, 1, 1) + cf
            )
            sc = relax / diag
            dface[at_layer(z), :] = df
            rface[at_layer(z), :] = rf
            cface[at_layer(z), :] = cf
            scale[at_layer(z), :] = sc
            v = sc * res_ref[z]
            first[at_layer(z), :] = v
            va[at_layer(z), :] = v
            below, here = df, above
        return below, here

    lax.fori_loop(0, layers // unroll, assemble, (zero, coef[pl.ds(0, brick_rows), :]))

    def sweep(src, dst):
        def body(i, carry):
            v_below, d_below, v = carry
            for u in range(32):
                z = i * 32 + u
                v_above = src[at_layer(z + 1), :]
                df = dface[at_layer(z), :]
                rf = rface[at_layer(z), :]
                cf = cface[at_layer(z), :]
                off = (
                    d_below * v_below + df * v_above
                    + pltpu.roll(rf * v, 1, 0) + rf * pltpu.roll(v, last_row, 0)
                    + pltpu.roll(cf * v, 1, 1) + cf * pltpu.roll(v, cols - 1, 1)
                )
                dst[at_layer(z), :] = (
                    (1.0 - relax) * v + first[at_layer(z), :] + scale[at_layer(z), :] * off
                )
                v_below, d_below, v = v, df, v_above
            return v_below, d_below, v

        lax.fori_loop(0, layers // 32, body, (zero, zero, src[pl.ds(0, brick_rows), :]))

    bricks = n_wide * n_narrow
    blane = lax.broadcasted_iota(jnp.int32, (bricks, cols), 1)
    brow = lax.broadcasted_iota(jnp.int32, (bricks, cols), 0)

    mine = k * n_wide + w

    def coarse_solve():
        gathered = cn[...]
        matrix = jnp.where(blane == brow, gathered[:, 1:2], 0.0)
        for i, away in ((2, -1), (3, 1), (4, -n_wide), (5, n_wide)):
            matrix = jnp.where(blane == brow + away, matrix - gathered[:, i:i + 1], matrix)
        right = jnp.broadcast_to(gathered[:, 0:1], (bricks, cols))
        def pivoted(j, block, side):
            column = jnp.broadcast_to(block[:, j:j + 1], (bricks, cols))
            factor = jnp.where(brow == j, 0.0, column / column[j:j + 1])
            return factor * block[j:j + 1], factor * side[j:j + 1]

        def colour(j):
            return (j // n_wide + j % n_wide) % 2

        block, side = matrix, right
        for j in range(bricks):
            if colour(j) == 0:
                change, side_change = pivoted(j, block, side)
                matrix, right = matrix - change, right - side_change
        for j in range(bricks):
            if colour(j) == 1:
                change, side_change = pivoted(j, matrix, right)
                matrix, right = matrix - change, right - side_change
        own = brow == mine
        pivot = jnp.sum(jnp.where(own & (blane == mine), matrix, 0.0), axis=(0, 1), keepdims=True)
        answer = jnp.sum(jnp.where(own & (blane == 0), right, 0.0), axis=(0, 1), keepdims=True)
        return answer / pivot

    src, dst = va, vb
    for number in range(SWEEPS - 1):
        sweep(src, dst)
        src, dst = dst, src
    wait_value_rows, wait_value_packs = send_sides(src, 1)
    wait_coarse()
    coarse_value = coarse_solve()

    wait_rows()
    wait_packs()
    wait_value_rows()
    wait_value_packs()
    for side, present in ((0, has_below), (1, has_above)):
        c = jnp.where(present, rowhalo[side, 0], 0.0)
        rowterm[side, 0] = c
        rowterm[side, 1] = jnp.where(present, c * rowhalo[side, 1], 0.0)
    for side, present in ((0, has_left), (1, has_right)):
        c = jnp.where(present, packhalo[side, 0], 0.0)
        packterm[side, 0] = c
        packterm[side, 1] = jnp.where(present, c * packhalo[side, 1], 0.0)

    def store(i):
        part = pl.ds(i * unroll, unroll)
        return pltpu.make_async_copy(prec_ref.at[part], prec_out.at[part], stores.at[i])

    for t in range(tiles):
        tile = pl.ds(t * brick_rows, brick_rows)

        def average(i, carry):
            for u in range(unroll):
                z = i * unroll + u
                layer = t * cols + z
                c = coef[at_layer(layer), :]
                sums = [c, c * src[at_layer(layer), :]]
                for j in range(2):
                    low = rowterm[0, j, pl.ds(layer, 1), :]
                    high = rowterm[1, j, pl.ds(layer, 1), :]
                    left = pltpu.roll(packterm[0, j, tile, :], lax.rem(cols - z, cols), 1)
                    right = pltpu.roll(packterm[1, j, tile, :], cols - 1 - z, 1)
                    sums[j] = (
                        sums[j]
                        + jnp.where(trow == 0, low, 0.0) + jnp.where(trow == last_row, high, 0.0)
                        + jnp.where(tlane == 0, left, 0.0)
                        + jnp.where(tlane == cols - 1, right, 0.0)
                    )
                prec_ref[layer] = sums[1] / sums[0] + coarse_value
            store(t * (cols // unroll) + i).start()
            return carry

        lax.fori_loop(0, cols // unroll, average, 0)

    storing.wait()
    for i in range(layers // unroll):
        store(i).wait()


def deliver(a_in, b_in, a_out, b_out, sems):
    copies = []
    for src, dst in ((a_in, a_out), (b_in, b_out)):
        part = src.shape[0] // 4
        for i in range(4):
            at = pl.ds(i * part, part)
            copies.append(pltpu.make_async_copy(src.at[at], dst.at[at], sems.at[len(copies)]))
            copies[-1].start()
    for copy in copies:
        copy.wait()


def shards(n_wide, n_narrow, *args):
    sat, residual = args[0], args[6]
    depth, rows, cols = sat.shape
    layers, brick_rows, _ = residual.shape
    tiles = layers // cols
    bricks = n_wide * n_narrow
    cells = layers * brick_rows
    copies = 2 * 7 + 3 * (n_wide - 1) + 2 * (n_narrow - 1)
    anywhere = pl.BlockSpec(memory_space=pl.ANY)
    table, wells = args[3].shape, args[4].shape

    def buffer(*shape):
        return pltpu.VMEM(shape, F32)

    outputs = pl.pallas_call(
        functools.partial(kernel, n_wide, n_narrow),
        out_shape=(
            jax.ShapeDtypeStruct(sat.shape, F32),
            jax.ShapeDtypeStruct(residual.shape, F32),
        ),
        in_specs=[anywhere] * 7,
        out_specs=(anywhere, anywhere),
        scratch_shapes=[
            buffer(*sat.shape),
            buffer(*residual.shape),
            buffer(*sat.shape),
            buffer(*sat.shape),
            buffer(*sat.shape),
            pltpu.VMEM(sat.shape, jnp.int32),
            pltpu.SMEM(table, F32),
            pltpu.SMEM(wells, jnp.int32),
            pltpu.SMEM(wells, F32),
            buffer(*residual.shape),
            buffer(depth + 2, 3, rows, cols),
            buffer(depth, 2, rows, cols),
            buffer(depth, rows, cols),
            buffer(2, rows, cols),
            buffer(2, rows, cols),
            buffer(2, rows, cols),
            buffer(rows, cols),
            buffer(n_wide, brick_rows, cols),
            buffer(n_narrow, brick_rows, cols),
            buffer(n_wide, depth * brick_rows, cols),
            buffer(cells + brick_rows, cols),
            buffer(cells, cols),
            buffer(cells, cols),
            buffer(cells, cols),
            buffer(cells, cols),
            buffer(cells, cols),
            buffer(cells + brick_rows, cols),
            buffer(cells + brick_rows, cols),
            buffer(2, 2, layers, cols),
            buffer(2, 2, layers, cols),
            buffer(2, 2, layers, cols),
            buffer(2, 2, tiles * brick_rows, cols),
            buffer(2, 2, tiles * brick_rows, cols),
            buffer(2, 2, tiles * brick_rows, cols),
            buffer(n_wide, n_wide, cols),
            buffer(bricks, cols),
            buffer(2, rows, cols),
            buffer(2, rows, cols),
            pltpu.SemaphoreType.DMA((7,)),
            pltpu.SemaphoreType.DMA((layers // 16,)),
            pltpu.SemaphoreType.DMA((copies,)),
            pltpu.SemaphoreType.DMA((copies,)),
        ],
        compiler_params=pltpu.CompilerParams(
            collective_id=0, has_side_effects=True, vmem_limit_bytes=56 * 1024 * 1024
        ),
    )(*args)
    return pl.pallas_call(
        deliver,
        out_shape=(
            jax.ShapeDtypeStruct(sat.shape, F32),
            jax.ShapeDtypeStruct(residual.shape, F32),
        ),
        in_specs=[anywhere] * 2,
        out_specs=(anywhere, anywhere),
        scratch_shapes=[pltpu.SemaphoreType.DMA((8,))],
        compiler_params=pltpu.CompilerParams(vmem_limit_bytes=60 * 1024 * 1024),
    )(*outputs)


def solution(mesh):
    placed = (
        P("wide", None, "narrow"),
        P("wide", None, "narrow"),
        P("wide", None, "narrow"),
        P(),
        P(),
        P(),
        P(None, "wide", "narrow"),
    )
    return jax.shard_map(
        functools.partial(shards, mesh.shape["wide"], mesh.shape["narrow"]),
        mesh=mesh,
        in_specs=placed,
        out_specs=(P("wide", None, "narrow"), P(None, "wide", "narrow")),
        check_vma=False,
    )
```

```python
import functools

import jax
import jax.numpy as jnp
from jax import lax
from jax.experimental import pallas as pl
from jax.experimental.pallas import tpu as pltpu
from jax.sharding import PartitionSpec as P

SWEEPS = 6

compress = 0.05
relax = 0.8
gravity = 0.5
courant = 0.5
tiny = 1e-06

F32 = jnp.float32


def harmonic(a, b):
    return 2.0 * a * b / (a + b)


def flows(low, high, lift):
    total = harmonic(low[1], high[1]) * (low[0] - high[0] + lift)
    return total, total * jnp.where(total > 0, low[2], high[2])


def lookup(bits, table_ref, row, count):
    level = [table_ref[row, i] for i in range(count)]
    for bit in bits:
        level = [jnp.where(bit, level[i + 1], level[i]) for i in range(0, len(level), 2)]
    return level[0]


def kernel(
    n_wide, n_narrow,
    sat_in, pres_in, rock_in, table_in, wcol_in, wrate_in, res_in,
    satnew_out, prec_out,
    satnew_ref, prec_ref, outs,
    sat_ref, pres_ref, rock_ref, table_ref, wcol_ref, wrate_ref, res_ref,
    fields, gains, net, colpack, colhalo, colflow, source, maxw, maxn,
    slab, coef, dface, rface, cface, scale, first, va, vb,
    rowsend, rowhalo, rowterm, packs, packhalo, packterm, cw, cn, sidepack, sidehalo,
    loads, stores, sends, recvs,
):
    depth, rows, cols = sat_ref.shape
    layers, brick_rows, _ = res_ref.shape
    w = lax.axis_index("wide")
    k = lax.axis_index("narrow")
    tiles = layers // cols
    band = depth * brick_rows
    has = {"wide": (w > 0, w < n_wide - 1), "narrow": (k > 0, k < n_narrow - 1)}
    place = {"wide": w, "narrow": k}
    size = {"wide": n_wide, "narrow": n_narrow}
    count = [0]

    loading = [
        pltpu.make_async_copy(src, dst, loads.at[i])
        for i, (src, dst) in enumerate((
            (table_in, table_ref), (rock_in, rock_ref), (sat_in, sat_ref), (pres_in, pres_ref),
            (wcol_in, wcol_ref), (wrate_in, wrate_ref), (res_in, res_ref),
        ))
    ]
    for copy in loading:
        copy.start()

    def slot():
        count[0] += 1
        return count[0] - 1

    barrier = pltpu.get_barrier_semaphore()
    for axis in ("wide", "narrow"):
        for off in range(1, size[axis]):
            peer = lax.rem(place[axis] + off, size[axis])
            pl.semaphore_signal(
                barrier, inc=1, device_id={axis: peer}, device_id_type=pl.DeviceIdType.MESH
            )

    def remote(src, dst, number, axis, peer):
        return pltpu.make_async_remote_copy(
            src_ref=src, dst_ref=dst, send_sem=sends.at[number], recv_sem=recvs.at[number],
            device_id={axis: peer}, device_id_type=pl.DeviceIdType.MESH,
        )

    def neighbours(axis, low_src, high_src, from_low, from_high):
        down, up = slot(), slot()
        me = place[axis]
        has_low, has_high = has[axis]

        @pl.when(has_low)
        def _():
            remote(low_src, from_high, down, axis, me - 1).start()

        @pl.when(has_high)
        def _():
            remote(high_src, from_low, up, axis, me + 1).start()

        def wait():
            @pl.when(has_low)
            def _():
                remote(low_src, from_high, down, axis, me - 1).wait_send()
                remote(high_src, from_low, up, axis, me - 1).wait_recv()

            @pl.when(has_high)
            def _():
                remote(high_src, from_low, up, axis, me + 1).wait_send()
                remote(low_src, from_high, down, axis, me + 1).wait_recv()

        return wait

    def everyone(axis, src_of, dst_from):
        copies = []
        me = place[axis]
        n = size[axis]
        for off in range(1, n):
            number = slot()
            peer = lax.rem(me + off, n)
            copy = remote(src_of(peer), dst_from(me), number, axis, peer)
            copy.start()
            sender = lax.rem(me + n - off, n)
            copies.append((copy, remote(src_of(peer), dst_from(sender), number, axis, peer)))

        def wait():
            for sent, received in copies:
                sent.wait_send()
                received.wait_recv()

        return wait

    lane = lax.broadcasted_iota(jnp.int32, (rows, cols), 1)
    row = lax.broadcasted_iota(jnp.int32, (rows, cols), 0)
    tlane = lax.broadcasted_iota(jnp.int32, (brick_rows, cols), 1)
    trow = lax.broadcasted_iota(jnp.int32, (brick_rows, cols), 0)
    zero = jnp.zeros((brick_rows, cols), F32)
    one = jnp.ones((brick_rows, cols), F32)

    @pl.when(w == 0)
    def _():
        fields[0] = jnp.ones((3, rows, cols), F32)
        rowhalo[0] = jnp.ones((2, layers, cols), F32)

    @pl.when(w == n_wide - 1)
    def _():
        fields[depth + 1] = jnp.ones((3, rows, cols), F32)
        rowhalo[1] = jnp.ones((2, layers, cols), F32)

    @pl.when(k == 0)
    def _():
        sidehalo[0] = jnp.ones((rows, cols), F32)
        colhalo[0] = jnp.ones((rows, cols), F32)
        packhalo[0] = jnp.ones((2, tiles * brick_rows, cols), F32)

    @pl.when(k == n_narrow - 1)
    def _():
        sidehalo[1] = jnp.ones((rows, cols), F32)
        colhalo[1] = jnp.ones((rows, cols), F32)
        packhalo[1] = jnp.ones((2, tiles * brick_rows, cols), F32)

    coef[pl.ds(layers * brick_rows, brick_rows), :] = one
    va[pl.ds(layers * brick_rows, brick_rows), :] = zero
    vb[pl.ds(layers * brick_rows, brick_rows), :] = zero

    rocks = table_ref.shape[1]
    for copy in loading[:4]:
        copy.wait()

    def derive(d, carry):
        packed_low, packed_high = carry
        rock = rock_ref[d]
        bits = []
        step = 1
        while step < rocks:
            bits.append((rock & step) != 0)
            step *= 2
        perm = lookup(bits, table_ref, 0, rocks)
        water = lookup(bits, table_ref, 1, rocks)
        oil = lookup(bits, table_ref, 2, rocks)
        s = sat_ref[d]
        water_mob = water * s * s
        oil_mob = oil * (1.0 - s) * (1.0 - s)
        frac = water_mob / (water_mob + oil_mob)
        gains[d, 0] = water
        gains[d, 1] = oil
        for f, value in enumerate((pres_ref[d], perm, frac)):
            fields[d + 1, f] = value
            spot = 2 * (d + f * depth)
            turned = pltpu.roll(value, spot, 1)
            packed_low = jnp.where(lane == spot, turned, packed_low)
            packed_high = jnp.where(lane == lax.rem(spot + cols - 1, cols), turned, packed_high)
        return packed_low, packed_high

    blank = jnp.ones((rows, cols), F32)
    packed_low, packed_high = lax.fori_loop(0, depth, derive, (blank, blank))
    colpack[0] = packed_low
    colpack[1] = pltpu.roll(packed_high, 1, 1)

    pl.semaphore_wait(barrier, n_wide + n_narrow - 2)
    wait_planes = neighbours(
        "wide", fields.at[1], fields.at[depth], fields.at[0], fields.at[depth + 1]
    )
    wait_cols = neighbours(
        "narrow", colpack.at[0], colpack.at[1], colhalo.at[0], colhalo.at[1]
    )

    nothing = jnp.zeros((rows, cols), F32)
    has_below, has_above = has["wide"]
    has_left, has_right = has["narrow"]

    def plane(d):
        return [fields[d, f] for f in range(3)]

    def transport(d, carry):
        below_total, below_water = carry
        here = plane(d + 1)
        above_total, above_water = flows(here, plane(lax.min(d + 2, depth)), gravity)
        above_total = jnp.where(d < depth - 1, above_total, nothing)
        above_water = jnp.where(d < depth - 1, above_water, nothing)
        flow = above_water - below_water
        out = jnp.maximum(above_total, 0.0) + jnp.maximum(-below_total, 0.0)

        total, water = flows(here, [pltpu.roll(x, rows - 1, 0) for x in here], 0.0)
        total = jnp.where(row == rows - 1, 0.0, total)
        water = jnp.where(row == rows - 1, 0.0, water)
        flow = flow + (water - pltpu.roll(water, 1, 0))
        out = out + (jnp.maximum(total, 0.0) + jnp.maximum(-pltpu.roll(total, 1, 0), 0.0))

        total, water = flows(here, [pltpu.roll(x, cols - 1, 1) for x in here], 0.0)
        total = jnp.where(lane == cols - 1, 0.0, total)
        water = jnp.where(lane == cols - 1, 0.0, water)
        net[d] = flow + (water - pltpu.roll(water, 1, 1))
        outs[d] = out + (jnp.maximum(total, 0.0) + jnp.maximum(-pltpu.roll(total, 1, 1), 0.0))
        return above_total, above_water

    lax.fori_loop(0, depth, transport, (nothing, nothing))

    wait_cols()

    def unpack(block):
        return [block] + [pltpu.roll(block, cols - 2 * f * depth, 1) for f in (1, 2)]

    low_total, low_water = flows(unpack(colhalo[0]), unpack(colpack[0]), 0.0)
    high_total, high_water = flows(unpack(colpack[1]), unpack(colhalo[1]), 0.0)
    even = lax.rem(lane, 2) == 0
    colflow[0] = jnp.where(
        even,
        jnp.where(has_right, high_water, nothing),
        pltpu.roll(jnp.where(has_left, -low_water, nothing), 1, 1),
    )
    colflow[1] = jnp.maximum(jnp.where(
        even,
        jnp.where(has_right, high_total, nothing),
        pltpu.roll(jnp.where(has_left, -low_total, nothing), 1, 1),
    ), 0.0)

    wait_planes()
    side_total, side_water = flows(plane(0), plane(1), gravity)
    net[0] = net[0] - jnp.where(has_below, side_water, nothing)
    outs[0] = outs[0] + jnp.maximum(jnp.where(has_below, -side_total, nothing), 0.0)
    side_total, side_water = flows(plane(depth), plane(depth + 1), gravity)
    net[depth - 1] = net[depth - 1] + jnp.where(has_above, side_water, nothing)
    outs[depth - 1] = outs[depth - 1] + jnp.maximum(jnp.where(has_above, side_total, nothing), 0.0)
    edge = (lane == 0) | (lane == cols - 1)

    def add_sides(i, most):
        for u in range(2):
            d = i * 2 + u
            turn = cols - 1 - 2 * d
            net[d] = net[d] + jnp.where(edge, pltpu.roll(colflow[0], turn, 1), 0.0)
            most = jnp.maximum(
                most, outs[d] + jnp.where(edge, pltpu.roll(colflow[1], turn, 1), 0.0)
            )
        return most

    most = lax.fori_loop(0, depth // 2, add_sides, nothing)

    maxw[w] = jnp.max(most.reshape(rows // brick_rows, brick_rows, cols), axis=0)
    wait_wide = everyone("wide", lambda peer: maxw.at[w], lambda sender: maxw.at[sender])

    all_cols = cols * n_narrow
    for copy in loading[4:]:
        copy.wait()
    cell = row * cols + lane

    def well(i, total):
        for u in range(8):
            column = wcol_ref[i * 8 + u]
            inside = lax.rem(column, all_cols) - k * cols
            target = lax.div(column, all_cols) * cols + inside
            target = jnp.where((inside >= 0) & (inside < cols), target, -1)
            total = total + jnp.where(cell == target, wrate_ref[i * 8 + u], 0.0)
        return total

    source[...] = lax.fori_loop(0, wcol_ref.shape[0] // 8, well, nothing)

    def add_res(i, total):
        return total + jnp.sum(res_ref[pl.ds(i * 16, 16)], axis=0)

    res_total = jnp.sum(lax.fori_loop(0, layers // 16, add_res, zero), axis=(0, 1), keepdims=True)
    wait_wide()
    maxn[k] = jnp.max(maxw[...], axis=0)
    everyone("narrow", lambda peer: maxn.at[k], lambda sender: maxn.at[sender])()
    top_rate = jnp.max(jnp.max(maxn[...], axis=0), axis=(0, 1), keepdims=True)
    step_size = courant / (top_rate + tiny)

    def update(d, carry):
        total, cross, packed_low, packed_high = carry
        s = sat_ref[d] - step_size * net[d] + step_size * source[...]
        satnew_ref[d] = s
        value = fields[d + 1, 1] * (gains[d, 0] * s * s + gains[d, 1] * (1.0 - s) * (1.0 - s))
        at = pl.multiple_of(d * brick_rows, brick_rows)
        for p in range(n_wide):
            slab[p, pl.ds(at, brick_rows), :] = value[p * brick_rows:(p + 1) * brick_rows]
        turned = pltpu.roll(value, d, 1)
        packed_low = jnp.where(lane == d, turned, packed_low)
        packed_high = jnp.where(lane == lax.rem(d + cols - 1, cols), turned, packed_high)
        cross = cross + harmonic(value, pltpu.roll(value, rows - 1, 0))
        return total + value, cross, packed_low, packed_high

    total, cross, packed_low, packed_high = lax.fori_loop(
        0, depth, update, (nothing, nothing, blank, blank)
    )
    storing = pltpu.make_async_copy(satnew_ref, satnew_out, loads.at[0])
    storing.start()
    sidepack[0] = packed_low
    sidepack[1] = pltpu.roll(packed_high, 1, 1)
    wait_sides = neighbours(
        "narrow", sidepack.at[0], sidepack.at[1], sidehalo.at[0], sidehalo.at[1]
    )

    def part(sender):
        return coef.at[pl.ds(pl.multiple_of(sender * band, band), band), :]

    bulk = count[0]

    def brick_copy(number, sender, peer):
        return remote(slab.at[peer], part(sender), bulk + number, "wide", peer)

    for off in range(1, n_wide):
        slot()
        brick_copy(off - 1, w, lax.rem(w + off, n_wide)).start()

    last_row = brick_rows - 1
    packs[...] = jnp.zeros(packs.shape, F32)

    def at_layer(z):
        return pl.ds(pl.multiple_of(z * brick_rows, brick_rows), brick_rows)

    def assemble_band(band_number):
        base = band_number * depth
        lane_base = lax.rem(base, cols)
        tile = at_layer(lax.div(base, cols))
        low = packs[0, 0, tile, :]
        high = packs[1, 0, tile, :]
        for u in range(depth):
            here = coef[at_layer(base + u), :]
            rf = jnp.where(trow == last_row, 0.0, harmonic(here, pltpu.roll(here, last_row, 0)))
            cf = jnp.where(tlane == cols - 1, 0.0, harmonic(here, pltpu.roll(here, cols - 1, 1)))
            rface[at_layer(base + u), :] = rf
            cface[at_layer(base + u), :] = cf
            scale[at_layer(base + u), :] = (
                compress * here + pltpu.roll(rf, 1, 0) + rf + pltpu.roll(cf, 1, 1) + cf
            )
            spot = lane_base + u
            turned = pltpu.roll(here, spot, 1)
            low = jnp.where(tlane == spot, turned, low)
            high = jnp.where(tlane == lax.rem(spot + cols - 1, cols), turned, high)
        packs[0, 0, tile, :] = low
        packs[1, 0, tile, :] = high

    coef[pl.ds(pl.multiple_of(w * band, band), band), :] = slab[w]
    assemble_band(w)

    brick_count = n_wide

    def by_brick(block):
        summed = jnp.sum(block.reshape(brick_count, brick_rows, cols), axis=1)
        return jnp.sum(summed, axis=1, keepdims=True)

    clane = lax.broadcasted_iota(jnp.int32, (brick_count, cols), 1)
    crow = lax.broadcasted_iota(jnp.int32, (brick_count, cols), 0)
    high_rows = by_brick(jnp.where((lax.rem(row, brick_rows) == brick_rows - 1) & (row < rows - 1), cross, 0.0))
    low_rows = by_brick(
        pltpu.roll(jnp.where((lax.rem(row, brick_rows) == brick_rows - 1) & (row < rows - 1), cross, 0.0), 1, 0)
    )
    coef_sum = by_brick(total)
    wait_sides()
    low_cols = by_brick(jnp.where((lane < depth) & has_left, harmonic(sidepack[0], sidehalo[0]), 0.0))
    high_cols = by_brick(jnp.where((lane < depth) & has_right, harmonic(sidepack[1], sidehalo[1]), 0.0))
    diagonal = compress * coef_sum + low_rows + high_rows + low_cols + high_cols
    message = jnp.where((clane == 0) & (crow == w), res_total, 0.0)
    for i, value in enumerate((diagonal, low_rows, high_rows, low_cols, high_cols)):
        message = jnp.where(clane == i + 1, value, message)
    cw[w] = message
    wait_sums = everyone("wide", lambda peer: cw.at[w], lambda sender: cw.at[sender])

    def take_band(off, carry):
        sender = lax.rem(w + n_wide - off, n_wide)
        brick_copy(off - 1, sender, sender).wait_recv()
        assemble_band(sender)
        return carry

    lax.fori_loop(1, n_wide, take_band, 0)
    wait_sums()

    def at_narrow(sender):
        return cn.at[pl.ds(pl.multiple_of(sender * n_wide, n_wide), n_wide), :]

    cn[pl.ds(pl.multiple_of(k * n_wide, n_wide), n_wide), :] = jnp.sum(cw[...], axis=0)
    wait_coarse = everyone("narrow", lambda peer: at_narrow(k), at_narrow)
    for off in range(1, n_wide):
        brick_copy(off - 1, w, lax.rem(w + off, n_wide)).wait_send()

    def send_sides(ref, which):
        rowsend[0, which] = ref[pl.ds(0, layers, stride=brick_rows), :]
        rowsend[1, which] = ref[pl.ds(last_row, layers, stride=brick_rows), :]
        wait_rows = neighbours(
            "wide", rowsend.at[0, which], rowsend.at[1, which],
            rowhalo.at[0, which], rowhalo.at[1, which],
        )
        for t in range(tiles):
            if which == 0:
                break

            def collect(i, carry):
                low, high = carry
                for u in range(32):
                    z = i * 32 + u
                    at = pl.multiple_of((t * cols + z) * brick_rows, brick_rows)
                    turned = pltpu.roll(ref[pl.ds(at, brick_rows), :], z, 1)
                    low = jnp.where(tlane == z, turned, low)
                    high = jnp.where(tlane == lax.rem(z + cols - 1, cols), turned, high)
                return low, high

            low, high = lax.fori_loop(0, cols // 32, collect, (zero, zero))
            packs[0, which, pl.ds(t * brick_rows, brick_rows), :] = low
            packs[1, which, pl.ds(t * brick_rows, brick_rows), :] = high
        packs[1, which] = pltpu.roll(packs[1, which], 1, 1)
        wait_packs = neighbours(
            "narrow", packs.at[0, which], packs.at[1, which],
            packhalo.at[0, which], packhalo.at[1, which],
        )
        return wait_rows, wait_packs

    wait_rows, wait_packs = send_sides(coef, 0)

    unroll = 16

    def assemble(i, carry):
        below, here = carry
        for u in range(32):
            z = i * 32 + u
            above = coef[at_layer(z + 1), :]
            df = jnp.where(z < layers - 1, harmonic(here, above), zero)
            sc = relax / (scale[at_layer(z), :] + below + df)
            dface[at_layer(z), :] = df
            scale[at_layer(z), :] = sc
            v = sc * res_ref[z]
            first[at_layer(z), :] = v
            va[at_layer(z), :] = v
            below, here = df, above
        return below, here

    lax.fori_loop(0, layers // 32, assemble, (zero, coef[pl.ds(0, brick_rows), :]))

    def sweep(src, dst):
        def body(i, carry):
            v_below, d_below, v = carry
            for u in range(32):
                z = i * 32 + u
                v_above = src[at_layer(z + 1), :]
                df = dface[at_layer(z), :]
                rf = rface[at_layer(z), :]
                cf = cface[at_layer(z), :]
                off = (
                    d_below * v_below + df * v_above
                    + pltpu.roll(rf * v, 1, 0) + rf * pltpu.roll(v, last_row, 0)
                    + pltpu.roll(cf * v, 1, 1) + cf * pltpu.roll(v, cols - 1, 1)
                )
                dst[at_layer(z), :] = (
                    (1.0 - relax) * v + first[at_layer(z), :] + scale[at_layer(z), :] * off
                )
                v_below, d_below, v = v, df, v_above
            return v_below, d_below, v

        lax.fori_loop(0, layers // 32, body, (zero, zero, src[pl.ds(0, brick_rows), :]))

    bricks = n_wide * n_narrow
    blane = lax.broadcasted_iota(jnp.int32, (bricks, cols), 1)
    brow = lax.broadcasted_iota(jnp.int32, (bricks, cols), 0)

    mine = k * n_wide + w

    def coarse_solve():
        gathered = cn[...]
        matrix = jnp.where(blane == brow, gathered[:, 1:2], 0.0)
        for i, away in ((2, -1), (3, 1), (4, -n_wide), (5, n_wide)):
            matrix = jnp.where(blane == brow + away, matrix - gathered[:, i:i + 1], matrix)
        right = jnp.broadcast_to(gathered[:, 0:1], (bricks, cols))
        def pivoted(j, block, side):
            column = jnp.broadcast_to(block[:, j:j + 1], (bricks, cols))
            factor = jnp.where(brow == j, 0.0, column / column[j:j + 1])
            return factor * block[j:j + 1], factor * side[j:j + 1]

        def colour(j):
            return (j // n_wide + j % n_wide) % 2

        block, side = matrix, right
        for j in range(bricks):
            if colour(j) == 0:
                change, side_change = pivoted(j, block, side)
                matrix, right = matrix - change, right - side_change
        for j in range(bricks):
            if colour(j) == 1:
                change, side_change = pivoted(j, matrix, right)
                matrix, right = matrix - change, right - side_change
        own = brow == mine
        pivot = jnp.sum(jnp.where(own & (blane == mine), matrix, 0.0), axis=(0, 1), keepdims=True)
        answer = jnp.sum(jnp.where(own & (blane == 0), right, 0.0), axis=(0, 1), keepdims=True)
        return answer / pivot

    src, dst = va, vb
    for number in range(SWEEPS - 1):
        sweep(src, dst)
        src, dst = dst, src
    wait_value_rows, wait_value_packs = send_sides(src, 1)
    wait_coarse()
    coarse_value = coarse_solve()

    wait_rows()
    wait_packs()
    wait_value_rows()
    wait_value_packs()
    for side, present in ((0, has_below), (1, has_above)):
        c = jnp.where(present, rowhalo[side, 0], 0.0)
        rowterm[side, 0] = c
        rowterm[side, 1] = jnp.where(present, c * rowhalo[side, 1], 0.0)
    for side, present in ((0, has_left), (1, has_right)):
        c = jnp.where(present, packhalo[side, 0], 0.0)
        packterm[side, 0] = c
        packterm[side, 1] = jnp.where(present, c * packhalo[side, 1], 0.0)

    def store(i):
        part = pl.ds(i * unroll, unroll)
        return pltpu.make_async_copy(prec_ref.at[part], prec_out.at[part], stores.at[i])

    for t in range(tiles):
        tile = pl.ds(t * brick_rows, brick_rows)

        def average(i, carry):
            for u in range(unroll):
                z = i * unroll + u
                layer = t * cols + z
                c = coef[at_layer(layer), :]
                sums = [c, c * src[at_layer(layer), :]]
                for j in range(2):
                    low = rowterm[0, j, pl.ds(layer, 1), :]
                    high = rowterm[1, j, pl.ds(layer, 1), :]
                    left = pltpu.roll(packterm[0, j, tile, :], lax.rem(cols - z, cols), 1)
                    right = pltpu.roll(packterm[1, j, tile, :], cols - 1 - z, 1)
                    sums[j] = (
                        sums[j]
                        + jnp.where(trow == 0, low, 0.0) + jnp.where(trow == last_row, high, 0.0)
                        + jnp.where(tlane == 0, left, 0.0)
                        + jnp.where(tlane == cols - 1, right, 0.0)
                    )
                prec_ref[layer] = sums[1] / sums[0] + coarse_value
            store(t * (cols // unroll) + i).start()
            return carry

        lax.fori_loop(0, cols // unroll, average, 0)

    storing.wait()
    for i in range(layers // unroll):
        store(i).wait()


def deliver(a_in, b_in, a_out, b_out, a_held, b_held, arrive, leave):
    arriving, leaving = [], []
    for src, held, dst in ((a_in, a_held, a_out), (b_in, b_held, b_out)):
        part = src.shape[0] // 4
        for i in range(4):
            at = pl.ds(i * part, part)
            number = len(arriving)
            arriving.append(pltpu.make_async_copy(src.at[at], held.at[at], arrive.at[number]))
            leaving.append(pltpu.make_async_copy(held.at[at], dst.at[at], leave.at[number]))
            arriving[-1].start()
    for first, second in zip(arriving, leaving):
        first.wait()
        second.start()
    for second in leaving:
        second.wait()


def shards(n_wide, n_narrow, *args):
    sat, residual = args[0], args[6]
    depth, rows, cols = sat.shape
    layers, brick_rows, _ = residual.shape
    tiles = layers // cols
    bricks = n_wide * n_narrow
    cells = layers * brick_rows
    copies = 2 * 7 + 3 * (n_wide - 1) + 2 * (n_narrow - 1)
    anywhere = pl.BlockSpec(memory_space=pl.ANY)
    table, wells = args[3].shape, args[4].shape

    def buffer(*shape):
        return pltpu.VMEM(shape, F32)

    outputs = pl.pallas_call(
        functools.partial(kernel, n_wide, n_narrow),
        out_shape=(
            jax.ShapeDtypeStruct(sat.shape, F32),
            jax.ShapeDtypeStruct(residual.shape, F32),
        ),
        in_specs=[anywhere] * 7,
        out_specs=(anywhere, anywhere),
        scratch_shapes=[
            buffer(*sat.shape),
            buffer(*residual.shape),
            buffer(*sat.shape),
            buffer(*sat.shape),
            buffer(*sat.shape),
            pltpu.VMEM(sat.shape, jnp.int32),
            pltpu.SMEM(table, F32),
            pltpu.SMEM(wells, jnp.int32),
            pltpu.SMEM(wells, F32),
            buffer(*residual.shape),
            buffer(depth + 2, 3, rows, cols),
            buffer(depth, 2, rows, cols),
            buffer(depth, rows, cols),
            buffer(2, rows, cols),
            buffer(2, rows, cols),
            buffer(2, rows, cols),
            buffer(rows, cols),
            buffer(n_wide, brick_rows, cols),
            buffer(n_narrow, brick_rows, cols),
            buffer(n_wide, depth * brick_rows, cols),
            buffer(cells + brick_rows, cols),
            buffer(cells, cols),
            buffer(cells, cols),
            buffer(cells, cols),
            buffer(cells, cols),
            buffer(cells, cols),
            buffer(cells + brick_rows, cols),
            buffer(cells + brick_rows, cols),
            buffer(2, 2, layers, cols),
            buffer(2, 2, layers, cols),
            buffer(2, 2, layers, cols),
            buffer(2, 2, tiles * brick_rows, cols),
            buffer(2, 2, tiles * brick_rows, cols),
            buffer(2, 2, tiles * brick_rows, cols),
            buffer(n_wide, n_wide, cols),
            buffer(bricks, cols),
            buffer(2, rows, cols),
            buffer(2, rows, cols),
            pltpu.SemaphoreType.DMA((7,)),
            pltpu.SemaphoreType.DMA((layers // 16,)),
            pltpu.SemaphoreType.DMA((copies,)),
            pltpu.SemaphoreType.DMA((copies,)),
        ],
        compiler_params=pltpu.CompilerParams(
            collective_id=0, has_side_effects=True, vmem_limit_bytes=56 * 1024 * 1024
        ),
    )(*args)
    return pl.pallas_call(
        deliver,
        out_shape=(
            jax.ShapeDtypeStruct(sat.shape, F32),
            jax.ShapeDtypeStruct(residual.shape, F32),
        ),
        in_specs=[anywhere] * 2,
        out_specs=(anywhere, anywhere),
        scratch_shapes=[
            buffer(*sat.shape),
            buffer(*residual.shape),
            pltpu.SemaphoreType.DMA((8,)),
            pltpu.SemaphoreType.DMA((8,)),
        ],
        compiler_params=pltpu.CompilerParams(vmem_limit_bytes=60 * 1024 * 1024),
    )(*outputs)


def solution(mesh):
    placed = (
        P("wide", None, "narrow"),
        P("wide", None, "narrow"),
        P("wide", None, "narrow"),
        P(),
        P(),
        P(),
        P(None, "wide", "narrow"),
    )
    return jax.shard_map(
        functools.partial(shards, mesh.shape["wide"], mesh.shape["narrow"]),
        mesh=mesh,
        in_specs=placed,
        out_specs=(P("wide", None, "narrow"), P(None, "wide", "narrow")),
        check_vma=False,
    )
```

```python
import functools

import jax
import jax.numpy as jnp
from jax import lax
from jax.experimental import pallas as pl
from jax.experimental.pallas import tpu as pltpu
from jax.sharding import PartitionSpec as P

SWEEPS = 6

compress = 0.05
relax = 0.8
gravity = 0.5
courant = 0.5
tiny = 1e-06

F32 = jnp.float32


def harmonic(a, b):
    return 2.0 * a * b / (a + b)


def flows(low, high, lift):
    total = harmonic(low[1], high[1]) * (low[0] - high[0] + lift)
    return total, total * jnp.where(total > 0, low[2], high[2])


def lookup(bits, table_ref, row, count):
    level = [table_ref[row, i] for i in range(count)]
    for bit in bits:
        level = [jnp.where(bit, level[i + 1], level[i]) for i in range(0, len(level), 2)]
    return level[0]


def kernel(
    n_wide, n_narrow,
    sat_in, pres_in, rock_in, table_in, wcol_in, wrate_in, res_in,
    satnew_out, prec_out,
    satnew_ref, prec_ref, outs,
    sat_ref, pres_ref, rock_ref, table_ref, wcol_ref, wrate_ref, res_ref,
    fields, gains, net, colpack, colhalo, colflow, source, maxw, maxn,
    slab, coef, dface, rface, cface, scale, first, va,
    rowsend, rowhalo, rowterm, packs, packhalo, packterm, cw, cn, sidepack, sidehalo,
    loads, stores, sends, recvs,
):
    depth, rows, cols = sat_ref.shape
    layers, brick_rows, _ = res_ref.shape
    w = lax.axis_index("wide")
    k = lax.axis_index("narrow")
    tiles = layers // cols
    band = depth * brick_rows
    has = {"wide": (w > 0, w < n_wide - 1), "narrow": (k > 0, k < n_narrow - 1)}
    place = {"wide": w, "narrow": k}
    size = {"wide": n_wide, "narrow": n_narrow}
    count = [0]

    loading = [
        pltpu.make_async_copy(src, dst, loads.at[i])
        for i, (src, dst) in enumerate((
            (table_in, table_ref), (rock_in, rock_ref), (sat_in, sat_ref), (pres_in, pres_ref),
            (wcol_in, wcol_ref), (wrate_in, wrate_ref), (res_in, res_ref),
        ))
    ]
    for copy in loading:
        copy.start()

    def slot():
        count[0] += 1
        return count[0] - 1

    barrier = pltpu.get_barrier_semaphore()
    for axis in ("wide", "narrow"):
        for off in range(1, size[axis]):
            peer = lax.rem(place[axis] + off, size[axis])
            pl.semaphore_signal(
                barrier, inc=1, device_id={axis: peer}, device_id_type=pl.DeviceIdType.MESH
            )

    def remote(src, dst, number, axis, peer):
        return pltpu.make_async_remote_copy(
            src_ref=src, dst_ref=dst, send_sem=sends.at[number], recv_sem=recvs.at[number],
            device_id={axis: peer}, device_id_type=pl.DeviceIdType.MESH,
        )

    def neighbours(axis, low_src, high_src, from_low, from_high):
        down, up = slot(), slot()
        me = place[axis]
        has_low, has_high = has[axis]

        @pl.when(has_low)
        def _():
            remote(low_src, from_high, down, axis, me - 1).start()

        @pl.when(has_high)
        def _():
            remote(high_src, from_low, up, axis, me + 1).start()

        def wait():
            @pl.when(has_low)
            def _():
                remote(low_src, from_high, down, axis, me - 1).wait_send()
                remote(high_src, from_low, up, axis, me - 1).wait_recv()

            @pl.when(has_high)
            def _():
                remote(high_src, from_low, up, axis, me + 1).wait_send()
                remote(low_src, from_high, down, axis, me + 1).wait_recv()

        return wait

    def everyone(axis, src_of, dst_from):
        copies = []
        me = place[axis]
        n = size[axis]
        for off in range(1, n):
            number = slot()
            peer = lax.rem(me + off, n)
            copy = remote(src_of(peer), dst_from(me), number, axis, peer)
            copy.start()
            sender = lax.rem(me + n - off, n)
            copies.append((copy, remote(src_of(peer), dst_from(sender), number, axis, peer)))

        def wait():
            for sent, received in copies:
                sent.wait_send()
                received.wait_recv()

        return wait

    lane = lax.broadcasted_iota(jnp.int32, (rows, cols), 1)
    row = lax.broadcasted_iota(jnp.int32, (rows, cols), 0)
    tlane = lax.broadcasted_iota(jnp.int32, (brick_rows, cols), 1)
    trow = lax.broadcasted_iota(jnp.int32, (brick_rows, cols), 0)
    zero = jnp.zeros((brick_rows, cols), F32)
    one = jnp.ones((brick_rows, cols), F32)

    @pl.when(w == 0)
    def _():
        fields[0] = jnp.ones((3, rows, cols), F32)
        rowhalo[0] = jnp.ones((2, layers, cols), F32)

    @pl.when(w == n_wide - 1)
    def _():
        fields[depth + 1] = jnp.ones((3, rows, cols), F32)
        rowhalo[1] = jnp.ones((2, layers, cols), F32)

    @pl.when(k == 0)
    def _():
        sidehalo[0] = jnp.ones((rows, cols), F32)
        colhalo[0] = jnp.ones((rows, cols), F32)
        packhalo[0] = jnp.ones((2, tiles * brick_rows, cols), F32)

    @pl.when(k == n_narrow - 1)
    def _():
        sidehalo[1] = jnp.ones((rows, cols), F32)
        colhalo[1] = jnp.ones((rows, cols), F32)
        packhalo[1] = jnp.ones((2, tiles * brick_rows, cols), F32)

    coef[pl.ds(layers * brick_rows, brick_rows), :] = one
    va[pl.ds(layers * brick_rows, brick_rows), :] = zero

    rocks = table_ref.shape[1]
    for copy in loading[:4]:
        copy.wait()

    def derive(d, carry):
        packed_low, packed_high = carry
        rock = rock_ref[d]
        bits = []
        step = 1
        while step < rocks:
            bits.append((rock & step) != 0)
            step *= 2
        perm = lookup(bits, table_ref, 0, rocks)
        water = lookup(bits, table_ref, 1, rocks)
        oil = lookup(bits, table_ref, 2, rocks)
        s = sat_ref[d]
        water_mob = water * s * s
        oil_mob = oil * (1.0 - s) * (1.0 - s)
        frac = water_mob / (water_mob + oil_mob)
        gains[d, 0] = water
        gains[d, 1] = oil
        for f, value in enumerate((pres_ref[d], perm, frac)):
            fields[d + 1, f] = value
            spot = 2 * (d + f * depth)
            turned = pltpu.roll(value, spot, 1)
            packed_low = jnp.where(lane == spot, turned, packed_low)
            packed_high = jnp.where(lane == lax.rem(spot + cols - 1, cols), turned, packed_high)
        return packed_low, packed_high

    blank = jnp.ones((rows, cols), F32)
    packed_low, packed_high = lax.fori_loop(0, depth, derive, (blank, blank))
    colpack[0] = packed_low
    colpack[1] = pltpu.roll(packed_high, 1, 1)

    pl.semaphore_wait(barrier, n_wide + n_narrow - 2)
    wait_planes = neighbours(
        "wide", fields.at[1], fields.at[depth], fields.at[0], fields.at[depth + 1]
    )
    wait_cols = neighbours(
        "narrow", colpack.at[0], colpack.at[1], colhalo.at[0], colhalo.at[1]
    )

    nothing = jnp.zeros((rows, cols), F32)
    has_below, has_above = has["wide"]
    has_left, has_right = has["narrow"]

    def plane(d):
        return [fields[d, f] for f in range(3)]

    def transport(d, below_total, below_water):
        here = plane(d + 1)
        above_total, above_water = flows(here, plane(lax.min(d + 2, depth)), gravity)
        above_total = jnp.where(d < depth - 1, above_total, nothing)
        above_water = jnp.where(d < depth - 1, above_water, nothing)
        flow = above_water - below_water
        out = jnp.maximum(above_total, 0.0) + jnp.maximum(-below_total, 0.0)

        total, water = flows(here, [pltpu.roll(x, rows - 1, 0) for x in here], 0.0)
        total = jnp.where(row == rows - 1, 0.0, total)
        water = jnp.where(row == rows - 1, 0.0, water)
        flow = flow + (water - pltpu.roll(water, 1, 0))
        out = out + (jnp.maximum(total, 0.0) + jnp.maximum(-pltpu.roll(total, 1, 0), 0.0))

        total, water = flows(here, [pltpu.roll(x, cols - 1, 1) for x in here], 0.0)
        total = jnp.where(lane == cols - 1, 0.0, total)
        water = jnp.where(lane == cols - 1, 0.0, water)
        net[d] = flow + (water - pltpu.roll(water, 1, 1))
        outs[d] = out + (jnp.maximum(total, 0.0) + jnp.maximum(-pltpu.roll(total, 1, 1), 0.0))
        return above_total, above_water

    def transport_group(i, carry):
        for u in range(4):
            carry = transport(i * 4 + u, *carry)
        return carry

    lax.fori_loop(0, depth // 4, transport_group, (nothing, nothing))

    wait_cols()

    def unpack(block):
        return [block] + [pltpu.roll(block, cols - 2 * f * depth, 1) for f in (1, 2)]

    low_total, low_water = flows(unpack(colhalo[0]), unpack(colpack[0]), 0.0)
    high_total, high_water = flows(unpack(colpack[1]), unpack(colhalo[1]), 0.0)
    even = lax.rem(lane, 2) == 0
    colflow[0] = jnp.where(
        even,
        jnp.where(has_right, high_water, nothing),
        pltpu.roll(jnp.where(has_left, -low_water, nothing), 1, 1),
    )
    colflow[1] = jnp.maximum(jnp.where(
        even,
        jnp.where(has_right, high_total, nothing),
        pltpu.roll(jnp.where(has_left, -low_total, nothing), 1, 1),
    ), 0.0)

    wait_planes()
    side_total, side_water = flows(plane(0), plane(1), gravity)
    net[0] = net[0] - jnp.where(has_below, side_water, nothing)
    outs[0] = outs[0] + jnp.maximum(jnp.where(has_below, -side_total, nothing), 0.0)
    side_total, side_water = flows(plane(depth), plane(depth + 1), gravity)
    net[depth - 1] = net[depth - 1] + jnp.where(has_above, side_water, nothing)
    outs[depth - 1] = outs[depth - 1] + jnp.maximum(jnp.where(has_above, side_total, nothing), 0.0)
    edge = (lane == 0) | (lane == cols - 1)

    def add_sides(i, most):
        for u in range(2):
            d = i * 2 + u
            turn = cols - 1 - 2 * d
            net[d] = net[d] + jnp.where(edge, pltpu.roll(colflow[0], turn, 1), 0.0)
            most = jnp.maximum(
                most, outs[d] + jnp.where(edge, pltpu.roll(colflow[1], turn, 1), 0.0)
            )
        return most

    most = lax.fori_loop(0, depth // 2, add_sides, nothing)

    maxw[w] = jnp.max(most.reshape(rows // brick_rows, brick_rows, cols), axis=0)
    wait_wide = everyone("wide", lambda peer: maxw.at[w], lambda sender: maxw.at[sender])

    all_cols = cols * n_narrow
    for copy in loading[4:]:
        copy.wait()
    cell = row * cols + lane

    def well(i, total):
        for u in range(8):
            column = wcol_ref[i * 8 + u]
            inside = lax.rem(column, all_cols) - k * cols
            target = lax.div(column, all_cols) * cols + inside
            target = jnp.where((inside >= 0) & (inside < cols), target, -1)
            total = total + jnp.where(cell == target, wrate_ref[i * 8 + u], 0.0)
        return total

    source[...] = lax.fori_loop(0, wcol_ref.shape[0] // 8, well, nothing)

    def add_res(i, total):
        return total + jnp.sum(res_ref[pl.ds(i * 16, 16)], axis=0)

    res_total = jnp.sum(lax.fori_loop(0, layers // 16, add_res, zero), axis=(0, 1), keepdims=True)
    wait_wide()
    maxn[k] = jnp.max(maxw[...], axis=0)
    everyone("narrow", lambda peer: maxn.at[k], lambda sender: maxn.at[sender])()
    top_rate = jnp.max(jnp.max(maxn[...], axis=0), axis=(0, 1), keepdims=True)
    step_size = courant / (top_rate + tiny)

    def update(i, carry):
        for u in range(2):
            d = i * 2 + u
            s = sat_ref[d] - step_size * net[d] + step_size * source[...]
            satnew_ref[d] = s
            value = fields[d + 1, 1] * (gains[d, 0] * s * s + gains[d, 1] * (1.0 - s) * (1.0 - s))
            at = pl.multiple_of(d * brick_rows, brick_rows)
            for p in range(n_wide):
                slab[p, pl.ds(at, brick_rows), :] = value[p * brick_rows:(p + 1) * brick_rows]
        return carry

    lax.fori_loop(0, depth // 2, update, 0)

    def part(sender):
        return coef.at[pl.ds(pl.multiple_of(sender * band, band), band), :]

    bulk = count[0]

    def brick_copy(number, sender, peer):
        return remote(slab.at[peer], part(sender), bulk + number, "wide", peer)

    for off in range(1, n_wide):
        slot()
        brick_copy(off - 1, w, lax.rem(w + off, n_wide)).start()
    storing = pltpu.make_async_copy(satnew_ref, satnew_out, loads.at[0])
    storing.start()

    def survey(i, carry):
        total, cross, packed_low, packed_high = carry
        for u in range(2):
            d = i * 2 + u
            at = pl.ds(pl.multiple_of(d * brick_rows, brick_rows), brick_rows)
            value = jnp.concatenate([slab[p, at, :] for p in range(n_wide)], axis=0)
            turned = pltpu.roll(value, d, 1)
            packed_low = jnp.where(lane == d, turned, packed_low)
            packed_high = jnp.where(lane == lax.rem(d + cols - 1, cols), turned, packed_high)
            cross = cross + harmonic(value, pltpu.roll(value, rows - 1, 0))
            total = total + value
        return total, cross, packed_low, packed_high

    total, cross, packed_low, packed_high = lax.fori_loop(
        0, depth // 2, survey, (nothing, nothing, blank, blank)
    )
    sidepack[0] = packed_low
    sidepack[1] = pltpu.roll(packed_high, 1, 1)
    wait_sides = neighbours(
        "narrow", sidepack.at[0], sidepack.at[1], sidehalo.at[0], sidehalo.at[1]
    )

    last_row = brick_rows - 1
    packs[...] = jnp.zeros(packs.shape, F32)

    def at_layer(z):
        return pl.ds(pl.multiple_of(z * brick_rows, brick_rows), brick_rows)

    def assemble_band(band_number):
        base = band_number * depth
        lane_base = lax.rem(base, cols)
        tile = at_layer(lax.div(base, cols))
        low = packs[0, 0, tile, :]
        high = packs[1, 0, tile, :]
        for u in range(depth):
            here = coef[at_layer(base + u), :]
            rf = jnp.where(trow == last_row, 0.0, harmonic(here, pltpu.roll(here, last_row, 0)))
            cf = jnp.where(tlane == cols - 1, 0.0, harmonic(here, pltpu.roll(here, cols - 1, 1)))
            rface[at_layer(base + u), :] = rf
            cface[at_layer(base + u), :] = cf
            scale[at_layer(base + u), :] = (
                compress * here + pltpu.roll(rf, 1, 0) + rf + pltpu.roll(cf, 1, 1) + cf
            )
            spot = lane_base + u
            turned = pltpu.roll(here, spot, 1)
            low = jnp.where(tlane == spot, turned, low)
            high = jnp.where(tlane == lax.rem(spot + cols - 1, cols), turned, high)
        packs[0, 0, tile, :] = low
        packs[1, 0, tile, :] = high

    coef[pl.ds(pl.multiple_of(w * band, band), band), :] = slab[w]
    assemble_band(w)

    brick_count = n_wide

    def by_brick(block):
        summed = jnp.sum(block.reshape(brick_count, brick_rows, cols), axis=1)
        return jnp.sum(summed, axis=1, keepdims=True)

    clane = lax.broadcasted_iota(jnp.int32, (brick_count, cols), 1)
    crow = lax.broadcasted_iota(jnp.int32, (brick_count, cols), 0)
    high_rows = by_brick(jnp.where((lax.rem(row, brick_rows) == brick_rows - 1) & (row < rows - 1), cross, 0.0))
    low_rows = by_brick(
        pltpu.roll(jnp.where((lax.rem(row, brick_rows) == brick_rows - 1) & (row < rows - 1), cross, 0.0), 1, 0)
    )
    coef_sum = by_brick(total)
    wait_sides()
    low_cols = by_brick(jnp.where((lane < depth) & has_left, harmonic(sidepack[0], sidehalo[0]), 0.0))
    high_cols = by_brick(jnp.where((lane < depth) & has_right, harmonic(sidepack[1], sidehalo[1]), 0.0))
    diagonal = compress * coef_sum + low_rows + high_rows + low_cols + high_cols
    message = jnp.where((clane == 0) & (crow == w), res_total, 0.0)
    for i, value in enumerate((diagonal, low_rows, high_rows, low_cols, high_cols)):
        message = jnp.where(clane == i + 1, value, message)
    cw[w] = message
    wait_sums = everyone("wide", lambda peer: cw.at[w], lambda sender: cw.at[sender])

    def take_band(off, carry):
        sender = lax.rem(w + n_wide - off, n_wide)
        brick_copy(off - 1, sender, sender).wait_recv()
        assemble_band(sender)
        return carry

    lax.fori_loop(1, n_wide, take_band, 0)
    wait_sums()

    def at_narrow(sender):
        return cn.at[pl.ds(pl.multiple_of(sender * n_wide, n_wide), n_wide), :]

    cn[pl.ds(pl.multiple_of(k * n_wide, n_wide), n_wide), :] = jnp.sum(cw[...], axis=0)
    wait_coarse = everyone("narrow", lambda peer: at_narrow(k), at_narrow)
    for off in range(1, n_wide):
        brick_copy(off - 1, w, lax.rem(w + off, n_wide)).wait_send()

    def send_sides(ref, which):
        rowsend[0, which] = ref[pl.ds(0, layers, stride=brick_rows), :]
        rowsend[1, which] = ref[pl.ds(last_row, layers, stride=brick_rows), :]
        wait_rows = neighbours(
            "wide", rowsend.at[0, which], rowsend.at[1, which],
            rowhalo.at[0, which], rowhalo.at[1, which],
        )
        packs[1, which] = pltpu.roll(packs[1, which], 1, 1)
        wait_packs = neighbours(
            "narrow", packs.at[0, which], packs.at[1, which],
            packhalo.at[0, which], packhalo.at[1, which],
        )
        return wait_rows, wait_packs

    wait_rows, wait_packs = send_sides(coef, 0)

    unroll = 32

    def assemble(i, carry):
        below, here = carry
        for u in range(32):
            z = i * 32 + u
            above = coef[at_layer(z + 1), :]
            df = jnp.where(z < layers - 1, harmonic(here, above), zero)
            sc = relax / (scale[at_layer(z), :] + below + df)
            dface[at_layer(z), :] = df
            scale[at_layer(z), :] = sc
            v = sc * res_ref[z]
            first[at_layer(z), :] = v
            va[at_layer(z), :] = v
            below, here = df, above
        return below, here

    lax.fori_loop(0, layers // 32, assemble, (zero, coef[pl.ds(0, brick_rows), :]))

    group = min(64, layers)

    def sweep(packing):
        def body(i, carry):
            v_below, d_below, v, low, high = carry
            for u in range(group):
                z = i * group + u
                v_above = va[at_layer(z + 1), :]
                df = dface[at_layer(z), :]
                rf = rface[at_layer(z), :]
                cf = cface[at_layer(z), :]
                off = (
                    d_below * v_below + df * v_above
                    + pltpu.roll(rf * v, 1, 0) + rf * pltpu.roll(v, last_row, 0)
                    + pltpu.roll(cf * v, 1, 1) + cf * pltpu.roll(v, cols - 1, 1)
                )
                fresh = (1.0 - relax) * v + first[at_layer(z), :] + scale[at_layer(z), :] * off
                va[at_layer(z), :] = fresh
                if packing:
                    spot = lax.rem(z, cols)
                    turned = pltpu.roll(fresh, spot, 1)
                    low = jnp.where(tlane == spot, turned, low)
                    high = jnp.where(tlane == lax.rem(spot + cols - 1, cols), turned, high)
                v_below, d_below, v = v, df, v_above
            if packing:
                tile = at_layer(lax.div(i * group, cols))
                packs[0, 1, tile, :] = low
                packs[1, 1, tile, :] = high
            return v_below, d_below, v, low, high

        lax.fori_loop(0, layers // group, body, (zero, zero, va[pl.ds(0, brick_rows), :], zero, zero))

    bricks = n_wide * n_narrow
    blane = lax.broadcasted_iota(jnp.int32, (bricks, cols), 1)
    brow = lax.broadcasted_iota(jnp.int32, (bricks, cols), 0)

    mine = k * n_wide + w

    def coarse_solve():
        gathered = cn[...]
        matrix = jnp.where(blane == brow, gathered[:, 1:2], 0.0)
        for i, away in ((2, -1), (3, 1), (4, -n_wide), (5, n_wide)):
            matrix = jnp.where(blane == brow + away, matrix - gathered[:, i:i + 1], matrix)
        right = jnp.broadcast_to(gathered[:, 0:1], (bricks, cols))
        def pivoted(j, block, side):
            column = jnp.broadcast_to(block[:, j:j + 1], (bricks, cols))
            factor = jnp.where(brow == j, 0.0, column / column[j:j + 1])
            return factor * block[j:j + 1], factor * side[j:j + 1]

        def colour(j):
            return (j // n_wide + j % n_wide) % 2

        block, side = matrix, right
        for j in range(bricks):
            if colour(j) == 0:
                change, side_change = pivoted(j, block, side)
                matrix, right = matrix - change, right - side_change
        for j in range(bricks):
            if colour(j) == 1:
                change, side_change = pivoted(j, matrix, right)
                matrix, right = matrix - change, right - side_change
        own = brow == mine
        pivot = jnp.sum(jnp.where(own & (blane == mine), matrix, 0.0), axis=(0, 1), keepdims=True)
        answer = jnp.sum(jnp.where(own & (blane == 0), right, 0.0), axis=(0, 1), keepdims=True)
        return answer / pivot

    def plain_sweep(number, carry):
        sweep(False)
        return carry

    lax.fori_loop(0, SWEEPS - 2, plain_sweep, 0)
    sweep(True)
    wait_value_rows, wait_value_packs = send_sides(va, 1)
    wait_coarse()
    coarse_value = coarse_solve()

    wait_rows()
    wait_packs()
    wait_value_rows()
    wait_value_packs()
    for side, present in ((0, has_below), (1, has_above)):
        c = jnp.where(present, rowhalo[side, 0], 0.0)
        rowterm[side, 0] = c
        rowterm[side, 1] = jnp.where(present, c * rowhalo[side, 1], 0.0)
    for side, present in ((0, has_left), (1, has_right)):
        c = jnp.where(present, packhalo[side, 0], 0.0)
        packterm[side, 0] = c
        packterm[side, 1] = jnp.where(present, c * packhalo[side, 1], 0.0)

    def store(i):
        part = pl.ds(i * unroll, unroll)
        return pltpu.make_async_copy(prec_ref.at[part], prec_out.at[part], stores.at[i])

    for t in range(tiles):
        tile = pl.ds(t * brick_rows, brick_rows)

        def average(i, carry):
            for u in range(unroll):
                z = i * unroll + u
                layer = t * cols + z
                c = coef[at_layer(layer), :]
                sums = [c, c * va[at_layer(layer), :]]
                for j in range(2):
                    low = rowterm[0, j, pl.ds(layer, 1), :]
                    high = rowterm[1, j, pl.ds(layer, 1), :]
                    left = pltpu.roll(packterm[0, j, tile, :], lax.rem(cols - z, cols), 1)
                    right = pltpu.roll(packterm[1, j, tile, :], cols - 1 - z, 1)
                    sums[j] = (
                        sums[j]
                        + jnp.where(trow == 0, low, 0.0) + jnp.where(trow == last_row, high, 0.0)
                        + jnp.where(tlane == 0, left, 0.0)
                        + jnp.where(tlane == cols - 1, right, 0.0)
                    )
                prec_ref[layer] = sums[1] / sums[0] + coarse_value
            store(t * (cols // unroll) + i).start()
            return carry

        lax.fori_loop(0, cols // unroll, average, 0)

    storing.wait()
    for i in range(layers // unroll):
        store(i).wait()


def deliver(a_in, b_in, a_out, b_out, a_held, b_held, arrive, leave):
    arriving, leaving = [], []
    for src, held, dst in ((a_in, a_held, a_out), (b_in, b_held, b_out)):
        part = src.shape[0] // 4
        for i in range(4):
            at = pl.ds(i * part, part)
            number = len(arriving)
            arriving.append(pltpu.make_async_copy(src.at[at], held.at[at], arrive.at[number]))
            leaving.append(pltpu.make_async_copy(held.at[at], dst.at[at], leave.at[number]))
            arriving[-1].start()
    for first, second in zip(arriving, leaving):
        first.wait()
        second.start()
    for second in leaving:
        second.wait()


def shards(n_wide, n_narrow, *args):
    sat, residual = args[0], args[6]
    depth, rows, cols = sat.shape
    layers, brick_rows, _ = residual.shape
    tiles = layers // cols
    bricks = n_wide * n_narrow
    cells = layers * brick_rows
    copies = 2 * 7 + 3 * (n_wide - 1) + 2 * (n_narrow - 1)
    anywhere = pl.BlockSpec(memory_space=pl.ANY)
    table, wells = args[3].shape, args[4].shape

    def buffer(*shape):
        return pltpu.VMEM(shape, F32)

    outputs = pl.pallas_call(
        functools.partial(kernel, n_wide, n_narrow),
        out_shape=(
            jax.ShapeDtypeStruct(sat.shape, F32),
            jax.ShapeDtypeStruct(residual.shape, F32),
        ),
        in_specs=[anywhere] * 7,
        out_specs=(anywhere, anywhere),
        scratch_shapes=[
            buffer(*sat.shape),
            buffer(*residual.shape),
            buffer(*sat.shape),
            buffer(*sat.shape),
            buffer(*sat.shape),
            pltpu.VMEM(sat.shape, jnp.int32),
            pltpu.SMEM(table, F32),
            pltpu.SMEM(wells, jnp.int32),
            pltpu.SMEM(wells, F32),
            buffer(*residual.shape),
            buffer(depth + 2, 3, rows, cols),
            buffer(depth, 2, rows, cols),
            buffer(depth, rows, cols),
            buffer(2, rows, cols),
            buffer(2, rows, cols),
            buffer(2, rows, cols),
            buffer(rows, cols),
            buffer(n_wide, brick_rows, cols),
            buffer(n_narrow, brick_rows, cols),
            buffer(n_wide, depth * brick_rows, cols),
            buffer(cells + brick_rows, cols),
            buffer(cells, cols),
            buffer(cells, cols),
            buffer(cells, cols),
            buffer(cells, cols),
            buffer(cells, cols),
            buffer(cells + brick_rows, cols),
            buffer(2, 2, layers, cols),
            buffer(2, 2, layers, cols),
            buffer(2, 2, layers, cols),
            buffer(2, 2, tiles * brick_rows, cols),
            buffer(2, 2, tiles * brick_rows, cols),
            buffer(2, 2, tiles * brick_rows, cols),
            buffer(n_wide, n_wide, cols),
            buffer(bricks, cols),
            buffer(2, rows, cols),
            buffer(2, rows, cols),
            pltpu.SemaphoreType.DMA((7,)),
            pltpu.SemaphoreType.DMA((layers // 32,)),
            pltpu.SemaphoreType.DMA((copies,)),
            pltpu.SemaphoreType.DMA((copies,)),
        ],
        compiler_params=pltpu.CompilerParams(
            collective_id=0, has_side_effects=True, vmem_limit_bytes=56 * 1024 * 1024
        ),
    )(*args)
    return pl.pallas_call(
        deliver,
        out_shape=(
            jax.ShapeDtypeStruct(sat.shape, F32),
            jax.ShapeDtypeStruct(residual.shape, F32),
        ),
        in_specs=[anywhere] * 2,
        out_specs=(anywhere, anywhere),
        scratch_shapes=[
            buffer(*sat.shape),
            buffer(*residual.shape),
            pltpu.SemaphoreType.DMA((8,)),
            pltpu.SemaphoreType.DMA((8,)),
        ],
        compiler_params=pltpu.CompilerParams(vmem_limit_bytes=60 * 1024 * 1024),
    )(*outputs)


def solution(mesh):
    placed = (
        P("wide", None, "narrow"),
        P("wide", None, "narrow"),
        P("wide", None, "narrow"),
        P(),
        P(),
        P(),
        P(None, "wide", "narrow"),
    )
    return jax.shard_map(
        functools.partial(shards, mesh.shape["wide"], mesh.shape["narrow"]),
        mesh=mesh,
        in_specs=placed,
        out_specs=(P("wide", None, "narrow"), P(None, "wide", "narrow")),
        check_vma=False,
    )
```

```python
import functools

import jax
import jax.numpy as jnp
from jax import lax
from jax.experimental import pallas as pl
from jax.experimental.pallas import tpu as pltpu
from jax.sharding import PartitionSpec as P

SWEEPS = 6

compress = 0.05
relax = 0.8
gravity = 0.5
courant = 0.5
tiny = 1e-06

F32 = jnp.float32


def harmonic(a, b):
    return 2.0 * a * b / (a + b)


def flows(low, high, lift):
    total = harmonic(low[1], high[1]) * (low[0] - high[0] + lift)
    return total, total * jnp.where(total > 0, low[2], high[2])


def lookup(bits, table_ref, row, count):
    level = [table_ref[row, i] for i in range(count)]
    for bit in bits:
        level = [jnp.where(bit, level[i + 1], level[i]) for i in range(0, len(level), 2)]
    return level[0]


def kernel(
    n_wide, n_narrow,
    sat_in, pres_in, rock_in, table_in, wcol_in, wrate_in, res_in,
    satnew_out, prec_out,
    satnew_ref, prec_ref, outs,
    sat_ref, pres_ref, rock_ref, table_ref, wcol_ref, wrate_ref, res_ref,
    fields, gains, net, colpack, colhalo, colflow, source, maxw, maxn,
    slab, coef, dface, rface, cface, scale, first, va,
    rowsend, rowhalo, rowterm, packs, packhalo, packterm, cw, cn, sidepack, sidehalo,
    sathalo, preshalo, rockhalo, satb, rockb, netb,
    loads, stores, sends, recvs,
):
    depth, rows, cols = sat_ref.shape
    layers, brick_rows, _ = res_ref.shape
    w = lax.axis_index("wide")
    k = lax.axis_index("narrow")
    tiles = layers // cols
    band = depth * brick_rows
    has = {"wide": (w > 0, w < n_wide - 1), "narrow": (k > 0, k < n_narrow - 1)}
    place = {"wide": w, "narrow": k}
    size = {"wide": n_wide, "narrow": n_narrow}
    count = [0]

    loading = [
        pltpu.make_async_copy(src, dst, loads.at[i])
        for i, (src, dst) in enumerate((
            (table_in, table_ref), (rock_in, rock_ref), (sat_in, sat_ref), (pres_in, pres_ref),
            (wcol_in, wcol_ref), (wrate_in, wrate_ref), (res_in, res_ref),
        ))
    ]
    for copy in loading:
        copy.start()

    def slot():
        count[0] += 1
        return count[0] - 1

    barrier = pltpu.get_barrier_semaphore()
    for axis in ("wide", "narrow"):
        for off in range(1, size[axis]):
            peer = lax.rem(place[axis] + off, size[axis])
            pl.semaphore_signal(
                barrier, inc=1, device_id={axis: peer}, device_id_type=pl.DeviceIdType.MESH
            )

    def remote(src, dst, number, axis, peer):
        return pltpu.make_async_remote_copy(
            src_ref=src, dst_ref=dst, send_sem=sends.at[number], recv_sem=recvs.at[number],
            device_id={axis: peer}, device_id_type=pl.DeviceIdType.MESH,
        )

    def neighbours(axis, low_src, high_src, from_low, from_high):
        down, up = slot(), slot()
        me = place[axis]
        has_low, has_high = has[axis]

        @pl.when(has_low)
        def _():
            remote(low_src, from_high, down, axis, me - 1).start()

        @pl.when(has_high)
        def _():
            remote(high_src, from_low, up, axis, me + 1).start()

        def wait():
            @pl.when(has_low)
            def _():
                remote(low_src, from_high, down, axis, me - 1).wait_send()
                remote(high_src, from_low, up, axis, me - 1).wait_recv()

            @pl.when(has_high)
            def _():
                remote(high_src, from_low, up, axis, me + 1).wait_send()
                remote(low_src, from_high, down, axis, me + 1).wait_recv()

        return wait

    def everyone(axis, src_of, dst_from):
        copies = []
        me = place[axis]
        n = size[axis]
        for off in range(1, n):
            number = slot()
            peer = lax.rem(me + off, n)
            copy = remote(src_of(peer), dst_from(me), number, axis, peer)
            copy.start()
            sender = lax.rem(me + n - off, n)
            copies.append((copy, remote(src_of(peer), dst_from(sender), number, axis, peer)))

        def wait():
            for sent, received in copies:
                sent.wait_send()
                received.wait_recv()

        return wait

    lane = lax.broadcasted_iota(jnp.int32, (rows, cols), 1)
    row = lax.broadcasted_iota(jnp.int32, (rows, cols), 0)
    tlane = lax.broadcasted_iota(jnp.int32, (brick_rows, cols), 1)
    trow = lax.broadcasted_iota(jnp.int32, (brick_rows, cols), 0)
    zero = jnp.zeros((brick_rows, cols), F32)
    one = jnp.ones((brick_rows, cols), F32)

    @pl.when(w == 0)
    def _():
        fields[0] = jnp.ones((3, rows, cols), F32)
        rowhalo[0] = jnp.ones((2, layers, cols), F32)

    @pl.when(w == n_wide - 1)
    def _():
        fields[depth + 1] = jnp.ones((3, rows, cols), F32)
        rowhalo[1] = jnp.ones((2, layers, cols), F32)

    @pl.when(k == 0)
    def _():
        sidehalo[0] = jnp.ones((rows, cols), F32)
        colhalo[0] = jnp.ones((rows, cols), F32)
        packhalo[0] = jnp.ones((2, tiles * brick_rows, cols), F32)

    @pl.when(k == n_narrow - 1)
    def _():
        sidehalo[1] = jnp.ones((rows, cols), F32)
        colhalo[1] = jnp.ones((rows, cols), F32)
        packhalo[1] = jnp.ones((2, tiles * brick_rows, cols), F32)

    coef[pl.ds(layers * brick_rows, brick_rows), :] = one
    va[pl.ds(layers * brick_rows, brick_rows), :] = zero

    pl.semaphore_wait(barrier, n_wide + n_narrow - 2)

    wait_raw = [
        neighbours("wide", src.at[0], src.at[depth - 1], halo.at[0], halo.at[1])
        for src, halo in ((sat_in, sathalo), (pres_in, preshalo), (rock_in, rockhalo))
    ]

    def brick_part(ref, sender):
        return ref.at[pl.ds(pl.multiple_of(sender * depth, depth), depth)]

    def brick_rows_of(ref, peer):
        return ref.at[:, pl.ds(pl.multiple_of(peer * brick_rows, brick_rows), brick_rows), :]

    raw = count[0]
    raw_fields = ((sat_in, satb), (rock_in, rockb))

    def raw_copy(off, f, sender, peer):
        src, dst = raw_fields[f]
        return remote(
            brick_rows_of(src, peer), brick_part(dst, sender), raw + 2 * (off - 1) + f, "wide", peer
        )

    for off in range(1, n_wide):
        for f in range(2):
            slot()
            raw_copy(off, f, w, lax.rem(w + off, n_wide)).start()
    own_raw = [
        pltpu.make_async_copy(brick_rows_of(src, w), brick_part(dst, w), loads.at[7 + f])
        for f, (src, dst) in enumerate(raw_fields)
    ]
    for copy in own_raw:
        copy.start()

    rocks = table_ref.shape[1]
    for copy in loading[:4]:
        copy.wait()

    def properties(rock):
        bits = []
        step = 1
        while step < rocks:
            bits.append((rock & step) != 0)
            step *= 2
        return [lookup(bits, table_ref, i, rocks) for i in range(3)]

    def fraction(water, oil, s):
        water_mob = water * s * s
        oil_mob = oil * (1.0 - s) * (1.0 - s)
        return water_mob / (water_mob + oil_mob)

    def derive(d, carry):
        packed_low, packed_high = carry
        perm, water, oil = properties(rock_ref[d])
        frac = fraction(water, oil, sat_ref[d])
        gains[d, 0] = water
        gains[d, 1] = oil
        for f, value in enumerate((pres_ref[d], perm, frac)):
            fields[d + 1, f] = value
            spot = 2 * (d + f * depth)
            turned = pltpu.roll(value, spot, 1)
            packed_low = jnp.where(lane == spot, turned, packed_low)
            packed_high = jnp.where(lane == lax.rem(spot + cols - 1, cols), turned, packed_high)
        return packed_low, packed_high

    blank = jnp.ones((rows, cols), F32)
    packed_low, packed_high = lax.fori_loop(0, depth, derive, (blank, blank))
    colpack[0] = packed_low
    colpack[1] = pltpu.roll(packed_high, 1, 1)
    wait_cols = neighbours(
        "narrow", colpack.at[0], colpack.at[1], colhalo.at[0], colhalo.at[1]
    )

    nothing = jnp.zeros((rows, cols), F32)
    has_below, has_above = has["wide"]
    has_left, has_right = has["narrow"]

    def plane(d):
        return [fields[d, f] for f in range(3)]

    def transport(d, below_total, below_water):
        here = plane(d + 1)
        above_total, above_water = flows(here, plane(lax.min(d + 2, depth)), gravity)
        above_total = jnp.where(d < depth - 1, above_total, nothing)
        above_water = jnp.where(d < depth - 1, above_water, nothing)
        flow = above_water - below_water
        out = jnp.maximum(above_total, 0.0) + jnp.maximum(-below_total, 0.0)

        total, water = flows(here, [pltpu.roll(x, rows - 1, 0) for x in here], 0.0)
        total = jnp.where(row == rows - 1, 0.0, total)
        water = jnp.where(row == rows - 1, 0.0, water)
        flow = flow + (water - pltpu.roll(water, 1, 0))
        out = out + (jnp.maximum(total, 0.0) + jnp.maximum(-pltpu.roll(total, 1, 0), 0.0))

        total, water = flows(here, [pltpu.roll(x, cols - 1, 1) for x in here], 0.0)
        total = jnp.where(lane == cols - 1, 0.0, total)
        water = jnp.where(lane == cols - 1, 0.0, water)
        net[d] = flow + (water - pltpu.roll(water, 1, 1))
        outs[d] = out + (jnp.maximum(total, 0.0) + jnp.maximum(-pltpu.roll(total, 1, 1), 0.0))
        return above_total, above_water

    def transport_group(i, carry):
        for u in range(4):
            carry = transport(i * 4 + u, *carry)
        return carry

    lax.fori_loop(0, depth // 4, transport_group, (nothing, nothing))

    wait_cols()

    def unpack(block):
        return [block] + [pltpu.roll(block, cols - 2 * f * depth, 1) for f in (1, 2)]

    low_total, low_water = flows(unpack(colhalo[0]), unpack(colpack[0]), 0.0)
    high_total, high_water = flows(unpack(colpack[1]), unpack(colhalo[1]), 0.0)
    even = lax.rem(lane, 2) == 0
    colflow[0] = jnp.where(
        even,
        jnp.where(has_right, high_water, nothing),
        pltpu.roll(jnp.where(has_left, -low_water, nothing), 1, 1),
    )
    colflow[1] = jnp.maximum(jnp.where(
        even,
        jnp.where(has_right, high_total, nothing),
        pltpu.roll(jnp.where(has_left, -low_total, nothing), 1, 1),
    ), 0.0)

    for wait in wait_raw:
        wait()
    for side, at, present in ((0, 0, has_below), (1, depth + 1, has_above)):
        @pl.when(present)
        def _():
            perm, water, oil = properties(rockhalo[side])
            fields[at, 0] = preshalo[side]
            fields[at, 1] = perm
            fields[at, 2] = fraction(water, oil, sathalo[side])

    side_total, side_water = flows(plane(0), plane(1), gravity)
    net[0] = net[0] - jnp.where(has_below, side_water, nothing)
    outs[0] = outs[0] + jnp.maximum(jnp.where(has_below, -side_total, nothing), 0.0)
    side_total, side_water = flows(plane(depth), plane(depth + 1), gravity)
    net[depth - 1] = net[depth - 1] + jnp.where(has_above, side_water, nothing)
    outs[depth - 1] = outs[depth - 1] + jnp.maximum(jnp.where(has_above, side_total, nothing), 0.0)
    edge = (lane == 0) | (lane == cols - 1)

    def add_sides(i, most):
        for u in range(2):
            d = i * 2 + u
            turn = cols - 1 - 2 * d
            flow = net[d] + jnp.where(edge, pltpu.roll(colflow[0], turn, 1), 0.0)
            net[d] = flow
            at = pl.multiple_of(d * brick_rows, brick_rows)
            for p in range(n_wide):
                slab[p, pl.ds(at, brick_rows), :] = flow[p * brick_rows:(p + 1) * brick_rows]
            most = jnp.maximum(
                most, outs[d] + jnp.where(edge, pltpu.roll(colflow[1], turn, 1), 0.0)
            )
        return most

    most = lax.fori_loop(0, depth // 2, add_sides, nothing)

    maxw[w] = jnp.max(most.reshape(rows // brick_rows, brick_rows, cols), axis=0)
    wait_wide = everyone("wide", lambda peer: maxw.at[w], lambda sender: maxw.at[sender])

    def part(sender):
        return netb.at[pl.ds(pl.multiple_of(sender * band, band), band), :]

    bulk = count[0]

    def brick_copy(number, sender, peer):
        return remote(slab.at[peer], part(sender), bulk + number, "wide", peer)

    for off in range(1, n_wide):
        slot()
        brick_copy(off - 1, w, lax.rem(w + off, n_wide)).start()
    netb[pl.ds(pl.multiple_of(w * band, band), band), :] = slab[w]

    all_cols = cols * n_narrow
    for copy in loading[4:]:
        copy.wait()
    cell = row * cols + lane

    def split(column):
        if all_cols & (all_cols - 1):
            return lax.div(column, all_cols), lax.rem(column, all_cols)
        return column >> (all_cols.bit_length() - 1), column & (all_cols - 1)

    def well(i, total):
        for u in range(8):
            well_row, well_col = split(wcol_ref[i * 8 + u])
            inside = well_col - k * cols
            target = jnp.where(
                (inside >= 0) & (inside < cols), well_row * cols + inside, -1
            )
            total = total + jnp.where(cell == target, wrate_ref[i * 8 + u], 0.0)
        return total

    source[...] = lax.fori_loop(0, wcol_ref.shape[0] // 8, well, nothing)

    def add_res(i, total):
        return total + jnp.sum(res_ref[pl.ds(i * 16, 16)], axis=0)

    res_total = jnp.sum(lax.fori_loop(0, layers // 16, add_res, zero), axis=(0, 1), keepdims=True)

    def at_layer(z):
        return pl.ds(pl.multiple_of(z * brick_rows, brick_rows), brick_rows)

    def look_up_band(band_number):
        for u in range(depth):
            z = band_number * depth + u
            perm, water, oil = properties(rockb[z])
            coef[at_layer(z), :] = perm
            rface[at_layer(z), :] = water
            cface[at_layer(z), :] = oil

    for copy in own_raw:
        copy.wait()
    look_up_band(w)

    def take_raw(off, carry):
        sender = lax.rem(w + n_wide - off, n_wide)
        for f in range(2):
            raw_copy(off, f, sender, sender).wait_recv()
        look_up_band(sender)
        return carry

    lax.fori_loop(1, n_wide, take_raw, 0)

    wait_wide()
    maxn[k] = jnp.max(maxw[...], axis=0)
    everyone("narrow", lambda peer: maxn.at[k], lambda sender: maxn.at[sender])()
    top_rate = jnp.max(jnp.max(maxn[...], axis=0), axis=(0, 1), keepdims=True)
    step_size = courant / (top_rate + tiny)

    last_row = brick_rows - 1
    packs[...] = jnp.zeros(packs.shape, F32)

    def assemble_band(band_number):
        base = band_number * depth
        lane_base = lax.rem(base, cols)
        tile = at_layer(lax.div(base, cols))
        low = packs[0, 0, tile, :]
        high = packs[1, 0, tile, :]
        wells = step_size * source[pl.ds(pl.multiple_of(w * brick_rows, brick_rows), brick_rows), :]
        for u in range(depth):
            at = at_layer(base + u)
            s = satb[base + u] - step_size * netb[at, :] + wells
            here = coef[at, :] * (rface[at, :] * s * s + cface[at, :] * (1.0 - s) * (1.0 - s))
            coef[at, :] = here
            rf = jnp.where(trow == last_row, 0.0, harmonic(here, pltpu.roll(here, last_row, 0)))
            cf = jnp.where(tlane == cols - 1, 0.0, harmonic(here, pltpu.roll(here, cols - 1, 1)))
            rface[at, :] = rf
            cface[at, :] = cf
            scale[at, :] = (
                compress * here + pltpu.roll(rf, 1, 0) + rf + pltpu.roll(cf, 1, 1) + cf
            )
            spot = lane_base + u
            turned = pltpu.roll(here, spot, 1)
            low = jnp.where(tlane == spot, turned, low)
            high = jnp.where(tlane == lax.rem(spot + cols - 1, cols), turned, high)
        packs[0, 0, tile, :] = low
        packs[1, 0, tile, :] = high

    assemble_band(w)

    def take_band(off, carry):
        sender = lax.rem(w + n_wide - off, n_wide)
        brick_copy(off - 1, sender, sender).wait_recv()
        assemble_band(sender)
        return carry

    lax.fori_loop(1, n_wide, take_band, 0)

    def update(i, carry):
        total, cross, packed_low, packed_high = carry
        for u in range(2):
            d = i * 2 + u
            s = sat_ref[d] - step_size * net[d] + step_size * source[...]
            satnew_ref[d] = s
            value = fields[d + 1, 1] * (gains[d, 0] * s * s + gains[d, 1] * (1.0 - s) * (1.0 - s))
            turned = pltpu.roll(value, d, 1)
            packed_low = jnp.where(lane == d, turned, packed_low)
            packed_high = jnp.where(lane == lax.rem(d + cols - 1, cols), turned, packed_high)
            cross = cross + harmonic(value, pltpu.roll(value, rows - 1, 0))
            total = total + value
        return total, cross, packed_low, packed_high

    total, cross, packed_low, packed_high = lax.fori_loop(
        0, depth // 2, update, (nothing, nothing, blank, blank)
    )
    sidepack[0] = packed_low
    sidepack[1] = pltpu.roll(packed_high, 1, 1)
    wait_sides = neighbours(
        "narrow", sidepack.at[0], sidepack.at[1], sidehalo.at[0], sidehalo.at[1]
    )
    storing = pltpu.make_async_copy(satnew_ref, satnew_out, loads.at[0])
    storing.start()

    def by_brick(block):
        summed = jnp.sum(block.reshape(n_wide, brick_rows, cols), axis=1)
        return jnp.sum(summed, axis=1, keepdims=True)

    clane = lax.broadcasted_iota(jnp.int32, (n_wide, cols), 1)
    crow = lax.broadcasted_iota(jnp.int32, (n_wide, cols), 0)

    def send_sums():
        crossing = jnp.where(
            (lax.rem(row, brick_rows) == last_row) & (row < rows - 1), cross, 0.0
        )
        high_rows = by_brick(crossing)
        low_rows = by_brick(pltpu.roll(crossing, 1, 0))
        coef_sum = by_brick(total)
        wait_sides()
        low_cols = by_brick(
            jnp.where((lane < depth) & has_left, harmonic(sidepack[0], sidehalo[0]), 0.0)
        )
        high_cols = by_brick(
            jnp.where((lane < depth) & has_right, harmonic(sidepack[1], sidehalo[1]), 0.0)
        )
        diagonal = compress * coef_sum + low_rows + high_rows + low_cols + high_cols
        message = jnp.where((clane == 0) & (crow == w), res_total, 0.0)
        for i, value in enumerate((diagonal, low_rows, high_rows, low_cols, high_cols)):
            message = jnp.where(clane == i + 1, value, message)
        cw[w] = message
        return everyone("wide", lambda peer: cw.at[w], lambda sender: cw.at[sender])

    def at_narrow(sender):
        return cn.at[pl.ds(pl.multiple_of(sender * n_wide, n_wide), n_wide), :]

    def send_rows():
        cn[pl.ds(pl.multiple_of(k * n_wide, n_wide), n_wide), :] = jnp.sum(cw[...], axis=0)
        return everyone("narrow", lambda peer: at_narrow(k), at_narrow)

    def send_sides(ref, which):
        rowsend[0, which] = ref[pl.ds(0, layers, stride=brick_rows), :]
        rowsend[1, which] = ref[pl.ds(last_row, layers, stride=brick_rows), :]
        wait_rows = neighbours(
            "wide", rowsend.at[0, which], rowsend.at[1, which],
            rowhalo.at[0, which], rowhalo.at[1, which],
        )
        packs[1, which] = pltpu.roll(packs[1, which], 1, 1)
        wait_packs = neighbours(
            "narrow", packs.at[0, which], packs.at[1, which],
            packhalo.at[0, which], packhalo.at[1, which],
        )
        return wait_rows, wait_packs

    wait_rows, wait_packs = send_sides(coef, 0)

    unroll = 32

    def assemble(i, carry):
        below, here = carry
        for u in range(32):
            z = i * 32 + u
            above = coef[at_layer(z + 1), :]
            df = jnp.where(z < layers - 1, harmonic(here, above), zero)
            sc = relax / (scale[at_layer(z), :] + below + df)
            dface[at_layer(z), :] = df
            scale[at_layer(z), :] = sc
            v = sc * res_ref[z]
            first[at_layer(z), :] = v
            va[at_layer(z), :] = v
            below, here = df, above
        return below, here

    lax.fori_loop(0, layers // 32, assemble, (zero, coef[pl.ds(0, brick_rows), :]))

    group = min(64, layers)

    def sweep(packing):
        def body(i, carry):
            v_below, d_below, v, low, high = carry
            for u in range(group):
                z = i * group + u
                v_above = va[at_layer(z + 1), :]
                df = dface[at_layer(z), :]
                rf = rface[at_layer(z), :]
                cf = cface[at_layer(z), :]
                off = (
                    d_below * v_below + df * v_above
                    + pltpu.roll(rf * v, 1, 0) + rf * pltpu.roll(v, last_row, 0)
                    + pltpu.roll(cf * v, 1, 1) + cf * pltpu.roll(v, cols - 1, 1)
                )
                fresh = (1.0 - relax) * v + first[at_layer(z), :] + scale[at_layer(z), :] * off
                va[at_layer(z), :] = fresh
                if packing:
                    spot = lax.rem(z, cols)
                    turned = pltpu.roll(fresh, spot, 1)
                    low = jnp.where(tlane == spot, turned, low)
                    high = jnp.where(tlane == lax.rem(spot + cols - 1, cols), turned, high)
                v_below, d_below, v = v, df, v_above
            if packing:
                tile = at_layer(lax.div(i * group, cols))
                packs[0, 1, tile, :] = low
                packs[1, 1, tile, :] = high
            return v_below, d_below, v, low, high

        lax.fori_loop(0, layers // group, body, (zero, zero, va[pl.ds(0, brick_rows), :], zero, zero))

    bricks = n_wide * n_narrow
    blane = lax.broadcasted_iota(jnp.int32, (bricks, cols), 1)
    brow = lax.broadcasted_iota(jnp.int32, (bricks, cols), 0)

    mine = k * n_wide + w

    def coarse_solve():
        gathered = cn[...]
        matrix = jnp.where(blane == brow, gathered[:, 1:2], 0.0)
        for i, away in ((2, -1), (3, 1), (4, -n_wide), (5, n_wide)):
            matrix = jnp.where(blane == brow + away, matrix - gathered[:, i:i + 1], matrix)
        right = jnp.broadcast_to(gathered[:, 0:1], (bricks, cols))
        def pivoted(j, block, side):
            column = jnp.broadcast_to(block[:, j:j + 1], (bricks, cols))
            factor = jnp.where(brow == j, 0.0, column / column[j:j + 1])
            return factor * block[j:j + 1], factor * side[j:j + 1]

        def colour(j):
            return (j // n_wide + j % n_wide) % 2

        block, side = matrix, right
        for j in range(bricks):
            if colour(j) == 0:
                change, side_change = pivoted(j, block, side)
                matrix, right = matrix - change, right - side_change
        for j in range(bricks):
            if colour(j) == 1:
                change, side_change = pivoted(j, matrix, right)
                matrix, right = matrix - change, right - side_change
        own = brow == mine
        pivot = jnp.sum(jnp.where(own & (blane == mine), matrix, 0.0), axis=(0, 1), keepdims=True)
        answer = jnp.sum(jnp.where(own & (blane == 0), right, 0.0), axis=(0, 1), keepdims=True)
        return answer / pivot

    def plain_sweep(number, carry):
        sweep(False)
        return carry

    wait_sums = send_sums()
    early = (SWEEPS - 2) // 2
    lax.fori_loop(0, early, plain_sweep, 0)
    wait_sums()
    wait_coarse = send_rows()
    lax.fori_loop(early, SWEEPS - 2, plain_sweep, 0)
    sweep(True)
    wait_value_rows, wait_value_packs = send_sides(va, 1)
    wait_coarse()
    coarse_value = coarse_solve()

    wait_rows()
    wait_packs()
    wait_value_rows()
    wait_value_packs()
    for side, present in ((0, has_below), (1, has_above)):
        c = jnp.where(present, rowhalo[side, 0], 0.0)
        rowterm[side, 0] = c
        rowterm[side, 1] = jnp.where(present, c * rowhalo[side, 1], 0.0)
    for side, present in ((0, has_left), (1, has_right)):
        c = jnp.where(present, packhalo[side, 0], 0.0)
        packterm[side, 0] = c
        packterm[side, 1] = jnp.where(present, c * packhalo[side, 1], 0.0)

    def store(i):
        part = pl.ds(i * unroll, unroll)
        return pltpu.make_async_copy(prec_ref.at[part], prec_out.at[part], stores.at[i])

    for t in range(tiles):
        tile = pl.ds(t * brick_rows, brick_rows)

        def average(i, carry):
            for u in range(unroll):
                z = i * unroll + u
                layer = t * cols + z
                c = coef[at_layer(layer), :]
                sums = [c, c * va[at_layer(layer), :]]
                for j in range(2):
                    low = rowterm[0, j, pl.ds(layer, 1), :]
                    high = rowterm[1, j, pl.ds(layer, 1), :]
                    left = pltpu.roll(packterm[0, j, tile, :], lax.rem(cols - z, cols), 1)
                    right = pltpu.roll(packterm[1, j, tile, :], cols - 1 - z, 1)
                    sums[j] = (
                        sums[j]
                        + jnp.where(trow == 0, low, 0.0) + jnp.where(trow == last_row, high, 0.0)
                        + jnp.where(tlane == 0, left, 0.0)
                        + jnp.where(tlane == cols - 1, right, 0.0)
                    )
                prec_ref[layer] = sums[1] / sums[0] + coarse_value
            store(t * (cols // unroll) + i).start()
            return carry

        lax.fori_loop(0, cols // unroll, average, 0)

    for off in range(1, n_wide):
        peer = lax.rem(w + off, n_wide)
        for f in range(2):
            raw_copy(off, f, w, peer).wait_send()
        brick_copy(off - 1, w, peer).wait_send()
    storing.wait()
    for i in range(layers // unroll):
        store(i).wait()


def deliver(a_in, b_in, a_out, b_out, a_held, b_held, arrive, leave):
    arriving, leaving = [], []
    for src, held, dst in ((a_in, a_held, a_out), (b_in, b_held, b_out)):
        part = src.shape[0] // 4
        for i in range(4):
            at = pl.ds(i * part, part)
            number = len(arriving)
            arriving.append(pltpu.make_async_copy(src.at[at], held.at[at], arrive.at[number]))
            leaving.append(pltpu.make_async_copy(held.at[at], dst.at[at], leave.at[number]))
            arriving[-1].start()
    for first, second in zip(arriving, leaving):
        first.wait()
        second.start()
    for second in leaving:
        second.wait()


def shards(n_wide, n_narrow, *args):
    sat, residual = args[0], args[6]
    depth, rows, cols = sat.shape
    layers, brick_rows, _ = residual.shape
    tiles = layers // cols
    bricks = n_wide * n_narrow
    cells = layers * brick_rows
    copies = 2 * 9 + 5 * (n_wide - 1) + 2 * (n_narrow - 1)
    anywhere = pl.BlockSpec(memory_space=pl.ANY)
    table, wells = args[3].shape, args[4].shape

    def buffer(*shape):
        return pltpu.VMEM(shape, F32)

    outputs = pl.pallas_call(
        functools.partial(kernel, n_wide, n_narrow),
        out_shape=(
            jax.ShapeDtypeStruct(sat.shape, F32),
            jax.ShapeDtypeStruct(residual.shape, F32),
        ),
        in_specs=[anywhere] * 7,
        out_specs=(anywhere, anywhere),
        scratch_shapes=[
            buffer(*sat.shape),
            buffer(*residual.shape),
            buffer(*sat.shape),
            buffer(*sat.shape),
            buffer(*sat.shape),
            pltpu.VMEM(sat.shape, jnp.int32),
            pltpu.SMEM(table, F32),
            pltpu.SMEM(wells, jnp.int32),
            pltpu.SMEM(wells, F32),
            buffer(*residual.shape),
            buffer(depth + 2, 3, rows, cols),
            buffer(depth, 2, rows, cols),
            buffer(depth, rows, cols),
            buffer(2, rows, cols),
            buffer(2, rows, cols),
            buffer(2, rows, cols),
            buffer(rows, cols),
            buffer(n_wide, brick_rows, cols),
            buffer(n_narrow, brick_rows, cols),
            buffer(n_wide, depth * brick_rows, cols),
            buffer(cells + brick_rows, cols),
            buffer(cells, cols),
            buffer(cells, cols),
            buffer(cells, cols),
            buffer(cells, cols),
            buffer(cells, cols),
            buffer(cells + brick_rows, cols),
            buffer(2, 2, layers, cols),
            buffer(2, 2, layers, cols),
            buffer(2, 2, layers, cols),
            buffer(2, 2, tiles * brick_rows, cols),
            buffer(2, 2, tiles * brick_rows, cols),
            buffer(2, 2, tiles * brick_rows, cols),
            buffer(n_wide, n_wide, cols),
            buffer(bricks, cols),
            buffer(2, rows, cols),
            buffer(2, rows, cols),
            buffer(2, rows, cols),
            buffer(2, rows, cols),
            pltpu.VMEM((2, rows, cols), jnp.int32),
            buffer(*residual.shape),
            pltpu.VMEM(residual.shape, jnp.int32),
            buffer(cells, cols),
            pltpu.SemaphoreType.DMA((9,)),
            pltpu.SemaphoreType.DMA((layers // 32,)),
            pltpu.SemaphoreType.DMA((copies,)),
            pltpu.SemaphoreType.DMA((copies,)),
        ],
        compiler_params=pltpu.CompilerParams(
            collective_id=0, has_side_effects=True, vmem_limit_bytes=56 * 1024 * 1024
        ),
    )(*args)
    return pl.pallas_call(
        deliver,
        out_shape=(
            jax.ShapeDtypeStruct(sat.shape, F32),
            jax.ShapeDtypeStruct(residual.shape, F32),
        ),
        in_specs=[anywhere] * 2,
        out_specs=(anywhere, anywhere),
        scratch_shapes=[
            buffer(*sat.shape),
            buffer(*residual.shape),
            pltpu.SemaphoreType.DMA((8,)),
            pltpu.SemaphoreType.DMA((8,)),
        ],
        compiler_params=pltpu.CompilerParams(vmem_limit_bytes=60 * 1024 * 1024),
    )(*outputs)


def solution(mesh):
    placed = (
        P("wide", None, "narrow"),
        P("wide", None, "narrow"),
        P("wide", None, "narrow"),
        P(),
        P(),
        P(),
        P(None, "wide", "narrow"),
    )
    return jax.shard_map(
        functools.partial(shards, mesh.shape["wide"], mesh.shape["narrow"]),
        mesh=mesh,
        in_specs=placed,
        out_specs=(P("wide", None, "narrow"), P(None, "wide", "narrow")),
        check_vma=False,
    )
```

```python
import functools

import jax
import jax.numpy as jnp
from jax import lax
from jax.experimental import pallas as pl
from jax.experimental.pallas import tpu as pltpu
from jax.sharding import PartitionSpec as P

SWEEPS = 6

compress = 0.05
relax = 0.8
gravity = 0.5
courant = 0.5
tiny = 1e-06

F32 = jnp.float32


def harmonic(a, b):
    return 2.0 * a * b / (a + b)


def flows(low, high, lift):
    total = harmonic(low[1], high[1]) * (low[0] - high[0] + lift)
    return total, total * jnp.where(total > 0, low[2], high[2])


def lookup(bits, table_ref, row, count):
    level = [table_ref[row, i] for i in range(count)]
    for bit in bits:
        level = [jnp.where(bit, level[i + 1], level[i]) for i in range(0, len(level), 2)]
    return level[0]


def kernel(
    n_wide, n_narrow,
    sat_in, pres_in, rock_in, table_in, wcol_in, wrate_in, res_in,
    satnew_out, prec_out,
    satnew_ref, prec_ref, outs,
    sat_ref, pres_ref, rock_ref, table_ref, wcol_ref, wrate_ref, res_ref,
    fields, gains, net, colpack, colhalo, colflow, source, maxw, maxn,
    slab, coef, dface, rface, cface, scale, first, va,
    rowsend, rowhalo, rowterm, packs, packhalo, packterm, cw, cn, sidepack, sidehalo,
    satb, rockb, netb, netslab,
    loads, stores, sends, recvs,
):
    depth, rows, cols = sat_ref.shape
    layers, brick_rows, _ = res_ref.shape
    w = lax.axis_index("wide")
    k = lax.axis_index("narrow")
    tiles = layers // cols
    band = depth * brick_rows
    has = {"wide": (w > 0, w < n_wide - 1), "narrow": (k > 0, k < n_narrow - 1)}
    place = {"wide": w, "narrow": k}
    size = {"wide": n_wide, "narrow": n_narrow}
    count = [0]

    loading = [
        pltpu.make_async_copy(src, dst, loads.at[i])
        for i, (src, dst) in enumerate((
            (table_in, table_ref), (rock_in, rock_ref), (sat_in, sat_ref), (pres_in, pres_ref),
            (wcol_in, wcol_ref), (wrate_in, wrate_ref), (res_in, res_ref),
        ))
    ]
    for copy in loading:
        copy.start()

    def slot():
        count[0] += 1
        return count[0] - 1

    barrier = pltpu.get_barrier_semaphore()
    for axis in ("wide", "narrow"):
        for off in range(1, size[axis]):
            peer = lax.rem(place[axis] + off, size[axis])
            pl.semaphore_signal(
                barrier, inc=1, device_id={axis: peer}, device_id_type=pl.DeviceIdType.MESH
            )

    def remote(src, dst, number, axis, peer):
        return pltpu.make_async_remote_copy(
            src_ref=src, dst_ref=dst, send_sem=sends.at[number], recv_sem=recvs.at[number],
            device_id={axis: peer}, device_id_type=pl.DeviceIdType.MESH,
        )

    def neighbours(axis, low_src, high_src, from_low, from_high):
        down, up = slot(), slot()
        me = place[axis]
        has_low, has_high = has[axis]

        @pl.when(has_low)
        def _():
            remote(low_src, from_high, down, axis, me - 1).start()

        @pl.when(has_high)
        def _():
            remote(high_src, from_low, up, axis, me + 1).start()

        def wait():
            @pl.when(has_low)
            def _():
                remote(low_src, from_high, down, axis, me - 1).wait_send()
                remote(high_src, from_low, up, axis, me - 1).wait_recv()

            @pl.when(has_high)
            def _():
                remote(high_src, from_low, up, axis, me + 1).wait_send()
                remote(low_src, from_high, down, axis, me + 1).wait_recv()

        return wait

    def everyone(axis, src_of, dst_from):
        copies = []
        me = place[axis]
        n = size[axis]
        for off in range(1, n):
            number = slot()
            peer = lax.rem(me + off, n)
            copy = remote(src_of(peer), dst_from(me), number, axis, peer)
            copy.start()
            sender = lax.rem(me + n - off, n)
            copies.append((copy, remote(src_of(peer), dst_from(sender), number, axis, peer)))

        def wait():
            for sent, received in copies:
                sent.wait_send()
                received.wait_recv()

        return wait

    def xor(a, b):
        total, bit = 0, 1
        while bit < n_wide:
            total = total + bit * lax.rem(lax.div(a, bit) + lax.div(b, bit), 2)
            bit *= 2
        return total

    odd = lax.rem(w, 2)
    order = list(range(2, n_wide, 2)) + list(range(3, n_wide, 2)) + [1]
    distances = []
    for off in order:
        other = off ^ 6 if n_wide >= 8 and off in (2, 3, 4, 5) else off
        distances.append(off + odd * (other - off))

    lane = lax.broadcasted_iota(jnp.int32, (rows, cols), 1)
    row = lax.broadcasted_iota(jnp.int32, (rows, cols), 0)
    tlane = lax.broadcasted_iota(jnp.int32, (brick_rows, cols), 1)
    trow = lax.broadcasted_iota(jnp.int32, (brick_rows, cols), 0)
    zero = jnp.zeros((brick_rows, cols), F32)
    one = jnp.ones((brick_rows, cols), F32)

    @pl.when(w == 0)
    def _():
        fields[0] = jnp.ones((3, rows, cols), F32)
        rowhalo[0] = jnp.ones((2, layers, cols), F32)

    @pl.when(w == n_wide - 1)
    def _():
        fields[depth + 1] = jnp.ones((3, rows, cols), F32)
        rowhalo[1] = jnp.ones((2, layers, cols), F32)

    @pl.when(k == 0)
    def _():
        sidehalo[0] = jnp.ones((rows, cols), F32)
        colhalo[0] = jnp.ones((rows, cols), F32)
        packhalo[0] = jnp.ones((2, tiles * brick_rows, cols), F32)

    @pl.when(k == n_narrow - 1)
    def _():
        sidehalo[1] = jnp.ones((rows, cols), F32)
        colhalo[1] = jnp.ones((rows, cols), F32)
        packhalo[1] = jnp.ones((2, tiles * brick_rows, cols), F32)

    coef[pl.ds(layers * brick_rows, brick_rows), :] = one
    va[pl.ds(layers * brick_rows, brick_rows), :] = zero

    rocks = table_ref.shape[1]
    for copy in loading[:4]:
        copy.wait()

    def properties(rock):
        bits = []
        step = 1
        while step < rocks:
            bits.append((rock & step) != 0)
            step *= 2
        return [lookup(bits, table_ref, i, rocks) for i in range(3)]

    def derive(d, carry):
        packed_low, packed_high = carry
        perm, water, oil = properties(rock_ref[d])
        s = sat_ref[d]
        water_mob = water * s * s
        oil_mob = oil * (1.0 - s) * (1.0 - s)
        frac = water_mob / (water_mob + oil_mob)
        gains[d, 0] = water
        gains[d, 1] = oil
        for f, value in enumerate((pres_ref[d], perm, frac)):
            fields[d + 1, f] = value
            spot = 2 * (d + f * depth)
            turned = pltpu.roll(value, spot, 1)
            packed_low = jnp.where(lane == spot, turned, packed_low)
            packed_high = jnp.where(lane == lax.rem(spot + cols - 1, cols), turned, packed_high)
        return packed_low, packed_high

    blank = jnp.ones((rows, cols), F32)
    packed_low, packed_high = lax.fori_loop(0, depth, derive, (blank, blank))
    colpack[0] = packed_low
    colpack[1] = pltpu.roll(packed_high, 1, 1)

    pl.semaphore_wait(barrier, n_wide + n_narrow - 2)
    wait_planes = neighbours(
        "wide", fields.at[1], fields.at[depth], fields.at[0], fields.at[depth + 1]
    )
    wait_cols = neighbours(
        "narrow", colpack.at[0], colpack.at[1], colhalo.at[0], colhalo.at[1]
    )

    ahead = depth // 4

    def brick_part(ref, sender):
        return ref.at[pl.ds(sender * ahead, ahead)]

    def brick_rows_of(ref, peer):
        return ref.at[
            pl.ds(0, ahead), pl.ds(pl.multiple_of(peer * brick_rows, brick_rows), brick_rows), :
        ]

    raw = count[0]
    raw_fields = ((sat_ref, satb), (rock_ref, rockb))

    def raw_copy(distance, f, sender, peer):
        src, dst = raw_fields[f]
        return remote(
            brick_rows_of(src, peer), brick_part(dst, sender),
            raw + 2 * (distance - 1) + f, "wide", peer,
        )

    for distance in distances:
        for f in range(2):
            slot()
            raw_copy(distance, f, w, xor(w, distance)).start()
    own_raw = [
        pltpu.make_async_copy(brick_rows_of(src, w), brick_part(dst, w), loads.at[7 + f])
        for f, (src, dst) in enumerate(raw_fields)
    ]
    for copy in own_raw:
        copy.start()

    nothing = jnp.zeros((rows, cols), F32)
    has_below, has_above = has["wide"]
    has_left, has_right = has["narrow"]

    def plane(d):
        return [fields[d, f] for f in range(3)]

    def transport(d, below_total, below_water):
        here = plane(d + 1)
        above_total, above_water = flows(here, plane(lax.min(d + 2, depth)), gravity)
        above_total = jnp.where(d < depth - 1, above_total, nothing)
        above_water = jnp.where(d < depth - 1, above_water, nothing)
        flow = above_water - below_water
        out = jnp.maximum(above_total, 0.0) + jnp.maximum(-below_total, 0.0)

        total, water = flows(here, [pltpu.roll(x, rows - 1, 0) for x in here], 0.0)
        total = jnp.where(row == rows - 1, 0.0, total)
        water = jnp.where(row == rows - 1, 0.0, water)
        flow = flow + (water - pltpu.roll(water, 1, 0))
        out = out + (jnp.maximum(total, 0.0) + jnp.maximum(-pltpu.roll(total, 1, 0), 0.0))

        total, water = flows(here, [pltpu.roll(x, cols - 1, 1) for x in here], 0.0)
        total = jnp.where(lane == cols - 1, 0.0, total)
        water = jnp.where(lane == cols - 1, 0.0, water)
        net[d] = flow + (water - pltpu.roll(water, 1, 1))
        outs[d] = out + (jnp.maximum(total, 0.0) + jnp.maximum(-pltpu.roll(total, 1, 1), 0.0))
        return above_total, above_water

    def transport_group(i, carry):
        for u in range(4):
            carry = transport(i * 4 + u, *carry)
        return carry

    lax.fori_loop(0, depth // 4, transport_group, (nothing, nothing))

    wait_cols()

    def unpack(block):
        return [block] + [pltpu.roll(block, cols - 2 * f * depth, 1) for f in (1, 2)]

    low_total, low_water = flows(unpack(colhalo[0]), unpack(colpack[0]), 0.0)
    high_total, high_water = flows(unpack(colpack[1]), unpack(colhalo[1]), 0.0)
    even = lax.rem(lane, 2) == 0
    colflow[0] = jnp.where(
        even,
        jnp.where(has_right, high_water, nothing),
        pltpu.roll(jnp.where(has_left, -low_water, nothing), 1, 1),
    )
    colflow[1] = jnp.maximum(jnp.where(
        even,
        jnp.where(has_right, high_total, nothing),
        pltpu.roll(jnp.where(has_left, -low_total, nothing), 1, 1),
    ), 0.0)

    wait_planes()
    side_total, side_water = flows(plane(0), plane(1), gravity)
    net[0] = net[0] - jnp.where(has_below, side_water, nothing)
    outs[0] = outs[0] + jnp.maximum(jnp.where(has_below, -side_total, nothing), 0.0)
    side_total, side_water = flows(plane(depth), plane(depth + 1), gravity)
    net[depth - 1] = net[depth - 1] + jnp.where(has_above, side_water, nothing)
    outs[depth - 1] = outs[depth - 1] + jnp.maximum(jnp.where(has_above, side_total, nothing), 0.0)
    edge = (lane == 0) | (lane == cols - 1)

    def add_sides(i, most):
        for u in range(2):
            d = i * 2 + u
            turn = cols - 1 - 2 * d
            net[d] = net[d] + jnp.where(edge, pltpu.roll(colflow[0], turn, 1), 0.0)
            most = jnp.maximum(
                most, outs[d] + jnp.where(edge, pltpu.roll(colflow[1], turn, 1), 0.0)
            )
        return most

    most = lax.fori_loop(0, depth // 2, add_sides, nothing)

    maxw[w] = jnp.max(most.reshape(rows // brick_rows, brick_rows, cols), axis=0)
    wait_wide = everyone("wide", lambda peer: maxw.at[w], lambda sender: maxw.at[sender])
    ahead_rows = ahead * brick_rows
    for d in range(ahead):
        for p in range(n_wide):
            netslab[p, pl.ds(d * brick_rows, brick_rows), :] = net[
                d, pl.ds(p * brick_rows, brick_rows), :
            ]

    def net_part(sender):
        return netb.at[pl.ds(pl.multiple_of(sender * ahead_rows, ahead_rows), ahead_rows), :]

    net_base = count[0]

    def net_copy(distance, sender, peer):
        return remote(
            netslab.at[peer], net_part(sender), net_base + distance - 1, "wide", peer
        )

    for distance in distances:
        slot()
        net_copy(distance, w, xor(w, distance)).start()
    netb[pl.ds(pl.multiple_of(w * ahead_rows, ahead_rows), ahead_rows), :] = netslab[w]

    all_cols = cols * n_narrow
    for copy in loading[4:]:
        copy.wait()
    cell = row * cols + lane

    def split(column):
        if all_cols & (all_cols - 1):
            return lax.div(column, all_cols), lax.rem(column, all_cols)
        return column >> (all_cols.bit_length() - 1), column & (all_cols - 1)

    def well(i, total):
        for u in range(8):
            well_row, well_col = split(wcol_ref[i * 8 + u])
            inside = well_col - k * cols
            target = jnp.where(
                (inside >= 0) & (inside < cols), well_row * cols + inside, -1
            )
            total = total + jnp.where(cell == target, wrate_ref[i * 8 + u], 0.0)
        return total

    source[...] = lax.fori_loop(0, wcol_ref.shape[0] // 8, well, nothing)

    def add_res(i, total):
        return total + jnp.sum(res_ref[pl.ds(i * 16, 16)], axis=0)

    res_total = jnp.sum(lax.fori_loop(0, layers // 16, add_res, zero), axis=(0, 1), keepdims=True)

    def at_layer(z):
        return pl.ds(pl.multiple_of(z * brick_rows, brick_rows), brick_rows)

    def look_up_band(band_number):
        for u in range(ahead):
            at = at_layer(band_number * depth + u)
            perm, water, oil = properties(rockb[band_number * ahead + u])
            coef[at, :] = perm
            rface[at, :] = water
            cface[at, :] = oil

    for copy in own_raw:
        copy.wait()
    look_up_band(w)

    def take_raw(distance, carry):
        sender = xor(w, distance)
        for f in range(2):
            raw_copy(distance, f, sender, sender).wait_recv()
        look_up_band(sender)
        return carry

    lax.fori_loop(1, n_wide, take_raw, 0)
    wait_wide()
    maxn[k] = jnp.max(maxw[...], axis=0)
    everyone("narrow", lambda peer: maxn.at[k], lambda sender: maxn.at[sender])()
    top_rate = jnp.max(jnp.max(maxn[...], axis=0), axis=(0, 1), keepdims=True)
    step_size = courant / (top_rate + tiny)

    def update(i, carry):
        for u in range(2):
            d = i * 2 + u
            s = sat_ref[d] - step_size * net[d] + step_size * source[...]
            satnew_ref[d] = s
            value = fields[d + 1, 1] * (gains[d, 0] * s * s + gains[d, 1] * (1.0 - s) * (1.0 - s))
            at = pl.multiple_of(d * brick_rows, brick_rows)
            for p in range(n_wide):
                slab[p, pl.ds(at, brick_rows), :] = value[p * brick_rows:(p + 1) * brick_rows]
        return carry

    lax.fori_loop(0, depth // 2, update, 0)

    late_rows = band - ahead_rows

    def part(sender):
        return coef.at[
            pl.ds(pl.multiple_of(sender * band + ahead_rows, brick_rows), late_rows), :
        ]

    bulk = count[0]

    def brick_copy(distance, sender, peer):
        return remote(
            slab.at[peer, pl.ds(ahead_rows, late_rows), :], part(sender),
            bulk + distance - 1, "wide", peer,
        )

    for distance in distances:
        slot()
        brick_copy(distance, w, xor(w, distance)).start()
    storing = pltpu.make_async_copy(satnew_ref, satnew_out, loads.at[0])
    storing.start()

    def survey(i, carry):
        total, cross, packed_low, packed_high = carry
        for u in range(2):
            d = i * 2 + u
            at = pl.ds(pl.multiple_of(d * brick_rows, brick_rows), brick_rows)
            value = jnp.concatenate([slab[p, at, :] for p in range(n_wide)], axis=0)
            turned = pltpu.roll(value, d, 1)
            packed_low = jnp.where(lane == d, turned, packed_low)
            packed_high = jnp.where(lane == lax.rem(d + cols - 1, cols), turned, packed_high)
            cross = cross + harmonic(value, pltpu.roll(value, rows - 1, 0))
            total = total + value
        return total, cross, packed_low, packed_high

    total, cross, packed_low, packed_high = lax.fori_loop(
        0, depth // 2, survey, (nothing, nothing, blank, blank)
    )
    sidepack[0] = packed_low
    sidepack[1] = pltpu.roll(packed_high, 1, 1)
    wait_sides = neighbours(
        "narrow", sidepack.at[0], sidepack.at[1], sidehalo.at[0], sidehalo.at[1]
    )

    last_row = brick_rows - 1
    packs[...] = jnp.zeros(packs.shape, F32)

    def assemble_band(band_number):
        base = band_number * depth
        lane_base = lax.rem(base, cols)
        tile = at_layer(lax.div(base, cols))
        low = packs[0, 0, tile, :]
        high = packs[1, 0, tile, :]
        own_wells = step_size * source[at_layer(w), :]
        for u in range(depth):
            here = coef[at_layer(base + u), :]
            if u < ahead:
                at = at_layer(base + u)
                near = band_number * ahead + u
                s = satb[near] - step_size * netb[at_layer(near), :] + own_wells
                here = here * (rface[at, :] * s * s + cface[at, :] * (1.0 - s) * (1.0 - s))
                coef[at, :] = here
            rf = jnp.where(trow == last_row, 0.0, harmonic(here, pltpu.roll(here, last_row, 0)))
            cf = jnp.where(tlane == cols - 1, 0.0, harmonic(here, pltpu.roll(here, cols - 1, 1)))
            rface[at_layer(base + u), :] = rf
            cface[at_layer(base + u), :] = cf
            scale[at_layer(base + u), :] = (
                compress * here + pltpu.roll(rf, 1, 0) + rf + pltpu.roll(cf, 1, 1) + cf
            )
            spot = lane_base + u
            turned = pltpu.roll(here, spot, 1)
            low = jnp.where(tlane == spot, turned, low)
            high = jnp.where(tlane == lax.rem(spot + cols - 1, cols), turned, high)
        packs[0, 0, tile, :] = low
        packs[1, 0, tile, :] = high

    coef[pl.ds(pl.multiple_of(w * band + ahead_rows, brick_rows), late_rows), :] = slab[
        w, pl.ds(ahead_rows, late_rows), :
    ]
    assemble_band(w)

    brick_count = n_wide

    def by_brick(block):
        summed = jnp.sum(block.reshape(brick_count, brick_rows, cols), axis=1)
        return jnp.sum(summed, axis=1, keepdims=True)

    clane = lax.broadcasted_iota(jnp.int32, (brick_count, cols), 1)
    crow = lax.broadcasted_iota(jnp.int32, (brick_count, cols), 0)
    high_rows = by_brick(jnp.where((lax.rem(row, brick_rows) == brick_rows - 1) & (row < rows - 1), cross, 0.0))
    low_rows = by_brick(
        pltpu.roll(jnp.where((lax.rem(row, brick_rows) == brick_rows - 1) & (row < rows - 1), cross, 0.0), 1, 0)
    )
    coef_sum = by_brick(total)
    wait_sides()
    low_cols = by_brick(jnp.where((lane < depth) & has_left, harmonic(sidepack[0], sidehalo[0]), 0.0))
    high_cols = by_brick(jnp.where((lane < depth) & has_right, harmonic(sidepack[1], sidehalo[1]), 0.0))
    diagonal = compress * coef_sum + low_rows + high_rows + low_cols + high_cols
    message = jnp.where((clane == 0) & (crow == w), res_total, 0.0)
    for i, value in enumerate((diagonal, low_rows, high_rows, low_cols, high_cols)):
        message = jnp.where(clane == i + 1, value, message)
    cw[w] = message
    wait_sums = everyone("wide", lambda peer: cw.at[w], lambda sender: cw.at[sender])

    def take_band(distance, carry):
        sender = xor(w, distance)
        net_copy(distance, sender, sender).wait_recv()
        brick_copy(distance, sender, sender).wait_recv()
        assemble_band(sender)
        return carry

    lax.fori_loop(1, n_wide, take_band, 0)
    wait_sums()

    def at_narrow(sender):
        return cn.at[pl.ds(pl.multiple_of(sender * n_wide, n_wide), n_wide), :]

    cn[pl.ds(pl.multiple_of(k * n_wide, n_wide), n_wide), :] = jnp.sum(cw[...], axis=0)
    wait_coarse = everyone("narrow", lambda peer: at_narrow(k), at_narrow)

    def send_sides(ref, which):
        rowsend[0, which] = ref[pl.ds(0, layers, stride=brick_rows), :]
        rowsend[1, which] = ref[pl.ds(last_row, layers, stride=brick_rows), :]
        wait_rows = neighbours(
            "wide", rowsend.at[0, which], rowsend.at[1, which],
            rowhalo.at[0, which], rowhalo.at[1, which],
        )
        packs[1, which] = pltpu.roll(packs[1, which], 1, 1)
        wait_packs = neighbours(
            "narrow", packs.at[0, which], packs.at[1, which],
            packhalo.at[0, which], packhalo.at[1, which],
        )
        return wait_rows, wait_packs

    wait_rows, wait_packs = send_sides(coef, 0)

    unroll = 32

    def assemble(i, carry):
        below, here = carry
        for u in range(32):
            z = i * 32 + u
            above = coef[at_layer(z + 1), :]
            df = jnp.where(z < layers - 1, harmonic(here, above), zero)
            sc = relax / (scale[at_layer(z), :] + below + df)
            dface[at_layer(z), :] = df
            scale[at_layer(z), :] = sc
            v = sc * res_ref[z]
            first[at_layer(z), :] = v
            va[at_layer(z), :] = v
            below, here = df, above
        return below, here

    lax.fori_loop(0, layers // 32, assemble, (zero, coef[pl.ds(0, brick_rows), :]))

    group = min(64, layers)

    def sweep(packing):
        def body(i, carry):
            v_below, d_below, v, low, high = carry
            for u in range(group):
                z = i * group + u
                v_above = va[at_layer(z + 1), :]
                df = dface[at_layer(z), :]
                rf = rface[at_layer(z), :]
                cf = cface[at_layer(z), :]
                off = (
                    d_below * v_below + df * v_above
                    + pltpu.roll(rf * v, 1, 0) + rf * pltpu.roll(v, last_row, 0)
                    + pltpu.roll(cf * v, 1, 1) + cf * pltpu.roll(v, cols - 1, 1)
                )
                fresh = (1.0 - relax) * v + first[at_layer(z), :] + scale[at_layer(z), :] * off
                va[at_layer(z), :] = fresh
                if packing:
                    spot = lax.rem(z, cols)
                    turned = pltpu.roll(fresh, spot, 1)
                    low = jnp.where(tlane == spot, turned, low)
                    high = jnp.where(tlane == lax.rem(spot + cols - 1, cols), turned, high)
                v_below, d_below, v = v, df, v_above
            if packing:
                tile = at_layer(lax.div(i * group, cols))
                packs[0, 1, tile, :] = low
                packs[1, 1, tile, :] = high
            return v_below, d_below, v, low, high

        lax.fori_loop(0, layers // group, body, (zero, zero, va[pl.ds(0, brick_rows), :], zero, zero))

    bricks = n_wide * n_narrow
    blane = lax.broadcasted_iota(jnp.int32, (bricks, cols), 1)
    brow = lax.broadcasted_iota(jnp.int32, (bricks, cols), 0)

    mine = k * n_wide + w

    def coarse_solve():
        gathered = cn[...]
        matrix = jnp.where(blane == brow, gathered[:, 1:2], 0.0)
        for i, away in ((2, -1), (3, 1), (4, -n_wide), (5, n_wide)):
            matrix = jnp.where(blane == brow + away, matrix - gathered[:, i:i + 1], matrix)
        right = jnp.broadcast_to(gathered[:, 0:1], (bricks, cols))
        def pivoted(j, block, side):
            column = jnp.broadcast_to(block[:, j:j + 1], (bricks, cols))
            factor = jnp.where(brow == j, 0.0, column / column[j:j + 1])
            return factor * block[j:j + 1], factor * side[j:j + 1]

        def colour(j):
            return (j // n_wide + j % n_wide) % 2

        block, side = matrix, right
        for j in range(bricks):
            if colour(j) == 0:
                change, side_change = pivoted(j, block, side)
                matrix, right = matrix - change, right - side_change
        for j in range(bricks):
            if colour(j) == 1:
                change, side_change = pivoted(j, matrix, right)
                matrix, right = matrix - change, right - side_change
        own = brow == mine
        pivot = jnp.sum(jnp.where(own & (blane == mine), matrix, 0.0), axis=(0, 1), keepdims=True)
        answer = jnp.sum(jnp.where(own & (blane == 0), right, 0.0), axis=(0, 1), keepdims=True)
        return answer / pivot

    def plain_sweep(number, carry):
        sweep(False)
        return carry

    lax.fori_loop(0, SWEEPS - 2, plain_sweep, 0)
    sweep(True)
    wait_value_rows, wait_value_packs = send_sides(va, 1)
    wait_coarse()
    coarse_value = coarse_solve()

    wait_rows()
    wait_packs()
    wait_value_rows()
    wait_value_packs()
    for side, present in ((0, has_below), (1, has_above)):
        c = jnp.where(present, rowhalo[side, 0], 0.0)
        rowterm[side, 0] = c
        rowterm[side, 1] = jnp.where(present, c * rowhalo[side, 1], 0.0)
    for side, present in ((0, has_left), (1, has_right)):
        c = jnp.where(present, packhalo[side, 0], 0.0)
        packterm[side, 0] = c
        packterm[side, 1] = jnp.where(present, c * packhalo[side, 1], 0.0)

    def store(i):
        part = pl.ds(i * unroll, unroll)
        return pltpu.make_async_copy(prec_ref.at[part], prec_out.at[part], stores.at[i])

    for t in range(tiles):
        tile = pl.ds(t * brick_rows, brick_rows)

        def average(i, carry):
            for u in range(unroll):
                z = i * unroll + u
                layer = t * cols + z
                c = coef[at_layer(layer), :]
                sums = [c, c * va[at_layer(layer), :]]
                for j in range(2):
                    low = rowterm[0, j, pl.ds(layer, 1), :]
                    high = rowterm[1, j, pl.ds(layer, 1), :]
                    left = pltpu.roll(packterm[0, j, tile, :], lax.rem(cols - z, cols), 1)
                    right = pltpu.roll(packterm[1, j, tile, :], cols - 1 - z, 1)
                    sums[j] = (
                        sums[j]
                        + jnp.where(trow == 0, low, 0.0) + jnp.where(trow == last_row, high, 0.0)
                        + jnp.where(tlane == 0, left, 0.0)
                        + jnp.where(tlane == cols - 1, right, 0.0)
                    )
                prec_ref[layer] = sums[1] / sums[0] + coarse_value
            store(t * (cols // unroll) + i).start()
            return carry

        lax.fori_loop(0, cols // unroll, average, 0)

    for distance in range(1, n_wide):
        peer = xor(w, distance)
        for f in range(2):
            raw_copy(distance, f, w, peer).wait_send()
        net_copy(distance, w, peer).wait_send()
        brick_copy(distance, w, peer).wait_send()
    storing.wait()
    for i in range(layers // unroll):
        store(i).wait()


def deliver(a_in, b_in, a_out, b_out, a_held, b_held, arrive, leave):
    arriving, leaving = [], []
    for src, held, dst in ((a_in, a_held, a_out), (b_in, b_held, b_out)):
        part = src.shape[0] // 4
        for i in range(4):
            at = pl.ds(i * part, part)
            number = len(arriving)
            arriving.append(pltpu.make_async_copy(src.at[at], held.at[at], arrive.at[number]))
            leaving.append(pltpu.make_async_copy(held.at[at], dst.at[at], leave.at[number]))
            arriving[-1].start()
    for first, second in zip(arriving, leaving):
        first.wait()
        second.start()
    for second in leaving:
        second.wait()


def shards(n_wide, n_narrow, *args):
    sat, residual = args[0], args[6]
    depth, rows, cols = sat.shape
    layers, brick_rows, _ = residual.shape
    tiles = layers // cols
    bricks = n_wide * n_narrow
    cells = layers * brick_rows
    ahead = depth // 4
    copies = 2 * 7 + 6 * (n_wide - 1) + 2 * (n_narrow - 1)
    anywhere = pl.BlockSpec(memory_space=pl.ANY)
    table, wells = args[3].shape, args[4].shape

    def buffer(*shape):
        return pltpu.VMEM(shape, F32)

    outputs = pl.pallas_call(
        functools.partial(kernel, n_wide, n_narrow),
        out_shape=(
            jax.ShapeDtypeStruct(sat.shape, F32),
            jax.ShapeDtypeStruct(residual.shape, F32),
        ),
        in_specs=[anywhere] * 7,
        out_specs=(anywhere, anywhere),
        scratch_shapes=[
            buffer(*sat.shape),
            buffer(*residual.shape),
            buffer(*sat.shape),
            buffer(*sat.shape),
            buffer(*sat.shape),
            pltpu.VMEM(sat.shape, jnp.int32),
            pltpu.SMEM(table, F32),
            pltpu.SMEM(wells, jnp.int32),
            pltpu.SMEM(wells, F32),
            buffer(*residual.shape),
            buffer(depth + 2, 3, rows, cols),
            buffer(depth, 2, rows, cols),
            buffer(depth, rows, cols),
            buffer(2, rows, cols),
            buffer(2, rows, cols),
            buffer(2, rows, cols),
            buffer(rows, cols),
            buffer(n_wide, brick_rows, cols),
            buffer(n_narrow, brick_rows, cols),
            buffer(n_wide, depth * brick_rows, cols),
            buffer(cells + brick_rows, cols),
            buffer(cells, cols),
            buffer(cells, cols),
            buffer(cells, cols),
            buffer(cells, cols),
            buffer(cells, cols),
            buffer(cells + brick_rows, cols),
            buffer(2, 2, layers, cols),
            buffer(2, 2, layers, cols),
            buffer(2, 2, layers, cols),
            buffer(2, 2, tiles * brick_rows, cols),
            buffer(2, 2, tiles * brick_rows, cols),
            buffer(2, 2, tiles * brick_rows, cols),
            buffer(n_wide, n_wide, cols),
            buffer(bricks, cols),
            buffer(2, rows, cols),
            buffer(2, rows, cols),
            buffer(n_wide * ahead, brick_rows, cols),
            pltpu.VMEM((n_wide * ahead, brick_rows, cols), jnp.int32),
            buffer(n_wide * ahead * brick_rows, cols),
            buffer(n_wide, ahead * brick_rows, cols),
            pltpu.SemaphoreType.DMA((9,)),
            pltpu.SemaphoreType.DMA((layers // 32,)),
            pltpu.SemaphoreType.DMA((copies,)),
            pltpu.SemaphoreType.DMA((copies,)),
        ],
        compiler_params=pltpu.CompilerParams(
            collective_id=0, has_side_effects=True, vmem_limit_bytes=56 * 1024 * 1024
        ),
    )(*args)
    return pl.pallas_call(
        deliver,
        out_shape=(
            jax.ShapeDtypeStruct(sat.shape, F32),
            jax.ShapeDtypeStruct(residual.shape, F32),
        ),
        in_specs=[anywhere] * 2,
        out_specs=(anywhere, anywhere),
        scratch_shapes=[
            buffer(*sat.shape),
            buffer(*residual.shape),
            pltpu.SemaphoreType.DMA((8,)),
            pltpu.SemaphoreType.DMA((8,)),
        ],
        compiler_params=pltpu.CompilerParams(vmem_limit_bytes=60 * 1024 * 1024),
    )(*outputs)


def solution(mesh):
    placed = (
        P("wide", None, "narrow"),
        P("wide", None, "narrow"),
        P("wide", None, "narrow"),
        P(),
        P(),
        P(),
        P(None, "wide", "narrow"),
    )
    return jax.shard_map(
        functools.partial(shards, mesh.shape["wide"], mesh.shape["narrow"]),
        mesh=mesh,
        in_specs=placed,
        out_specs=(P("wide", None, "narrow"), P(None, "wide", "narrow")),
        check_vma=False,
    )
```
